32 devices in a mesh: lon: 4 (over y, core), lat: 8 (over z, x).
Axes of the slice: x: 2, y: 2, z: 4, core: 2. Of those that a mesh axis runs over, the one named last changes fastest.
Arguments:
- theta: float32 [16, 1024, 1024], P(None, 'lat', 'lon'), may hold values from -6 to 6
- kappa: float32 [1024, 1024], P('lat', 'lon'), may hold values from 0.03 to 0.24
- layer_weight: float32 [16], replicated, may hold values from 0.25 to 1.5
- diag: float32 [1024, 1024], P(('lon', 'lat')), may hold values from 0.2 to 2
- land_blocks: int32 [32, 32], replicated, may hold values 0 or 1
Outputs:
- new_theta: float32 [16, 1024, 1024], P(None, 'lat', 'lon')
- psi: float32 [1024, 1024], P(('lon', 'lat'))
The draws below stay inside these ranges and needn't reach their ends.
All inputs are finite; a program needn't handle non-finite values.
Results may differ from the reference program's by a relative error of at most 0.0001.
Values sent between devices are 32-bit elements; how exact they have to be, the bound alone decides.
No kernel may reach another device: no remote copies, remote signals or barrier semaphores. Data moves between devices by JAX's collectives and lax.ppermute only.
A program may use at most 64 MiB of HBM per device.

```python
import math
import jax
import jax.numpy as jnp
from jax import lax

K = 16
BS = 32
ITERS = 4
NX = 1024
NY = 1024
MBX = 32
MBY = 32


def set_ends(result, rng, low, high):
    extent = result.shape
    spot = [jax.random.randint(jax.random.fold_in(rng, axis), (), 0, extent[axis]) for axis in range(len(extent))]
    result = result.at[tuple(spot)].set(low)
    longest = extent.index(max(extent))
    spot[longest] = (spot[longest] + 1) % extent[longest]
    return result.at[tuple(spot)].set(high)


def shard_levels(rng, dims, pieces, smallest, high):
    def one(dim, shards_of):
        steps = jax.random.uniform(jax.random.fold_in(jax.random.fold_in(rng, 6), dim), (shards_of,), jnp.float32, smallest / len(pieces), high / len(pieces))
        return jnp.repeat(jnp.exp(steps), dims[dim] // shards_of).reshape((-1,) + (1,) * (len(dims) - dim - 1))

    factor_of = one(*pieces[0])
    for cut in pieces[1:]:
        factor_of = factor_of * one(*cut)
    return factor_of


def gaussian(own_key, shape, spread, limit, split=(), held_as=jnp.bfloat16):
    drawn = jax.random.normal(own_key, shape, jnp.float32) * spread
    if len(split) > 0:
        drawn = shard_levels(own_key, shape, split, -0.22, 0.18) * drawn
    return jnp.clip(drawn, min=-limit, max=limit).astype(held_as)


def setup_inputs(seed: int = 0) -> dict:
    key_list = jax.random.split(jax.random.key(seed), 6)
    theta = gaussian(key_list[0], (K, NY, NX), 1.0, 6.0, ((1, 8), (2, 4)), jnp.float32)
    kappa = jnp.clip(jnp.exp(math.log(0.24) - 2.0794415 * jax.random.uniform(key_list[1], (NY, NX), jnp.float32) ** shard_levels(key_list[1], (NY, NX), ((0, 8), (1, 4)), -0.2, 0.2)), 0.03, 0.24)
    layer_weight = jnp.clip(jax.random.uniform(key_list[2], (K,), jnp.float32, 0.25, 1.5), 0.25, 1.5)
    diag = jnp.clip(0.2 + 1.8 * jax.random.uniform(key_list[3], (NX, NY), jnp.float32) ** shard_levels(key_list[3], (NX, NY), ((0, 32),), -0.2, 0.2), 0.2, 2.0)
    land_blocks = set_ends((jax.random.randint(key_list[4], (MBY, MBX), 0, 4) < 3).astype(jnp.int32), jax.random.fold_in(key_list[4], 1), 0, 1)
    return dict(theta=theta, kappa=kappa, layer_weight=layer_weight, diag=diag, land_blocks=land_blocks)


def spread_mask(land_blocks):
    cells = jnp.repeat(land_blocks.astype(jnp.float32), BS, axis=0)
    return jnp.repeat(cells, BS, axis=1)


def around_levels(field):
    eastward = jnp.roll(field, -1, axis=2)
    westward = jnp.roll(field, 1, axis=2)
    southern = jnp.concatenate([jnp.zeros_like(field[:, :1, :]), field[:, :-1, :]], axis=1)
    northern = jnp.concatenate([field[:, 1:, :], field[:, -1:, ::-1]], axis=1)
    return eastward + westward + southern + northern


def around_plane(field):
    eastward = jnp.roll(field, -1, axis=0)
    westward = jnp.roll(field, 1, axis=0)
    southern = jnp.concatenate([jnp.zeros_like(field[:, :1]), field[:, :-1]], axis=1)
    northern = jnp.concatenate([field[:, 1:], field[::-1, -1:]], axis=1)
    return eastward + westward + southern + northern


def reference(theta, kappa, layer_weight, diag, land_blocks):
    ocean = spread_mask(land_blocks)
    masked = ocean[None] * theta
    new_theta = theta + ocean[None] * kappa[None] * (around_levels(masked) - 4.0 * masked)
    column_sum = jnp.einsum("k,kyx->yx", layer_weight, new_theta, precision=lax.Precision.HIGHEST)
    forcing = (ocean * column_sum).T
    ocean_plane = ocean.T

    def operate(field):
        return ocean_plane * ((4.0 + diag) * field - around_plane(field))

    solution = jnp.zeros_like(forcing)
    residual = forcing
    direction = forcing
    norm_now = jnp.sum(residual * residual)
    for iteration in range(ITERS):
        applied = operate(direction)
        step_size = norm_now / jnp.sum(direction * applied)
        solution = solution + step_size * direction
        residual = residual - step_size * applied
        norm_next = jnp.sum(residual * residual)
        direction = residual + (norm_next / norm_now) * direction
        norm_now = norm_next
    return new_theta, solution
```

```python
import functools

import jax
import jax.numpy as jnp
from jax import lax
from jax.experimental import pallas as pl
from jax.experimental.pallas import tpu as pltpu
from jax.sharding import PartitionSpec as P

ITERS = 4
EDGE = 8
HALO = ITERS
CENTRE = 5.1
WIDTH = 4.9
VMEM = pl.BlockSpec(memory_space=pltpu.VMEM)
SMEM = pl.BlockSpec(memory_space=pltpu.SMEM)
EXACT = lax.Precision.HIGHEST
PARAMS = pltpu.CompilerParams(vmem_limit_bytes=32 * 1024 * 1024)


def iota(shape, dim):
    return lax.broadcasted_iota(jnp.int32, shape, dim)


def ones_at(hit):
    return jnp.where(hit, 1.0, 0.0).astype(jnp.float32)


def mat(a, b, precision=None):
    return jnp.dot(a, b, precision=precision, preferred_element_type=jnp.float32)


def turn(x, shift, dim):
    return pltpu.roll(x, shift % x.shape[dim] if isinstance(shift, int) else shift, dim)


def beside(v):
    return turn(v, 1, 0) + turn(v, -1, 0) + turn(v, 1, 1) + turn(v, -1, 1)


def block_mask(table, row0, rows, col0, cols, cell):
    down, across = table.shape
    pick_rows = ones_at(lax.div(row0 + iota((rows, down), 0), cell) == iota((rows, down), 1))
    pick_cols = ones_at(lax.div(col0 + iota((across, cols), 1), cell) == iota((across, cols), 0))
    return mat(mat(pick_rows, table), pick_cols)


def sum_kernel(cell, levels, idx, weight, table, theta, kappa, tt, kt, pay_a, pay_b, ns_a, ns_b, acc, edges, tops, bottoms):
    step = pl.program_id(0)
    some, cy, cx = theta.shape

    @pl.when(step == 0)
    def _():
        acc[...] = jnp.zeros_like(acc)
        edges[...] = jnp.zeros_like(edges)

    lane = iota((cy, 128), 1)
    total = acc[...]
    sides = edges[...]
    for j in range(some):
        k = step * some + j
        th = theta[j]
        total = total + weight[k] * th
        sides = jnp.where(lane == k, turn(th[:, :128], k, 1), sides)
        sides = jnp.where(lane == levels + k, turn(th[:, cx - 128 :], levels + k + 1, 1), sides)
        tops[pl.ds(k, 1), :] = th[cy - 1 :, :]
        bottoms[pl.ds(k, 1), :] = th[:1, :]
    acc[...] = total
    edges[...] = sides

    @pl.when(step == pl.num_programs(0) - 1)
    def _():
        lon, lat = idx[0], idx[1]
        mask = block_mask(table[...], lat * cy, cy, lon * cx, cx, cell)
        t = mask * acc[...]
        ttv = t.T
        ktv = kappa[...].T
        tt[...] = ttv
        kt[...] = ktv
        sidest = (edges[...] * jnp.where(lane < levels, mask[:, :1], mask[:, cx - 1 :])).T
        even = lax.rem(lon, 2) == 0
        west = (ttv[:EDGE], ktv[:EDGE], sidest[:levels])
        east = (ttv[cx - EDGE :], ktv[cx - EDGE :], sidest[levels : 2 * levels])
        at = 0
        for w, e in zip(west, east):
            rows = w.shape[0]
            pay_a[at : at + rows, :] = jnp.where(even, e, w)
            pay_b[at : at + rows, :] = jnp.where(even, w, e)
            at += rows
        flip = ones_at(iota((cx, cx), 0) + iota((cx, cx), 1) == cx - 1)
        both = jnp.concatenate([t[cy - EDGE :], kappa[cy - EDGE :, :]], axis=0)
        turned = mat(both, flip, EXACT)
        for base in (0, EDGE):
            for c in range(cx // cy):
                for r in range(EDGE):
                    row = turned[base + EDGE - 1 - r : base + EDGE - r, c * cy : (c + 1) * cy]
                    pay_a[at + r : at + r + 1, :] = row
                    pay_b[at + r : at + r + 1, :] = row
                at += EDGE
        top = tops[...] * mask[cy - 1 :, :]
        bottom = bottoms[...] * mask[:1, :]
        even_row = lax.rem(lat, 2) == 0
        ns_a[...] = jnp.where(even_row, top, bottom)
        ns_b[...] = jnp.where(even_row, bottom, top)


def forcing_kernel(levels, last, width, idx, tt, kt, got_a, got_b, tops_m, tops_a, tops_b, out, *, at_m, at_a, at_b):
    cx, cy = tt.shape
    lon, lat = idx[0], idx[1]
    even = lax.rem(lon, 2) == 0
    nt = cx // cy

    def extended(own, at, which):
        a = got_a[at : at + EDGE, :]
        b = got_b[at : at + EDGE, :]
        rows = jnp.concatenate([jnp.where(even, b, a), own, jnp.where(even, a, b)], axis=0)

        def column(ref, start, tile):
            start = start + (which * nt + tile) * EDGE
            tile_rows = ref[start : start + EDGE, :]
            return jnp.concatenate([tile_rows, jnp.zeros((cy - EDGE, cy), jnp.float32)], axis=0).T

        a_first, b_first = column(tops_a, at_a, 0), column(tops_b, at_b, 0)
        a_last, b_last = column(tops_a, at_a, nt - 1), column(tops_b, at_b, nt - 1)
        left = jnp.where(even, b_last, a_last)[cy - EDGE :]
        right = jnp.where(even, a_first, b_first)[:EDGE]
        fold = jnp.concatenate([left] + [column(tops_m, at_m, c) for c in range(nt)] + [right], axis=0)
        return jnp.concatenate([rows, jnp.where(lat == last, fold, 0.0)], axis=1)

    t = extended(tt[...], 0, 0)
    k = extended(kt[...], EDGE, 1)
    f = t + k * (beside(t) - 4.0 * t)
    rows = cx + 2 * EDGE
    lane = iota((rows, cy), 1)
    t0, k0 = t[:, :cy], k[:, :cy]
    pack = jnp.where(lane == 0, t0, 0.0)
    pack = jnp.where(lane == 1, turn(t0, 2, 1), pack)
    pack = jnp.where(lane == 2, turn(k0, 2, 1), pack)
    pack = jnp.where(lane == 3, turn(k0, 4, 1), pack)
    pack = jnp.where((lane >= 4) & (lane < 8), turn(f[:, cy:], 4, 1), pack)
    wide = -(-rows // 128) * 128
    pack = jnp.concatenate([pack, jnp.zeros((wide - rows, cy), jnp.float32)], axis=0).T[:8]
    low = iota((EDGE, cy), 0) < HALO
    for d in range(cx // width):
        at = EDGE + d * width
        out[d, :width, :] = f[at : at + width, :cy]
        out[d, width : width + EDGE, :] = jnp.where(low, f[at + width : at + width + EDGE, :cy], f[at - EDGE : at, :cy])
        out[d, width + EDGE :, :] = turn(pack, -d * width, 1)[:, :128]


def strip_order(columns, width):
    low = iota((EDGE, columns.shape[1]), 0) < HALO
    ends = jnp.where(low, columns[EDGE + width : 2 * EDGE + width], columns[:EDGE])
    return jnp.concatenate([columns[EDGE : EDGE + width], ends], axis=0)


def krylov_kernel(cell, idx, table_t, got, diag, d_right, d_left, d_fold, basis, gram):
    count, chunk, cy = got.shape
    width, full = diag.shape
    rows = width + EDGE
    x0 = (idx[0] * count + idx[1]) * width
    across, down = table_t.shape
    nx = across * cell

    edges = jnp.concatenate([got[s, rows:, :] for s in range(count)], axis=0)
    if edges.shape[0] < 128:
        edges = jnp.concatenate([edges, jnp.zeros((128 - edges.shape[0], cy), jnp.float32)], axis=0)
    edges = strip_order(edges.T, width)
    from_south = edges * turn(edges, 9, 1)
    from_north = edges * turn(edges, -5, 1)
    lane = iota((rows, cy), 1)
    parts = []
    for s in range(count):
        part = got[s, :rows, :]
        if s > 0:
            part = part + jnp.where(lane == 0, turn(from_south, -(8 * s + 2), 1), 0.0)
        if s < count - 1:
            part = part + jnp.where(lane == cy - 1, turn(from_north, cy - 1 - (8 * s + 3), 1), 0.0)
        parts.append(part)
    parts.append(jnp.where(lane < HALO, turn(edges, -(8 * (count - 1) + 4), 1), 0.0))
    f = jnp.concatenate(parts, axis=1)

    place = iota((rows, across), 0)
    x = x0 + jnp.where(place < width + HALO, place, place - rows)
    x = jnp.where(x < 0, x + nx, jnp.where(x >= nx, x - nx, x))
    cells = iota((rows, across), 1)
    here = ones_at(lax.div(x, cell) == cells)
    there = ones_at(lax.div(nx - 1 - x, cell) == cells)
    up = ones_at(lax.div(iota((down, full), 1), cell) == iota((down, full), 0))
    above = ones_at((iota((down, cy), 0) == down - 1) & (iota((down, cy), 1) < HALO))
    t = table_t[...]
    mask = jnp.concatenate([mat(mat(here, t), up), mat(mat(there, t), above)], axis=1)

    low = iota((EDGE, full), 0) < HALO
    d_main = jnp.concatenate([diag[...], jnp.where(low, d_right[:, :full], d_left[:, :full])], axis=0)
    folds = jnp.concatenate([d_fold[...], d_right[:, full:], d_left[:, full:], jnp.zeros((128 - 3 * EDGE, 128), jnp.float32)], axis=0).T
    halo_low = iota((EDGE, 128), 0) < HALO
    d_ends = jnp.where(halo_low, turn(folds[:EDGE], -EDGE, 1), turn(folds[width - EDGE : width], -2 * EDGE, 1))
    d_all = jnp.concatenate([d_main, jnp.concatenate([folds[:width], d_ends], axis=0)], axis=1)

    near = mask * (1.0 / WIDTH)
    centre = near * ((4.0 - CENTRE) + jnp.where(mask > 0.0, d_all, 0.0))
    p = [mask * f]
    p.append(centre * p[0] - near * beside(p[0]))
    for j in range(2, ITERS + 1):
        p.append(2.0 * (centre * p[j - 1] - near * beside(p[j - 1])) - p[j - 2])
    for j in range(ITERS):
        basis[j] = p[j][:width, :full]
    sums = []
    for i in range(ITERS):
        for j in range(i, ITERS + 1):
            both = p[i][:width, :full] * p[j][:width, :full]
            both = sum(both[:, c : c + 128] for c in range(0, full, 128))
            sums.append(jnp.sum(both, axis=0, keepdims=True))
    sums = jnp.concatenate(sums + [jnp.zeros((128 - len(sums), 128), jnp.float32)], axis=0)
    gram[...] = jnp.broadcast_to(jnp.sum(sums.T, axis=0, keepdims=True), gram.shape)


def combine_kernel(gram, basis, psi):
    g = jnp.sum(gram[...], axis=0, keepdims=True)
    at = {}
    n = 0
    for i in range(ITERS):
        for j in range(i, ITERS + 1):
            at[i, j] = at[j, i] = g[:, n : n + 1]
            n += 1

    def applied(i, j):
        if j == 0:
            return CENTRE * at[i, 0] + WIDTH * at[i, 1]
        return CENTRE * at[i, j] + (0.5 * WIDTH) * (at[i, j + 1] + at[i, j - 1])

    low = {}
    pivot = []
    right = []
    for i in range(ITERS):
        row = []
        for j in range(i):
            value = applied(j, i)
            for k in range(j):
                value = value - row[k] * low[j, k]
            row.append(value)
            low[i, j] = value / pivot[j]
        value = applied(i, i)
        for k in range(i):
            value = value - row[k] * low[i, k]
        pivot.append(value)
        value = at[i, 0]
        for k in range(i):
            value = value - low[i, k] * right[k]
        right.append(value)
    c = [None] * ITERS
    for i in reversed(range(ITERS)):
        value = right[i] / pivot[i]
        for k in range(i + 1, ITERS):
            value = value - low[k, i] * c[k]
        c[i] = value
    total = c[0] * basis[0]
    for j in range(1, ITERS):
        total = total + c[j] * basis[j]
    psi[...] = total


def tracer_kernel(cell, levels, last, idx, table, theta, kappa, got_a, got_b, rows_a, rows_b, out, mask, coef, sides, north, south):
    step = pl.program_id(0)
    some, cy, cx = theta.shape
    lon, lat = idx[0], idx[1]

    @pl.when(step == 0)
    def _():
        ocean = block_mask(table[...], lat * cy, cy, lon * cx, cx, cell)
        mask[...] = ocean
        coef[...] = ocean * kappa[...]
        even = lax.rem(lon, 2) == 0
        a, b = got_a[2 * EDGE : 2 * EDGE + levels, :], got_b[2 * EDGE : 2 * EDGE + levels, :]
        both = jnp.concatenate([jnp.where(even, a, b), jnp.where(even, b, a), jnp.zeros((128 - 2 * levels, cy), jnp.float32)], axis=0)
        sides[...] = both.T
        even_row = lax.rem(lat, 2) == 0
        up = jnp.where(even_row, rows_a[...], rows_b[...])
        flip = ones_at(iota((cx, cx), 0) + iota((cx, cx), 1) == cx - 1)
        north[...] = jnp.where(lat == last, mat(up, flip, EXACT), up)
        south[...] = jnp.where(even_row, rows_b[...], rows_a[...])

    lane = iota((cy, cx), 1)
    row = iota((cy, cx), 0)
    spare = jnp.zeros((cy, cx - 128), jnp.float32)
    for j in range(some):
        k = step * some + j
        th = theta[j]
        m = mask[...] * th
        col = sides[...]
        from_east = jnp.concatenate([spare, turn(col, 127 - k, 1)], axis=1)
        from_west = jnp.concatenate([turn(col, 128 - levels - k, 1), spare], axis=1)
        east = jnp.where(lane == cx - 1, from_east, turn(m, -1, 1))
        west = jnp.where(lane == 0, from_west, turn(m, 1, 1))
        above = jnp.where(row == cy - 1, north[pl.ds(k, 1), :], turn(m, -1, 0))
        below = jnp.where(row == 0, south[pl.ds(k, 1), :], turn(m, 1, 0))
        out[j] = th + coef[...] * (east + west + above + below - 4.0 * m)


def per_device(theta, kappa, layer_weight, diag, land_blocks):
    lons, lats = lax.axis_size("lon"), lax.axis_size("lat")
    joint = ("lon", "lat")
    devices = lons * lats
    levels, cy, cx = theta.shape
    width, full = diag.shape
    cell = full // land_blocks.shape[0]
    last = lats - 1
    f32 = jnp.float32
    shape = lambda *dims: jax.ShapeDtypeStruct(dims, f32)
    idx = jnp.stack([lax.axis_index("lon"), lax.axis_index("lat")]).astype(jnp.int32)
    table = land_blocks.astype(f32)

    corner = diag[:, full - EDGE :][::-1, ::-1].T
    corner = jnp.pad(corner, ((0, 0), (0, 128 - width)))
    d_fold = lax.ppermute(corner, joint, [(i, devices - 1 - i) for i in range(devices)])
    d_east = jnp.concatenate([diag[width - EDGE :], d_fold], axis=1)
    d_west = jnp.concatenate([diag[:EDGE], d_fold], axis=1)
    d_left = lax.ppermute(d_east, joint, [(i, (i + 1) % devices) for i in range(devices)])
    d_right = lax.ppermute(d_west, joint, [((i + 1) % devices, i) for i in range(devices)])

    some = 4
    nt = cx // cy
    head = 2 * EDGE + levels
    own = 2 * nt * EDGE
    block = pl.BlockSpec((some, cy, cx), lambda s: (s, 0, 0))
    tt, kt, pay_a, pay_b, ns_a, ns_b = pl.pallas_call(
        functools.partial(sum_kernel, cell, levels),
        grid=(levels // some,),
        in_specs=[SMEM, SMEM, VMEM, block, VMEM],
        out_specs=[VMEM] * 6,
        out_shape=[shape(cx, cy), shape(cx, cy), shape(head + own, cy), shape(head + own, cy), shape(levels, cx), shape(levels, cx)],
        scratch_shapes=[pltpu.VMEM((cy, cx), f32), pltpu.VMEM((cy, 128), f32), pltpu.VMEM((levels, cx), f32), pltpu.VMEM((levels, cx), f32)],
        compiler_params=PARAMS,
        name="level_sum",
    )(idx, layer_weight, table, theta, kappa)

    pairs_b = [(i, (i + 1) % lons if i % 2 else (i - 1) % lons) for i in range(lons)]
    mirror = [(i, lons - 1 - i) for i in range(lons)]
    got_a = lax.ppermute(pay_a, "lon", [(i, i ^ 1) for i in range(lons)])
    if pairs_b == mirror:
        got_b = lax.ppermute(jnp.concatenate([pay_b, got_a[head:]], axis=0), "lon", pairs_b)
        folds = (got_b, got_b, pay_b)
        places = dict(at_m=head, at_a=head + own, at_b=head)
    else:
        got_b = lax.ppermute(pay_b, "lon", pairs_b)
        got_m = lax.ppermute(jnp.concatenate([pay_b[head:], got_a[head:], got_b[head:]], axis=0), "lon", mirror)
        folds = (got_m, got_m, got_m)
        places = dict(at_m=0, at_a=own, at_b=2 * own)
    chunks = pl.pallas_call(
        functools.partial(forcing_kernel, levels, last, width, **places),
        in_specs=[SMEM] + [VMEM] * 7,
        out_specs=VMEM,
        out_shape=shape(lats, width + 2 * EDGE, cy),
        compiler_params=PARAMS,
        name="forcing",
    )(idx, tt, kt, got_a, got_b, *folds)
    got = lax.all_to_all(chunks, "lat", split_axis=0, concat_axis=0, tiled=True)

    def flat(lon, lat):
        return lon * lats + lat

    first, second = [], []
    for lon in range(lons):
        for lat in range(lats):
            first.append((flat(lon, lat), flat(lon, lat ^ 1)))
            to = lat + 1 if lat % 2 else lat - 1
            if to == lats:
                second.append((flat(lon, lat), flat(lons - 1 - lon, lat)))
            elif to >= 0:
                second.append((flat(lon, lat), flat(lon, to)))
    rows_a = lax.ppermute(ns_a, joint, first)
    rows_b = lax.ppermute(ns_b, joint, second)
    new_theta = pl.pallas_call(
        functools.partial(tracer_kernel, cell, levels, last),
        grid=(levels // some,),
        in_specs=[SMEM, VMEM, block] + [VMEM] * 5,
        out_specs=block,
        out_shape=shape(levels, cy, cx),
        scratch_shapes=[pltpu.VMEM((cy, cx), f32), pltpu.VMEM((cy, cx), f32), pltpu.VMEM((cy, 128), f32), pltpu.VMEM((levels, cx), f32), pltpu.VMEM((levels, cx), f32)],
        compiler_params=PARAMS,
        cost_estimate=pl.CostEstimate(flops=12 * levels * cy * cx, bytes_accessed=8 * levels * cy * cx, transcendentals=0),
        name="tracer",
    )(idx, table, theta, kappa, got_a, got_b, rows_a, rows_b)

    basis, gram = pl.pallas_call(
        functools.partial(krylov_kernel, cell),
        in_specs=[SMEM] + [VMEM] * 6,
        out_specs=[VMEM, VMEM],
        out_shape=[shape(ITERS, width, full), shape(devices, 128)],
        compiler_params=PARAMS,
        name="krylov",
    )(idx, table.T, got, diag, d_right, d_left, d_fold)
    gram = lax.all_to_all(gram, joint, split_axis=0, concat_axis=0, tiled=True)
    psi = pl.pallas_call(
        combine_kernel,
        in_specs=[VMEM, VMEM],
        out_specs=VMEM,
        out_shape=shape(width, full),
        compiler_params=PARAMS,
        name="combine",
    )(gram, basis)
    return new_theta, psi


def solution(mesh):
    return jax.shard_map(
        per_device,
        mesh=mesh,
        in_specs=(P(None, "lat", "lon"), P("lat", "lon"), P(), P(("lon", "lat"), None), P()),
        out_specs=(P(None, "lat", "lon"), P(("lon", "lat"), None)),
        check_vma=False,
    )
```

```python
import functools

import jax
import jax.numpy as jnp
from jax import lax
from jax.experimental import pallas as pl
from jax.experimental.pallas import tpu as pltpu
from jax.sharding import PartitionSpec as P

ITERS = 4
EDGE = 8
HALO = ITERS
RIM = HALO - 1
CENTRE = 5.1
WIDTH = 4.9
VMEM = pl.BlockSpec(memory_space=pltpu.VMEM)
SMEM = pl.BlockSpec(memory_space=pltpu.SMEM)
HBM = pl.BlockSpec(memory_space=pltpu.HBM)
EXACT = lax.Precision.HIGHEST
PARAMS = pltpu.CompilerParams(vmem_limit_bytes=32 * 1024 * 1024)


def in_hbm(x):
    return pltpu.with_memory_space_constraint(x, pltpu.HBM)


def iota(shape, dim):
    return lax.broadcasted_iota(jnp.int32, shape, dim)


def ones_at(hit):
    return jnp.where(hit, 1.0, 0.0).astype(jnp.float32)


def mat(a, b, precision=None):
    return jnp.dot(a, b, precision=precision, preferred_element_type=jnp.float32)


def turn(x, shift, dim):
    return pltpu.roll(x, shift % x.shape[dim] if isinstance(shift, int) else shift, dim)


def beside(v):
    return turn(v, 1, 0) + turn(v, -1, 0) + turn(v, 1, 1) + turn(v, -1, 1)


def block_mask(table, row0, rows, col0, cols, cell):
    down, across = table.shape
    pick_rows = ones_at(lax.div(row0 + iota((rows, down), 0), cell) == iota((rows, down), 1))
    pick_cols = ones_at(lax.div(col0 + iota((across, cols), 1), cell) == iota((across, cols), 0))
    return mat(mat(pick_rows, table), pick_cols)


def sum_kernel(cell, weight_hbm, table_hbm, theta_hbm, kappa_hbm, diag_hbm, theta, ocean, coef, tt, kt, pay_a, pay_b, row_a, row_b, kappa, corner, rim, table, weight, sems):
    levels, cy, cx = theta.shape
    width, full = diag_hbm.shape
    copies = [
        pltpu.make_async_copy(table_hbm, table, sems.at[0]),
        pltpu.make_async_copy(weight_hbm, weight, sems.at[1]),
        pltpu.make_async_copy(kappa_hbm, kappa, sems.at[2]),
        pltpu.make_async_copy(diag_hbm.at[:, pl.ds(full - 128, 128)], corner, sems.at[3]),
        pltpu.make_async_copy(diag_hbm.at[pl.ds(0, EDGE)], rim.at[0], sems.at[4]),
        pltpu.make_async_copy(diag_hbm.at[pl.ds(width - EDGE, EDGE)], rim.at[1], sems.at[5]),
    ]
    pieces = 4
    some = levels // pieces
    for n in range(pieces):
        copies.append(pltpu.make_async_copy(theta_hbm.at[pl.ds(n * some, some)], theta.at[pl.ds(n * some, some)], sems.at[6 + n]))
    for copy in copies:
        copy.start()
    lon, lat = lax.axis_index("lon"), lax.axis_index("lat")
    even = lax.rem(lon, 2) == 0
    even_row = lax.rem(lat, 2) == 0
    copies[0].wait()
    mask = block_mask(table[...].astype(jnp.float32), lat * cy, cy, lon * cx, cx, cell)
    copies[3].wait()
    column = jnp.concatenate([corner[...], jnp.zeros((128 - width, 128), jnp.float32)], axis=0).T
    column = turn(column[128 - EDGE :], lon * width, 1)
    copies[4].wait()
    copies[5].wait()
    at = cx // cy * levels
    for c in range(full // cy):
        w = rim[0, :RIM, c * cy : (c + 1) * cy]
        e = rim[1, EDGE - RIM :, c * cy : (c + 1) * cy]
        row_a[at : at + RIM, :] = jnp.where(even_row, e, w)
        row_b[at : at + RIM, :] = jnp.where(even_row, w, e)
        at += RIM
    copies[2].wait()
    kappas = kappa[...]
    ocean[...] = mask
    coef[...] = mask * kappas
    ktv = kappas.T
    kt[...] = ktv

    lane = iota((cy, 128), 1)
    total = jnp.zeros((cy, cx), jnp.float32)
    sides = jnp.zeros((cy, 128), jnp.float32)
    copies[1].wait()
    for n in range(pieces):
        copies[6 + n].wait()
        for k in range(n * some, n * some + some):
            th = theta[k]
            total = total + weight[k] * th
            sides = jnp.where(lane == k, turn(th[:, :128], k, 1), sides)
            sides = jnp.where(lane == levels + k, turn(th[:, cx - 128 :], levels + k + 1, 1), sides)
    t = mask * total
    ttv = t.T
    tt[...] = ttv
    sidest = (sides * jnp.where(lane < levels, mask[:, :1], mask[:, cx - 1 :])).T
    west = (ttv[:EDGE], ktv[:EDGE], sidest[:levels])
    east = (ttv[cx - EDGE :], ktv[cx - EDGE :], sidest[levels : 2 * levels])
    at = 0
    for w, e in zip(west, east):
        rows = w.shape[0]
        pay_a[at : at + rows, :] = jnp.where(even, e, w)
        pay_b[at : at + rows, :] = jnp.where(even, w, e)
        at += rows
    flip = ones_at(iota((cx, cx), 0) + iota((cx, cx), 1) == cx - 1)
    both = jnp.concatenate([t[cy - EDGE :], kappas[cy - EDGE :, :]], axis=0)
    turned = mat(both, flip, EXACT)
    nt = cx // cy
    for base, to in ((0, at), (EDGE, at + EDGE)):
        for r in range(EDGE):
            row = turned[base + EDGE - 1 - r : base + EDGE - r]
            pay_a[to + r : to + r + 1, :] = jnp.where(even, row[:, :cy], row[:, cx - cy :])
            for c in range(nt):
                to_b = at + (base // EDGE * nt + c) * EDGE + r
                pay_b[to_b : to_b + 1, :] = row[:, c * cy : (c + 1) * cy]
    pay_a[at + 2 * EDGE :, :] = column
    at += 2 * nt * EDGE
    pay_b[at : at + EDGE, :] = column
    at += EDGE
    top = theta[:, cy - 1, :] * mask[cy - 1 :, :]
    bottom = theta[:, 0, :] * mask[:1, :]
    for c in range(nt):
        t, b = top[:, c * cy : (c + 1) * cy], bottom[:, c * cy : (c + 1) * cy]
        row_a[c * levels : (c + 1) * levels, :] = jnp.where(even_row, t, b)
        row_b[c * levels : (c + 1) * levels, :] = jnp.where(even_row, b, t)
        pay_b[at + c * levels : at + (c + 1) * levels, :] = t


def forcing_kernel(last, width, places, tt, kt, got_a, got_b, tops_m, tops_a, tops_b, *rest):
    *corners, out = rest
    at_m, at_a, at_b, at_corners = places
    cx, cy = tt.shape
    lon, lat = lax.axis_index("lon"), lax.axis_index("lat")
    even = lax.rem(lon, 2) == 0
    nt = cx // cy

    stack = []
    for which in (0, 1):
        a = tops_a[at_a + which * EDGE : at_a + (which + 1) * EDGE, :]
        b_first = tops_b[at_b + which * nt * EDGE : at_b + (which * nt + 1) * EDGE, :]
        b_last = tops_b[at_b + (which * nt + nt - 1) * EDGE : at_b + (which * nt + nt) * EDGE, :]
        stack.append(jnp.where(even, b_last, a))
        for c in range(nt):
            stack.append(tops_m[at_m + (which * nt + c) * EDGE : at_m + (which * nt + c + 1) * EDGE, :])
        stack.append(jnp.where(even, a, b_first))
    used = len(stack) * EDGE
    stack = jnp.concatenate(stack + [jnp.zeros((cy - used, cy), jnp.float32)], axis=0).T
    fold_lane = (iota((cy, cy), 1) < EDGE) & (lat == last)

    def extended(own, at, which):
        a = got_a[at : at + EDGE, :]
        b = got_b[at : at + EDGE, :]
        rows = jnp.concatenate([jnp.where(even, b, a), own, jnp.where(even, a, b)], axis=0)
        first = which * (nt + 2)
        tiles = [jnp.where(fold_lane, turn(stack, -(first + n) * EDGE, 1), 0.0) for n in range(nt + 2)]
        fold = jnp.concatenate([tiles[0][cy - EDGE :]] + tiles[1:-1] + [tiles[-1][:EDGE]], axis=0)
        return jnp.concatenate([rows, fold], axis=1)

    t = extended(tt[...], 0, 0)
    k = extended(kt[...], EDGE, 1)
    f = t + k * (beside(t) - 4.0 * t)
    rows = cx + 2 * EDGE
    lane = iota((rows, cy), 1)
    t0, k0 = t[:, :cy], k[:, :cy]
    pack = jnp.where(lane == 0, t0, 0.0)
    pack = jnp.where(lane == 1, turn(t0, 2, 1), pack)
    pack = jnp.where(lane == 2, turn(k0, 2, 1), pack)
    pack = jnp.where(lane == 3, turn(k0, 4, 1), pack)
    pack = jnp.where((lane >= 4) & (lane < 8), turn(f[:, cy:], 4, 1), pack)
    wide = -(-rows // 128) * 128
    pack = jnp.concatenate([pack, jnp.zeros((wide - rows, cy), jnp.float32)], axis=0).T[:8]
    low = iota((EDGE, cy), 0) < HALO
    corner = sum(ref[at : at + EDGE, :] for ref, at in zip(corners, at_corners))
    corner = jnp.where(low, turn(turn(corner, HALO, 0), 64, 1), corner)
    in_pack = iota((EDGE, cy), 1) < 64
    for d in range(cx // width):
        at = EDGE + d * width
        out[d, :width, :] = f[at : at + width, :cy]
        out[d, width : width + EDGE, :] = jnp.where(low, f[at + width : at + width + EDGE, :cy], f[at - EDGE : at, :cy])
        out[d, width + EDGE :, :] = jnp.where(in_pack, turn(pack, -d * width, 1)[:, :128], corner)


def strip_order(columns, width):
    low = iota((EDGE, columns.shape[1]), 0) < HALO
    ends = jnp.where(low, columns[EDGE + width : 2 * EDGE + width], columns[:EDGE])
    return jnp.concatenate([columns[EDGE : EDGE + width], ends], axis=0)


def krylov_kernel(cell, start, table, got, diag, rows_a, rows_b, basis, gram):
    count, chunk, cy = got.shape
    width, full = diag.shape
    rows = width + EDGE
    lon, lat = lax.axis_index("lon"), lax.axis_index("lat")
    x0 = (lon * count + lat) * width
    down, across = table.shape
    nx = across * cell
    lons = nx // (count * width)

    edges = jnp.concatenate([got[s, rows:, :] for s in range(count)], axis=0)
    if edges.shape[0] < 128:
        edges = jnp.concatenate([edges, jnp.zeros((128 - edges.shape[0], cy), jnp.float32)], axis=0)
    edges = strip_order(edges.T, width)
    from_south = edges * turn(edges, 9, 1)
    from_north = edges * turn(edges, -5, 1)
    lane = iota((rows, cy), 1)
    parts = []
    for s in range(count):
        part = got[s, :rows, :]
        if s > 0:
            part = part + jnp.where(lane == 0, turn(from_south, -(8 * s + 2), 1), 0.0)
        if s < count - 1:
            part = part + jnp.where(lane == cy - 1, turn(from_north, cy - 1 - (8 * s + 3), 1), 0.0)
        parts.append(part)
    parts.append(jnp.where(lane < HALO, turn(edges, -(8 * (count - 1) + 4), 1), 0.0))
    f = jnp.concatenate(parts, axis=1)

    place = iota((rows, across), 0)
    x = x0 + jnp.where(place < width + HALO, place, place - rows)
    x = jnp.where(x < 0, x + nx, jnp.where(x >= nx, x - nx, x))
    cells = iota((rows, across), 1)
    here = ones_at(lax.div(x, cell) == cells)
    there = ones_at(lax.div(nx - 1 - x, cell) == cells)
    up = ones_at(lax.div(iota((down, full), 1), cell) == iota((down, full), 0))
    above = ones_at((iota((down, cy), 0) == down - 1) & (iota((down, cy), 1) < HALO))
    land = table[...].astype(jnp.float32)
    pick = lax.dot_general(jnp.concatenate([here, there], axis=0), land, (((1,), (1,)), ((), ())), preferred_element_type=jnp.float32)
    mask = jnp.concatenate([mat(pick[:rows], up), mat(pick[rows:], above)], axis=1)

    even_row = lax.rem(lat, 2) == 0
    rim = full // cy * RIM
    d_a, d_b = rows_a[start : start + rim, :], rows_b[start : start + rim, :]
    d_east, d_west = jnp.where(even_row, d_a, d_b), jnp.where(even_row, d_b, d_a)
    unused = jnp.zeros((EDGE - 2 * RIM, cy), jnp.float32)
    d_ends = [
        jnp.concatenate([d_east[c * RIM : (c + 1) * RIM], unused, d_west[c * RIM : (c + 1) * RIM]], axis=0) for c in range(full // cy)
    ]
    d_main = jnp.concatenate([diag[...], jnp.concatenate(d_ends, axis=1)], axis=0)

    mine = lon * count + lat
    total = lons * count
    tiles = []
    for strip in (total - 1 - mine, lax.rem(2 * total - 2 - mine, total), lax.rem(total - mine, total)):
        tile = got[lax.rem(strip, count)][rows:, :]
        tile = jnp.where(iota((EDGE, 128), 1) < 64, turn(turn(tile, HALO, 0), 64, 1), tile)
        tiles.append(turn(tile, lax.rem(128 - lax.div(strip, count) * width, 128), 1))
    here = iota((128, 128), 0)
    there = iota((128, 128), 1)
    picks = [
        (here + there == width - 1) & (there < width),
        (here + there == 2 * width - 1) & (there >= width) & (there < width + HALO),
        (here + there == rows - 1) & (there >= rows - HALO) & (there < rows),
    ]
    fold = sum(mat(tile, ones_at(pick), EXACT) for tile, pick in zip(tiles, picks))
    fold = [fold[EDGE - 1 - r : EDGE - r] for r in range(HALO)] + [jnp.zeros((128 - HALO, 128), jnp.float32)]
    d_all = jnp.concatenate([d_main, jnp.concatenate(fold, axis=0).T[:rows]], axis=1)

    near = mask * (1.0 / WIDTH)
    centre = near * ((4.0 - CENTRE) + d_all)
    p = [mask * f]
    p.append(centre * p[0] - near * beside(p[0]))
    for j in range(2, ITERS + 1):
        p.append(2.0 * (centre * p[j - 1] - near * beside(p[j - 1])) - p[j - 2])
    for j in range(ITERS):
        basis[j] = p[j][:width, :full]
    sums = []
    for i in range(ITERS):
        for j in range(i, ITERS + 1):
            both = p[i][:width, :full] * p[j][:width, :full]
            both = sum(both[:, c : c + 128] for c in range(0, full, 128))
            sums.append(jnp.sum(both, axis=0, keepdims=True))
    sums = jnp.concatenate(sums + [jnp.zeros((128 - len(sums), 128), jnp.float32)], axis=0)
    gram[...] = jnp.broadcast_to(jnp.sum(sums.T, axis=0, keepdims=True), gram.shape)


def combine_kernel(gram, basis, psi):
    g = jnp.sum(gram[...], axis=0, keepdims=True)
    pairs = [(i, j) for i in range(ITERS) for j in range(i, ITERS + 1)]
    at = {}
    for n, (i, j) in enumerate(pairs):
        at[i, j] = at[j, i] = jnp.broadcast_to(g[:, n : n + 1], (8, 128))

    def applied(i, j):
        if j == 0:
            return CENTRE * at[i, 0] + WIDTH * at[i, 1]
        return CENTRE * at[i, j] + (0.5 * WIDTH) * (at[i, j + 1] + at[i, j - 1])

    a = {(i, j): applied(i, j) for i in range(ITERS) for j in range(i, ITERS)}
    b = [at[i, 0] for i in range(ITERS)]
    inverse = []
    for k in range(ITERS):
        inverse.append(1.0 / a[k, k])
        for i in range(k + 1, ITERS):
            factor = a[k, i] * inverse[k]
            for j in range(i, ITERS):
                a[i, j] = a[i, j] - factor * a[k, j]
            b[i] = b[i] - factor * b[k]
    c = [None] * ITERS
    for i in reversed(range(ITERS)):
        value = b[i]
        for j in range(i + 1, ITERS):
            value = value - a[i, j] * c[j]
        c[i] = value * inverse[i]
    total = c[0][:1, :1] * basis[0]
    for j in range(1, ITERS):
        total = total + c[j][:1, :1] * basis[j]
    psi[...] = total


def tracer_kernel(last, start, theta, ocean, coef, got_a, got_b, rows_a, rows_b, fold, out_hbm, out, sems):
    levels, cy, cx = theta.shape
    lon, lat = lax.axis_index("lon"), lax.axis_index("lat")
    even = lax.rem(lon, 2) == 0
    a, b = got_a[2 * EDGE : 2 * EDGE + levels, :], got_b[2 * EDGE : 2 * EDGE + levels, :]
    both = jnp.concatenate([jnp.where(even, a, b), jnp.where(even, b, a), jnp.zeros((128 - 2 * levels, cy), jnp.float32)], axis=0)
    sides = both.T
    even_row = lax.rem(lat, 2) == 0

    def joined(ref, at=0):
        return jnp.concatenate([ref[at + c * levels : at + (c + 1) * levels, :] for c in range(cx // cy)], axis=1)

    a, b = joined(rows_a), joined(rows_b)
    flip = ones_at(iota((cx, cx), 0) + iota((cx, cx), 1) == cx - 1)
    north = jnp.where(lat == last, mat(joined(fold, start), flip, EXACT), jnp.where(even_row, a, b))
    south = jnp.where(lat == 0, 0.0, jnp.where(even_row, b, a))

    lane = iota((cy, 128), 1)
    row = iota((cy, cx), 0)
    mask, scale = ocean[...], coef[...]
    some = 2
    copies = []
    for k in range(levels):
        th = theta[k]
        m = mask * th
        east, west = turn(m, -1, 1), turn(m, 1, 1)
        east = jnp.concatenate([east[:, : cx - 128], jnp.where(lane == 127, turn(sides, 127 - k, 1), east[:, cx - 128 :])], axis=1)
        west = jnp.concatenate([jnp.where(lane == 0, turn(sides, -levels - k, 1), west[:, :128]), west[:, 128:]], axis=1)
        above = jnp.where(row == cy - 1, north[k : k + 1], turn(m, -1, 0))
        below = jnp.where(row == 0, south[k : k + 1], turn(m, 1, 0))
        out[k] = th + scale * (east + west + above + below - 4.0 * m)
        if (k + 1) % some == 0:
            n = k // some
            piece = pl.ds(n * some, some)
            copies.append(pltpu.make_async_copy(out.at[piece], out_hbm.at[piece], sems.at[n]))
            copies[-1].start()
    for copy in copies:
        copy.wait()


def per_device(theta, kappa, layer_weight, diag, land_blocks):
    lons, lats = lax.axis_size("lon"), lax.axis_size("lat")
    joint = ("lon", "lat")
    devices = lons * lats
    levels, cy, cx = theta.shape
    width, full = diag.shape
    cell = full // land_blocks.shape[0]
    last = lats - 1
    f32 = jnp.float32
    shape = lambda *dims: jax.ShapeDtypeStruct(dims, f32)

    nt = cx // cy
    head = 2 * EDGE + levels
    own = (2 * nt + 1) * EDGE
    rim = RIM * (full // cy)
    held, ocean, coef, tt, kt, pay_a, pay_b, row_a, row_b = pl.pallas_call(
        functools.partial(sum_kernel, cell),
        in_specs=[HBM] * 5,
        out_specs=[VMEM] * 9,
        out_shape=[
            pltpu.VMEM((levels, cy, cx), f32),
            shape(cy, cx),
            shape(cy, cx),
            shape(cx, cy),
            shape(cx, cy),
            shape(head + 3 * EDGE, cy),
            shape(head + own + nt * levels, cy),
            shape(nt * levels + rim, cy),
            shape(nt * levels + rim, cy),
        ],
        scratch_shapes=[
            pltpu.VMEM((cy, cx), f32),
            pltpu.VMEM((width, 128), f32),
            pltpu.VMEM((2, EDGE, full), f32),
            pltpu.VMEM(land_blocks.shape, jnp.int32),
            pltpu.SMEM((levels,), f32),
            pltpu.SemaphoreType.DMA((10,)),
        ],
        compiler_params=PARAMS,
        name="level_sum",
    )(*map(in_hbm, (layer_weight, land_blocks, theta, kappa, diag)))

    pairs_b = [(i, (i + 1) % lons if i % 2 else (i - 1) % lons) for i in range(lons)]
    mirror = [(i, lons - 1 - i) for i in range(lons)]
    got_a = lax.ppermute(pay_a, "lon", [(i, i ^ 1) for i in range(lons)])
    if pairs_b == mirror:
        got_b = lax.ppermute(jnp.concatenate([pay_b, got_a[head:]], axis=0), "lon", pairs_b)
        fold, at_fold = got_b, head + own
        folds = (got_b, got_b, pay_b)
        corners = (pay_b, got_a, got_b, got_b)
        tail = at_fold + nt * levels
        places = (head, tail, head, (at_fold - EDGE, head + 2 * EDGE, at_fold - EDGE, tail + 2 * EDGE))
    else:
        got_b = lax.ppermute(pay_b, "lon", pairs_b)
        fold = lax.ppermute(jnp.concatenate([pay_b[head:], got_a[head:], got_b[head:]], axis=0), "lon", mirror)
        at_fold = own
        folds = (fold, fold, fold)
        corners = (lax.psum(pay_a[head + 2 * EDGE :], "lon"),)
        tail = own + nt * levels
        places = (0, tail, tail + 3 * EDGE, (0,))
    chunks = pl.pallas_call(
        functools.partial(forcing_kernel, last, width, places),
        in_specs=[VMEM] * (7 + len(corners)),
        out_specs=VMEM,
        out_shape=shape(lats, width + 2 * EDGE, cy),
        compiler_params=PARAMS,
        name="forcing",
    )(tt, kt, got_a, got_b, *folds, *corners)
    chunks, row_a = lax.optimization_barrier((chunks, row_a))
    got = lax.all_to_all(chunks, "lat", split_axis=0, concat_axis=0, tiled=True)

    rows_a = lax.ppermute(row_a, joint, [(i, i ^ 1) for i in range(devices)])
    rows_b = lax.ppermute(row_b, joint, [(i, (i + 1 if i % 2 else i - 1) % devices) for i in range(devices)])
    new_theta = pl.pallas_call(
        functools.partial(tracer_kernel, last, at_fold),
        in_specs=[VMEM] * 8,
        out_specs=HBM,
        out_shape=shape(levels, cy, cx),
        scratch_shapes=[pltpu.VMEM((levels, cy, cx), f32), pltpu.SemaphoreType.DMA((levels // 2,))],
        compiler_params=PARAMS,
        cost_estimate=pl.CostEstimate(flops=12 * levels * cy * cx, bytes_accessed=8 * levels * cy * cx, transcendentals=0),
        name="tracer",
    )(held, ocean, coef, got_a, got_b, rows_a, rows_b, fold)

    basis, gram = pl.pallas_call(
        functools.partial(krylov_kernel, cell, nt * levels),
        in_specs=[VMEM] * 5,
        out_specs=[VMEM, VMEM],
        out_shape=[shape(ITERS, width, full), shape(devices, 128)],
        compiler_params=PARAMS,
        name="krylov",
    )(land_blocks, got, diag, rows_a, rows_b)
    gram = lax.all_to_all(gram, joint, split_axis=0, concat_axis=0, tiled=True)
    psi = pl.pallas_call(
        combine_kernel,
        in_specs=[VMEM, VMEM],
        out_specs=VMEM,
        out_shape=shape(width, full),
        compiler_params=PARAMS,
        name="combine",
    )(gram, basis)
    return new_theta, psi


def solution(mesh):
    return jax.shard_map(
        per_device,
        mesh=mesh,
        in_specs=(P(None, "lat", "lon"), P("lat", "lon"), P(), P(("lon", "lat"), None), P()),
        out_specs=(P(None, "lat", "lon"), P(("lon", "lat"), None)),
        check_vma=False,
    )
```

```python
import functools

import jax
import jax.numpy as jnp
from jax import lax
from jax.experimental import pallas as pl
from jax.experimental.pallas import tpu as pltpu
from jax.sharding import PartitionSpec as P

ITERS = 4
EDGE = 8
HALO = ITERS
RIM = HALO - 1
CENTRE = 5.1
WIDTH = 4.9
VMEM = pl.BlockSpec(memory_space=pltpu.VMEM)
SMEM = pl.BlockSpec(memory_space=pltpu.SMEM)
HBM = pl.BlockSpec(memory_space=pltpu.HBM)
EXACT = lax.Precision.HIGHEST
PARAMS = pltpu.CompilerParams(vmem_limit_bytes=32 * 1024 * 1024)


def in_hbm(x):
    return pltpu.with_memory_space_constraint(x, pltpu.HBM)


def iota(shape, dim):
    return lax.broadcasted_iota(jnp.int32, shape, dim)


def ones_at(hit):
    return jnp.where(hit, 1.0, 0.0).astype(jnp.float32)


def mat(a, b, precision=None):
    return jnp.dot(a, b, precision=precision, preferred_element_type=jnp.float32)


def turn(x, shift, dim):
    return pltpu.roll(x, shift % x.shape[dim] if isinstance(shift, int) else shift, dim)


def beside(v):
    return turn(v, 1, 0) + turn(v, -1, 0) + turn(v, 1, 1) + turn(v, -1, 1)


def block_mask(table, row0, rows, col0, cols, cell):
    down, across = table.shape
    pick_rows = ones_at(lax.div(row0 + iota((rows, down), 0), cell) == iota((rows, down), 1))
    pick_cols = ones_at(lax.div(col0 + iota((across, cols), 1), cell) == iota((across, cols), 0))
    return mat(mat(pick_rows, table), pick_cols)


def sum_kernel(cell, weight_hbm, table_hbm, theta_hbm, kappa_hbm, diag_hbm, theta, ocean, coef, tt, kt, pay_a, pay_b, pay_c, pay_d, row_a, row_b, kappa, corner, rim, table, weight, sems):
    levels, cy, cx = theta.shape
    width, full = diag_hbm.shape
    copies = [
        pltpu.make_async_copy(table_hbm, table, sems.at[0]),
        pltpu.make_async_copy(weight_hbm, weight, sems.at[1]),
        pltpu.make_async_copy(kappa_hbm, kappa, sems.at[2]),
        pltpu.make_async_copy(diag_hbm.at[:, pl.ds(full - 128, 128)], corner, sems.at[3]),
        pltpu.make_async_copy(diag_hbm.at[pl.ds(0, EDGE)], rim.at[0], sems.at[4]),
        pltpu.make_async_copy(diag_hbm.at[pl.ds(width - EDGE, EDGE)], rim.at[1], sems.at[5]),
    ]
    pieces = 4
    some = levels // pieces
    for n in range(pieces):
        copies.append(pltpu.make_async_copy(theta_hbm.at[pl.ds(n * some, some)], theta.at[pl.ds(n * some, some)], sems.at[6 + n]))
    for copy in copies:
        copy.start()
    lon, lat = lax.axis_index("lon"), lax.axis_index("lat")
    even = lax.rem(lon, 2) == 0
    even_row = lax.rem(lat, 2) == 0
    copies[0].wait()
    mask = block_mask(table[...].astype(jnp.float32), lat * cy, cy, lon * cx, cx, cell)
    copies[3].wait()
    column = jnp.concatenate([corner[...], jnp.zeros((128 - width, 128), jnp.float32)], axis=0).T
    column = turn(column[128 - EDGE :], lon * width, 1)
    copies[4].wait()
    copies[5].wait()
    at = cx // cy * levels
    for c in range(full // cy):
        w = rim[0, :RIM, c * cy : (c + 1) * cy]
        e = rim[1, EDGE - RIM :, c * cy : (c + 1) * cy]
        row_a[at : at + RIM, :] = jnp.where(even_row, e, w)
        row_b[at : at + RIM, :] = jnp.where(even_row, w, e)
        at += RIM
    copies[2].wait()
    kappas = kappa[...]
    ocean[...] = mask
    coef[...] = mask * kappas
    ktv = kappas.T
    kt[...] = ktv

    lane = iota((cy, 128), 1)
    total = jnp.zeros((cy, cx), jnp.float32)
    sides = jnp.zeros((cy, 128), jnp.float32)
    copies[1].wait()
    for n in range(pieces):
        copies[6 + n].wait()
        for k in range(n * some, n * some + some):
            th = theta[k]
            total = total + weight[k] * th
            sides = jnp.where(lane == k, turn(th[:, :128], k, 1), sides)
            sides = jnp.where(lane == levels + k, turn(th[:, cx - 128 :], levels + k + 1, 1), sides)
    t = mask * total
    ttv = t.T
    tt[...] = ttv
    sidest = (sides * jnp.where(lane < levels, mask[:, :1], mask[:, cx - 1 :])).T
    west, east = sidest[:levels], sidest[levels : 2 * levels]
    pay_a[2 * EDGE : 2 * EDGE + levels, :] = jnp.where(even, east, west)
    pay_d[:levels, :] = jnp.where(even, west, east)
    for at, turned in ((0, ttv), (EDGE, ktv)):
        w, e = turned[:EDGE], turned[cx - EDGE :]
        pay_a[at : at + EDGE, :] = jnp.where(even, e, w)
        pay_b[at : at + EDGE, :] = jnp.where(even, w, e)
    at = 2 * EDGE
    flip = ones_at(iota((cx, cx), 0) + iota((cx, cx), 1) == cx - 1)
    both = jnp.concatenate([t[cy - EDGE :], kappas[cy - EDGE :, :]], axis=0)
    turned = mat(both, flip, EXACT)
    nt = cx // cy
    for base in (0, EDGE):
        for r in range(EDGE):
            row = turned[base + EDGE - 1 - r : base + EDGE - r]
            pay_c[base + r : base + r + 1, :] = jnp.where(even, row[:, :cy], row[:, cx - cy :])
            for c in range(nt):
                to_b = at + (base // EDGE * nt + c) * EDGE + r
                pay_b[to_b : to_b + 1, :] = row[:, c * cy : (c + 1) * cy]
    pay_a[at + levels :, :] = column
    pay_c[2 * EDGE :, :] = column
    pay_b[at + 2 * nt * EDGE :, :] = column
    top = theta[:, cy - 1, :] * mask[cy - 1 :, :]
    bottom = theta[:, 0, :] * mask[:1, :]
    for c in range(nt):
        t, b = top[:, c * cy : (c + 1) * cy], bottom[:, c * cy : (c + 1) * cy]
        row_a[c * levels : (c + 1) * levels, :] = jnp.where(even_row, t, b)
        row_b[c * levels : (c + 1) * levels, :] = jnp.where(even_row, b, t)
        pay_d[(c + 1) * levels : (c + 2) * levels, :] = t


def forcing_kernel(last, width, places, tt, kt, got_a, got_b, tops_m, tops_a, tops_b, *rest):
    *corners, out = rest
    at_m, at_a, at_b, at_corners = places
    cx, cy = tt.shape
    lon, lat = lax.axis_index("lon"), lax.axis_index("lat")
    even = lax.rem(lon, 2) == 0
    nt = cx // cy

    stack = []
    for which in (0, 1):
        a = tops_a[at_a + which * EDGE : at_a + (which + 1) * EDGE, :]
        b_first = tops_b[at_b + which * nt * EDGE : at_b + (which * nt + 1) * EDGE, :]
        b_last = tops_b[at_b + (which * nt + nt - 1) * EDGE : at_b + (which * nt + nt) * EDGE, :]
        stack.append(jnp.where(even, b_last, a))
        for c in range(nt):
            stack.append(tops_m[at_m + (which * nt + c) * EDGE : at_m + (which * nt + c + 1) * EDGE, :])
        stack.append(jnp.where(even, a, b_first))
    used = len(stack) * EDGE
    stack = jnp.concatenate(stack + [jnp.zeros((cy - used, cy), jnp.float32)], axis=0).T
    fold_lane = (iota((cy, cy), 1) < EDGE) & (lat == last)

    def extended(own, at, which):
        a = got_a[at : at + EDGE, :]
        b = got_b[at : at + EDGE, :]
        rows = jnp.concatenate([jnp.where(even, b, a), own, jnp.where(even, a, b)], axis=0)
        first = which * (nt + 2)
        tiles = [jnp.where(fold_lane, turn(stack, -(first + n) * EDGE, 1), 0.0) for n in range(nt + 2)]
        fold = jnp.concatenate([tiles[0][cy - EDGE :]] + tiles[1:-1] + [tiles[-1][:EDGE]], axis=0)
        return jnp.concatenate([rows, fold], axis=1)

    t = extended(tt[...], 0, 0)
    k = extended(kt[...], EDGE, 1)
    f = t + k * (beside(t) - 4.0 * t)
    rows = cx + 2 * EDGE
    lane = iota((rows, cy), 1)
    t0, k0 = t[:, :cy], k[:, :cy]
    pack = jnp.where(lane == 0, t0, 0.0)
    pack = jnp.where(lane == 1, turn(t0, 2, 1), pack)
    pack = jnp.where(lane == 2, turn(k0, 2, 1), pack)
    pack = jnp.where(lane == 3, turn(k0, 4, 1), pack)
    pack = jnp.where((lane >= 4) & (lane < 8), turn(f[:, cy:], 4, 1), pack)
    wide = -(-rows // 128) * 128
    pack = jnp.concatenate([pack, jnp.zeros((wide - rows, cy), jnp.float32)], axis=0).T[:8]
    low = iota((EDGE, cy), 0) < HALO
    corner = sum(ref[at : at + EDGE, :] for ref, at in zip(corners, at_corners))
    corner = jnp.where(low, turn(turn(corner, HALO, 0), 64, 1), corner)
    in_pack = iota((EDGE, cy), 1) < 64
    for d in range(cx // width):
        at = EDGE + d * width
        out[d, :width, :] = f[at : at + width, :cy]
        out[d, width : width + EDGE, :] = jnp.where(low, f[at + width : at + width + EDGE, :cy], f[at - EDGE : at, :cy])
        out[d, width + EDGE :, :] = jnp.where(in_pack, turn(pack, -d * width, 1)[:, :128], corner)


def strip_order(columns, width):
    low = iota((EDGE, columns.shape[1]), 0) < HALO
    ends = jnp.where(low, columns[EDGE + width : 2 * EDGE + width], columns[:EDGE])
    return jnp.concatenate([columns[EDGE : EDGE + width], ends], axis=0)


def krylov_kernel(cell, start, table, got, diag, rows_a, rows_b, basis, gram):
    count, chunk, cy = got.shape
    width, full = diag.shape
    rows = width + EDGE
    lon, lat = lax.axis_index("lon"), lax.axis_index("lat")
    x0 = (lon * count + lat) * width
    down, across = table.shape
    nx = across * cell
    lons = nx // (count * width)

    edges = jnp.concatenate([got[s, rows:, :] for s in range(count)], axis=0)
    if edges.shape[0] < 128:
        edges = jnp.concatenate([edges, jnp.zeros((128 - edges.shape[0], cy), jnp.float32)], axis=0)
    edges = strip_order(edges.T, width)
    from_south = edges * turn(edges, 9, 1)
    from_north = edges * turn(edges, -5, 1)
    lane = iota((rows, cy), 1)
    parts = []
    for s in range(count):
        part = got[s, :rows, :]
        if s > 0:
            part = part + jnp.where(lane == 0, turn(from_south, -(8 * s + 2), 1), 0.0)
        if s < count - 1:
            part = part + jnp.where(lane == cy - 1, turn(from_north, cy - 1 - (8 * s + 3), 1), 0.0)
        parts.append(part)
    parts.append(jnp.where(lane < HALO, turn(edges, -(8 * (count - 1) + 4), 1), 0.0))
    f = jnp.concatenate(parts, axis=1)

    place = iota((rows, across), 0)
    x = x0 + jnp.where(place < width + HALO, place, place - rows)
    x = jnp.where(x < 0, x + nx, jnp.where(x >= nx, x - nx, x))
    cells = iota((rows, across), 1)
    here = ones_at(lax.div(x, cell) == cells)
    there = ones_at(lax.div(nx - 1 - x, cell) == cells)
    up = ones_at(lax.div(iota((down, full), 1), cell) == iota((down, full), 0))
    above = ones_at((iota((down, cy), 0) == down - 1) & (iota((down, cy), 1) < HALO))
    land = table[...].astype(jnp.float32)
    pick = lax.dot_general(jnp.concatenate([here, there], axis=0), land, (((1,), (1,)), ((), ())), preferred_element_type=jnp.float32)
    mask = jnp.concatenate([mat(pick[:rows], up), mat(pick[rows:], above)], axis=1)

    even_row = lax.rem(lat, 2) == 0
    rim = full // cy * RIM
    d_a, d_b = rows_a[start : start + rim, :], rows_b[start : start + rim, :]
    d_east, d_west = jnp.where(even_row, d_a, d_b), jnp.where(even_row, d_b, d_a)
    unused = jnp.zeros((EDGE - 2 * RIM, cy), jnp.float32)
    d_ends = [
        jnp.concatenate([d_east[c * RIM : (c + 1) * RIM], unused, d_west[c * RIM : (c + 1) * RIM]], axis=0) for c in range(full // cy)
    ]
    d_main = jnp.concatenate([diag[...], jnp.concatenate(d_ends, axis=1)], axis=0)

    mine = lon * count + lat
    total = lons * count
    tiles = []
    for strip in (total - 1 - mine, lax.rem(2 * total - 2 - mine, total), lax.rem(total - mine, total)):
        tile = got[lax.rem(strip, count)][rows:, :]
        tile = jnp.where(iota((EDGE, 128), 1) < 64, turn(turn(tile, HALO, 0), 64, 1), tile)
        tiles.append(turn(tile, lax.rem(128 - lax.div(strip, count) * width, 128), 1))
    here = iota((128, 128), 0)
    there = iota((128, 128), 1)
    picks = [
        (here + there == width - 1) & (there < width),
        (here + there == 2 * width - 1) & (there >= width) & (there < width + HALO),
        (here + there == rows - 1) & (there >= rows - HALO) & (there < rows),
    ]
    fold = sum(mat(tile, ones_at(pick), EXACT) for tile, pick in zip(tiles, picks))
    fold = [fold[EDGE - 1 - r : EDGE - r] for r in range(HALO)] + [jnp.zeros((128 - HALO, 128), jnp.float32)]
    d_all = jnp.concatenate([d_main, jnp.concatenate(fold, axis=0).T[:rows]], axis=1)

    near = mask * (1.0 / WIDTH)
    centre = near * ((4.0 - CENTRE) + d_all)
    p = [mask * f]
    p.append(centre * p[0] - near * beside(p[0]))
    for j in range(2, ITERS + 1):
        p.append(2.0 * (centre * p[j - 1] - near * beside(p[j - 1])) - p[j - 2])
    for j in range(ITERS):
        basis[j] = p[j][:width, :full]
    sums = []
    for i in range(ITERS):
        for j in range(i, ITERS + 1):
            both = p[i][:width, :full] * p[j][:width, :full]
            both = sum(both[:, c : c + 128] for c in range(0, full, 128))
            sums.append(jnp.sum(both, axis=0, keepdims=True))
    sums = jnp.concatenate(sums + [jnp.zeros((128 - len(sums), 128), jnp.float32)], axis=0)
    gram[...] = jnp.broadcast_to(jnp.sum(sums.T, axis=0, keepdims=True), gram.shape)


def combine_kernel(gram, basis, psi):
    g = jnp.sum(gram[...], axis=0, keepdims=True)
    pairs = [(i, j) for i in range(ITERS) for j in range(i, ITERS + 1)]
    at = {}
    for n, (i, j) in enumerate(pairs):
        at[i, j] = at[j, i] = jnp.broadcast_to(g[:, n : n + 1], (8, 128))

    def applied(i, j):
        if j == 0:
            return CENTRE * at[i, 0] + WIDTH * at[i, 1]
        return CENTRE * at[i, j] + (0.5 * WIDTH) * (at[i, j + 1] + at[i, j - 1])

    a = {(i, j): applied(i, j) for i in range(ITERS) for j in range(i, ITERS)}
    b = [at[i, 0] for i in range(ITERS)]
    inverse = []
    for k in range(ITERS):
        inverse.append(1.0 / a[k, k])
        for i in range(k + 1, ITERS):
            factor = a[k, i] * inverse[k]
            for j in range(i, ITERS):
                a[i, j] = a[i, j] - factor * a[k, j]
            b[i] = b[i] - factor * b[k]
    c = [None] * ITERS
    for i in reversed(range(ITERS)):
        value = b[i]
        for j in range(i + 1, ITERS):
            value = value - a[i, j] * c[j]
        c[i] = value * inverse[i]
    total = c[0][:1, :1] * basis[0]
    for j in range(1, ITERS):
        total = total + c[j][:1, :1] * basis[j]
    psi[...] = total


def tracer_kernel(last, start, theta, ocean, coef, got_a, got_d, rows_a, rows_b, fold, out_hbm, out, sems):
    levels, cy, cx = theta.shape
    lon, lat = lax.axis_index("lon"), lax.axis_index("lat")
    even = lax.rem(lon, 2) == 0
    a, b = got_a[2 * EDGE : 2 * EDGE + levels, :], got_d[:levels, :]
    both = jnp.concatenate([jnp.where(even, a, b), jnp.where(even, b, a), jnp.zeros((128 - 2 * levels, cy), jnp.float32)], axis=0)
    sides = both.T
    even_row = lax.rem(lat, 2) == 0

    def joined(ref, at=0):
        return jnp.concatenate([ref[at + c * levels : at + (c + 1) * levels, :] for c in range(cx // cy)], axis=1)

    a, b = joined(rows_a), joined(rows_b)
    flip = ones_at(iota((cx, cx), 0) + iota((cx, cx), 1) == cx - 1)
    north = jnp.where(lat == last, mat(joined(fold, start), flip, EXACT), jnp.where(even_row, a, b))
    south = jnp.where(lat == 0, 0.0, jnp.where(even_row, b, a))

    lane = iota((cy, 128), 1)
    row = iota((cy, cx), 0)
    mask, scale = ocean[...], coef[...]
    some = 2
    copies = []
    for k in range(levels):
        th = theta[k]
        m = mask * th
        east, west = turn(m, -1, 1), turn(m, 1, 1)
        east = jnp.concatenate([east[:, : cx - 128], jnp.where(lane == 127, turn(sides, 127 - k, 1), east[:, cx - 128 :])], axis=1)
        west = jnp.concatenate([jnp.where(lane == 0, turn(sides, -levels - k, 1), west[:, :128]), west[:, 128:]], axis=1)
        above = jnp.where(row == cy - 1, north[k : k + 1], turn(m, -1, 0))
        below = jnp.where(row == 0, south[k : k + 1], turn(m, 1, 0))
        out[k] = th + scale * (east + west + above + below - 4.0 * m)
        if (k + 1) % some == 0:
            n = k // some
            piece = pl.ds(n * some, some)
            copies.append(pltpu.make_async_copy(out.at[piece], out_hbm.at[piece], sems.at[n]))
            copies[-1].start()
    for copy in copies:
        copy.wait()


def per_device(theta, kappa, layer_weight, diag, land_blocks):
    lons, lats = lax.axis_size("lon"), lax.axis_size("lat")
    joint = ("lon", "lat")
    devices = lons * lats
    levels, cy, cx = theta.shape
    width, full = diag.shape
    cell = full // land_blocks.shape[0]
    last = lats - 1
    f32 = jnp.float32
    shape = lambda *dims: jax.ShapeDtypeStruct(dims, f32)

    nt = cx // cy
    head = 2 * EDGE
    own = (2 * nt + 1) * EDGE
    rim = RIM * (full // cy)
    held, ocean, coef, tt, kt, pay_a, pay_b, pay_c, pay_d, row_a, row_b = pl.pallas_call(
        functools.partial(sum_kernel, cell),
        in_specs=[HBM] * 5,
        out_specs=[VMEM] * 11,
        out_shape=[
            pltpu.VMEM((levels, cy, cx), f32),
            shape(cy, cx),
            shape(cy, cx),
            shape(cx, cy),
            shape(cx, cy),
            shape(head + levels + EDGE, cy),
            shape(head + own, cy),
            shape(3 * EDGE, cy),
            shape((nt + 1) * levels, cy),
            shape(nt * levels + rim, cy),
            shape(nt * levels + rim, cy),
        ],
        scratch_shapes=[
            pltpu.VMEM((cy, cx), f32),
            pltpu.VMEM((width, 128), f32),
            pltpu.VMEM((2, EDGE, full), f32),
            pltpu.VMEM(land_blocks.shape, jnp.int32),
            pltpu.SMEM((levels,), f32),
            pltpu.SemaphoreType.DMA((10,)),
        ],
        compiler_params=PARAMS,
        name="level_sum",
    )(*map(in_hbm, (layer_weight, land_blocks, theta, kappa, diag)))

    pairs_b = [(i, (i + 1) % lons if i % 2 else (i - 1) % lons) for i in range(lons)]
    mirror = [(i, lons - 1 - i) for i in range(lons)]
    got_a = lax.ppermute(pay_a, "lon", [(i, i ^ 1) for i in range(lons)])
    got_b = lax.ppermute(pay_b, "lon", pairs_b)
    if pairs_b == mirror:
        got_c = lax.ppermute(pay_c, "lon", [(i, i ^ 2) for i in range(lons)])
        folds = (got_b, got_c, pay_b)
        corners = (pay_b, got_a, got_b, got_c)
        tail = head + own - EDGE
        places = (head, 0, head, (tail, head + levels, tail, 2 * EDGE))
    else:
        got_c = lax.ppermute(pay_c, "lon", [(i, i ^ 1) for i in range(lons)])
        tops = lax.ppermute(jnp.concatenate([pay_b[head:], got_c, got_b[head:]], axis=0), "lon", mirror)
        folds = (tops, tops, tops)
        corners = (lax.psum(pay_c[2 * EDGE :], "lon"),)
        places = (0, own, own + 3 * EDGE, (0,))
    chunks = pl.pallas_call(
        functools.partial(forcing_kernel, last, width, places),
        in_specs=[VMEM] * (7 + len(corners)),
        out_specs=VMEM,
        out_shape=shape(lats, width + 2 * EDGE, cy),
        compiler_params=PARAMS,
        name="forcing",
    )(tt, kt, got_a, got_b, *folds, *corners)
    chunks, row_a, pay_d = lax.optimization_barrier((chunks, row_a, pay_d))
    got = lax.all_to_all(chunks, "lat", split_axis=0, concat_axis=0, tiled=True)

    rows_a = lax.ppermute(row_a, joint, [(i, i ^ 1) for i in range(devices)])
    rows_b = lax.ppermute(row_b, joint, [(i, (i + 1 if i % 2 else i - 1) % devices) for i in range(devices)])
    got_d = lax.ppermute(pay_d, "lon", pairs_b)
    got, got_d = lax.optimization_barrier((got, got_d))
    fold = got_d if pairs_b == mirror else lax.ppermute(pay_d, "lon", mirror)
    new_theta = pl.pallas_call(
        functools.partial(tracer_kernel, last, levels),
        in_specs=[VMEM] * 8,
        out_specs=HBM,
        out_shape=shape(levels, cy, cx),
        scratch_shapes=[pltpu.VMEM((levels, cy, cx), f32), pltpu.SemaphoreType.DMA((levels // 2,))],
        compiler_params=PARAMS,
        cost_estimate=pl.CostEstimate(flops=12 * levels * cy * cx, bytes_accessed=8 * levels * cy * cx, transcendentals=0),
        name="tracer",
    )(held, ocean, coef, got_a, got_d, rows_a, rows_b, fold)

    basis, gram = pl.pallas_call(
        functools.partial(krylov_kernel, cell, nt * levels),
        in_specs=[VMEM] * 5,
        out_specs=[VMEM, VMEM],
        out_shape=[shape(ITERS, width, full), shape(devices, 128)],
        compiler_params=PARAMS,
        name="krylov",
    )(land_blocks, got, diag, rows_a, rows_b)
    gram = lax.all_to_all(gram, joint, split_axis=0, concat_axis=0, tiled=True)
    psi = pl.pallas_call(
        combine_kernel,
        in_specs=[VMEM, VMEM],
        out_specs=VMEM,
        out_shape=shape(width, full),
        compiler_params=PARAMS,
        name="combine",
    )(gram, basis)
    return new_theta, psi


def solution(mesh):
    return jax.shard_map(
        per_device,
        mesh=mesh,
        in_specs=(P(None, "lat", "lon"), P("lat", "lon"), P(), P(("lon", "lat"), None), P()),
        out_specs=(P(None, "lat", "lon"), P(("lon", "lat"), None)),
        check_vma=False,
    )
```

```python
import functools

import jax
import jax.numpy as jnp
from jax import lax
from jax.experimental import pallas as pl
from jax.experimental.pallas import tpu as pltpu
from jax.sharding import PartitionSpec as P

ITERS = 4
EDGE = 8
HALO = ITERS
RIM = HALO - 1
CENTRE = 5.1
WIDTH = 4.9
VMEM = pl.BlockSpec(memory_space=pltpu.VMEM)
SMEM = pl.BlockSpec(memory_space=pltpu.SMEM)
HBM = pl.BlockSpec(memory_space=pltpu.HBM)
EXACT = lax.Precision.HIGHEST
PARAMS = pltpu.CompilerParams(vmem_limit_bytes=32 * 1024 * 1024)


def in_hbm(x):
    return pltpu.with_memory_space_constraint(x, pltpu.HBM)


def iota(shape, dim):
    return lax.broadcasted_iota(jnp.int32, shape, dim)


def ones_at(hit):
    return jnp.where(hit, 1.0, 0.0).astype(jnp.float32)


def mat(a, b, precision=None):
    return jnp.dot(a, b, precision=precision, preferred_element_type=jnp.float32)


def turn(x, shift, dim):
    return pltpu.roll(x, shift % x.shape[dim] if isinstance(shift, int) else shift, dim)


def beside(v):
    return turn(v, 1, 0) + turn(v, -1, 0) + turn(v, 1, 1) + turn(v, -1, 1)


def block_mask(table, row0, rows, col0, cols, cell):
    down, across = table.shape
    pick_rows = ones_at(lax.div(row0 + iota((rows, down), 0), cell) == iota((rows, down), 1))
    pick_cols = ones_at(lax.div(col0 + iota((across, cols), 1), cell) == iota((across, cols), 0))
    return mat(mat(pick_rows, table), pick_cols)


def sum_kernel(cell, weight_hbm, table_hbm, theta_hbm, kappa_hbm, diag_hbm, theta, ocean, coef, tt, kt, pay_a, pay_b, pay_c, row_a, row_b, ns_b, kappa, corner, rim, table, weight, sems):
    levels, cy, cx = theta.shape
    width, full = diag_hbm.shape
    copies = [
        pltpu.make_async_copy(table_hbm, table, sems.at[0]),
        pltpu.make_async_copy(weight_hbm, weight, sems.at[1]),
        pltpu.make_async_copy(kappa_hbm, kappa, sems.at[2]),
        pltpu.make_async_copy(diag_hbm.at[:, pl.ds(full - 128, 128)], corner, sems.at[3]),
        pltpu.make_async_copy(diag_hbm.at[pl.ds(0, EDGE)], rim.at[0], sems.at[4]),
        pltpu.make_async_copy(diag_hbm.at[pl.ds(width - EDGE, EDGE)], rim.at[1], sems.at[5]),
    ]
    pieces = 4
    some = levels // pieces
    for n in range(pieces):
        copies.append(pltpu.make_async_copy(theta_hbm.at[pl.ds(n * some, some)], theta.at[pl.ds(n * some, some)], sems.at[6 + n]))
    for copy in copies:
        copy.start()
    lon, lat = lax.axis_index("lon"), lax.axis_index("lat")
    even = lax.rem(lon, 2) == 0
    even_row = lax.rem(lat, 2) == 0
    copies[0].wait()
    mask = block_mask(table[...].astype(jnp.float32), lat * cy, cy, lon * cx, cx, cell)
    copies[3].wait()
    column = jnp.concatenate([corner[...], jnp.zeros((128 - width, 128), jnp.float32)], axis=0).T
    column = turn(column[128 - EDGE :], lon * width, 1)
    copies[4].wait()
    copies[5].wait()
    at = cx // cy * levels
    for c in range(full // cy):
        w = rim[0, :RIM, c * cy : (c + 1) * cy]
        e = rim[1, EDGE - RIM :, c * cy : (c + 1) * cy]
        row_a[at : at + RIM, :] = jnp.where(even_row, e, w)
        row_b[c * RIM : (c + 1) * RIM, :] = jnp.where(even_row, w, e)
        at += RIM
    copies[2].wait()
    kappas = kappa[...]
    ocean[...] = mask
    coef[...] = mask * kappas
    ktv = kappas.T
    kt[...] = ktv

    lane = iota((cy, 128), 1)
    total = jnp.zeros((cy, cx), jnp.float32)
    sides = jnp.zeros((cy, 128), jnp.float32)
    copies[1].wait()
    for n in range(pieces):
        copies[6 + n].wait()
        for k in range(n * some, n * some + some):
            th = theta[k]
            total = total + weight[k] * th
            sides = jnp.where(lane == k, turn(th[:, :128], k, 1), sides)
            sides = jnp.where(lane == levels + k, turn(th[:, cx - 128 :], levels + k + 1, 1), sides)
    t = mask * total
    ttv = t.T
    tt[...] = ttv
    sidest = (sides * jnp.where(lane < levels, mask[:, :1], mask[:, cx - 1 :])).T
    west, east = sidest[:levels], sidest[levels : 2 * levels]
    pay_a[2 * EDGE : 2 * EDGE + levels, :] = jnp.where(even, east, west)
    pay_b[2 * EDGE : 2 * EDGE + levels, :] = jnp.where(even, west, east)
    for at, turned in ((0, ttv), (EDGE, ktv)):
        w, e = turned[:EDGE], turned[cx - EDGE :]
        pay_a[at : at + EDGE, :] = jnp.where(even, e, w)
        pay_b[at : at + EDGE, :] = jnp.where(even, w, e)
    at = 2 * EDGE + levels
    flip = ones_at(iota((cx, cx), 0) + iota((cx, cx), 1) == cx - 1)
    both = jnp.concatenate([t[cy - EDGE :], kappas[cy - EDGE :, :]], axis=0)
    turned = mat(both, flip, EXACT)
    nt = cx // cy
    for base in (0, EDGE):
        for r in range(EDGE):
            row = turned[base + EDGE - 1 - r : base + EDGE - r]
            pay_c[base + r : base + r + 1, :] = jnp.where(even, row[:, :cy], row[:, cx - cy :])
            for c in range(nt):
                to_b = at + (base // EDGE * nt + c) * EDGE + r
                pay_b[to_b : to_b + 1, :] = row[:, c * cy : (c + 1) * cy]
    pay_a[at:, :] = column
    pay_c[2 * EDGE :, :] = column
    pay_b[at + 2 * nt * EDGE :, :] = column
    top = theta[:, cy - 1, :] * mask[cy - 1 :, :]
    bottom = theta[:, 0, :] * mask[:1, :]
    for c in range(nt):
        t, b = top[:, c * cy : (c + 1) * cy], bottom[:, c * cy : (c + 1) * cy]
        row_a[c * levels : (c + 1) * levels, :] = jnp.where(even_row, t, b)
        ns_b[c * levels : (c + 1) * levels, :] = jnp.where(even_row, b, t)


def forcing_kernel(last, width, places, tt, kt, got_a, got_b, tops_m, tops_a, tops_b, *rest):
    *corners, out = rest
    at_m, at_a, at_b, at_corners = places
    cx, cy = tt.shape
    lon, lat = lax.axis_index("lon"), lax.axis_index("lat")
    even = lax.rem(lon, 2) == 0
    nt = cx // cy

    stack = []
    for which in (0, 1):
        a = tops_a[at_a + which * EDGE : at_a + (which + 1) * EDGE, :]
        b_first = tops_b[at_b + which * nt * EDGE : at_b + (which * nt + 1) * EDGE, :]
        b_last = tops_b[at_b + (which * nt + nt - 1) * EDGE : at_b + (which * nt + nt) * EDGE, :]
        stack.append(jnp.where(even, b_last, a))
        for c in range(nt):
            stack.append(tops_m[at_m + (which * nt + c) * EDGE : at_m + (which * nt + c + 1) * EDGE, :])
        stack.append(jnp.where(even, a, b_first))
    used = len(stack) * EDGE
    stack = jnp.concatenate(stack + [jnp.zeros((cy - used, cy), jnp.float32)], axis=0).T
    fold_lane = (iota((cy, cy), 1) < EDGE) & (lat == last)

    def extended(own, at, which):
        a = got_a[at : at + EDGE, :]
        b = got_b[at : at + EDGE, :]
        rows = jnp.concatenate([jnp.where(even, b, a), own, jnp.where(even, a, b)], axis=0)
        first = which * (nt + 2)
        tiles = [jnp.where(fold_lane, turn(stack, -(first + n) * EDGE, 1), 0.0) for n in range(nt + 2)]
        fold = jnp.concatenate([tiles[0][cy - EDGE :]] + tiles[1:-1] + [tiles[-1][:EDGE]], axis=0)
        return jnp.concatenate([rows, fold], axis=1)

    t = extended(tt[...], 0, 0)
    k = extended(kt[...], EDGE, 1)
    f = t + k * (beside(t) - 4.0 * t)
    rows = cx + 2 * EDGE
    lane = iota((rows, cy), 1)
    t0, k0 = t[:, :cy], k[:, :cy]
    pack = jnp.where(lane == 0, t0, 0.0)
    pack = jnp.where(lane == 1, turn(t0, 2, 1), pack)
    pack = jnp.where(lane == 2, turn(k0, 2, 1), pack)
    pack = jnp.where(lane == 3, turn(k0, 4, 1), pack)
    pack = jnp.where((lane >= 4) & (lane < 8), turn(f[:, cy:], 4, 1), pack)
    wide = -(-rows // 128) * 128
    pack = jnp.concatenate([pack, jnp.zeros((wide - rows, cy), jnp.float32)], axis=0).T[:8]
    low = iota((EDGE, cy), 0) < HALO
    corner = sum(ref[at : at + EDGE, :] for ref, at in zip(corners, at_corners))
    corner = jnp.where(low, turn(turn(corner, HALO, 0), 64, 1), corner)
    in_pack = iota((EDGE, cy), 1) < 64
    for d in range(cx // width):
        at = EDGE + d * width
        out[d, :width, :] = f[at : at + width, :cy]
        out[d, width : width + EDGE, :] = jnp.where(low, f[at + width : at + width + EDGE, :cy], f[at - EDGE : at, :cy])
        out[d, width + EDGE :, :] = jnp.where(in_pack, turn(pack, -d * width, 1)[:, :128], corner)


def strip_order(columns, width):
    low = iota((EDGE, columns.shape[1]), 0) < HALO
    ends = jnp.where(low, columns[EDGE + width : 2 * EDGE + width], columns[:EDGE])
    return jnp.concatenate([columns[EDGE : EDGE + width], ends], axis=0)


def krylov_kernel(cell, start, table, got, diag, rows_a, rows_b, basis, gram):
    count, chunk, cy = got.shape
    width, full = diag.shape
    rows = width + EDGE
    lon, lat = lax.axis_index("lon"), lax.axis_index("lat")
    x0 = (lon * count + lat) * width
    down, across = table.shape
    nx = across * cell
    lons = nx // (count * width)

    edges = jnp.concatenate([got[s, rows:, :] for s in range(count)], axis=0)
    if edges.shape[0] < 128:
        edges = jnp.concatenate([edges, jnp.zeros((128 - edges.shape[0], cy), jnp.float32)], axis=0)
    edges = strip_order(edges.T, width)
    from_south = edges * turn(edges, 9, 1)
    from_north = edges * turn(edges, -5, 1)
    lane = iota((rows, cy), 1)
    parts = []
    for s in range(count):
        part = got[s, :rows, :]
        if s > 0:
            part = part + jnp.where(lane == 0, turn(from_south, -(8 * s + 2), 1), 0.0)
        if s < count - 1:
            part = part + jnp.where(lane == cy - 1, turn(from_north, cy - 1 - (8 * s + 3), 1), 0.0)
        parts.append(part)
    parts.append(jnp.where(lane < HALO, turn(edges, -(8 * (count - 1) + 4), 1), 0.0))
    f = jnp.concatenate(parts, axis=1)

    place = iota((rows, across), 0)
    x = x0 + jnp.where(place < width + HALO, place, place - rows)
    x = jnp.where(x < 0, x + nx, jnp.where(x >= nx, x - nx, x))
    cells = iota((rows, across), 1)
    here = ones_at(lax.div(x, cell) == cells)
    there = ones_at(lax.div(nx - 1 - x, cell) == cells)
    up = ones_at(lax.div(iota((down, full), 1), cell) == iota((down, full), 0))
    above = ones_at((iota((down, cy), 0) == down - 1) & (iota((down, cy), 1) < HALO))
    land = table[...].astype(jnp.float32)
    pick = lax.dot_general(jnp.concatenate([here, there], axis=0), land, (((1,), (1,)), ((), ())), preferred_element_type=jnp.float32)
    mask = jnp.concatenate([mat(pick[:rows], up), mat(pick[rows:], above)], axis=1)

    even_row = lax.rem(lat, 2) == 0
    rim = full // cy * RIM
    d_a, d_b = rows_a[start : start + rim, :], rows_b[...]
    d_east, d_west = jnp.where(even_row, d_a, d_b), jnp.where(even_row, d_b, d_a)
    unused = jnp.zeros((EDGE - 2 * RIM, cy), jnp.float32)
    d_ends = [
        jnp.concatenate([d_east[c * RIM : (c + 1) * RIM], unused, d_west[c * RIM : (c + 1) * RIM]], axis=0) for c in range(full // cy)
    ]
    d_main = jnp.concatenate([diag[...], jnp.concatenate(d_ends, axis=1)], axis=0)

    mine = lon * count + lat
    total = lons * count
    tiles = []
    for strip in (total - 1 - mine, lax.rem(2 * total - 2 - mine, total), lax.rem(total - mine, total)):
        tile = got[lax.rem(strip, count)][rows:, :]
        tile = jnp.where(iota((EDGE, 128), 1) < 64, turn(turn(tile, HALO, 0), 64, 1), tile)
        tiles.append(turn(tile, lax.rem(128 - lax.div(strip, count) * width, 128), 1))
    here = iota((128, 128), 0)
    there = iota((128, 128), 1)
    picks = [
        (here + there == width - 1) & (there < width),
        (here + there == 2 * width - 1) & (there >= width) & (there < width + HALO),
        (here + there == rows - 1) & (there >= rows - HALO) & (there < rows),
    ]
    fold = sum(mat(tile, ones_at(pick), EXACT) for tile, pick in zip(tiles, picks))
    fold = [fold[EDGE - 1 - r : EDGE - r] for r in range(HALO)] + [jnp.zeros((128 - HALO, 128), jnp.float32)]
    d_all = jnp.concatenate([d_main, jnp.concatenate(fold, axis=0).T[:rows]], axis=1)

    near = mask * (1.0 / WIDTH)
    centre = near * ((4.0 - CENTRE) + d_all)
    p = [mask * f]
    p.append(centre * p[0] - near * beside(p[0]))
    for j in range(2, ITERS + 1):
        p.append(2.0 * (centre * p[j - 1] - near * beside(p[j - 1])) - p[j - 2])
    for j in range(ITERS):
        basis[j] = p[j][:width, :full]
    sums = []
    for i in range(ITERS):
        for j in range(i, ITERS + 1):
            both = p[i][:width, :full] * p[j][:width, :full]
            both = sum(both[:, c : c + 128] for c in range(0, full, 128))
            sums.append(jnp.sum(both, axis=0, keepdims=True))
    sums = jnp.concatenate(sums + [jnp.zeros((128 - len(sums), 128), jnp.float32)], axis=0)
    gram[...] = jnp.broadcast_to(jnp.sum(sums.T, axis=0, keepdims=True), gram.shape)


def combine_kernel(gram, basis, psi):
    g = jnp.sum(gram[...], axis=0, keepdims=True)
    pairs = [(i, j) for i in range(ITERS) for j in range(i, ITERS + 1)]
    at = {}
    for n, (i, j) in enumerate(pairs):
        at[i, j] = at[j, i] = jnp.broadcast_to(g[:, n : n + 1], (8, 128))

    def applied(i, j):
        if j == 0:
            return CENTRE * at[i, 0] + WIDTH * at[i, 1]
        return CENTRE * at[i, j] + (0.5 * WIDTH) * (at[i, j + 1] + at[i, j - 1])

    a = {(i, j): applied(i, j) for i in range(ITERS) for j in range(i, ITERS)}
    b = [at[i, 0] for i in range(ITERS)]
    inverse = []
    for k in range(ITERS):
        inverse.append(1.0 / a[k, k])
        for i in range(k + 1, ITERS):
            factor = a[k, i] * inverse[k]
            for j in range(i, ITERS):
                a[i, j] = a[i, j] - factor * a[k, j]
            b[i] = b[i] - factor * b[k]
    c = [None] * ITERS
    for i in reversed(range(ITERS)):
        value = b[i]
        for j in range(i + 1, ITERS):
            value = value - a[i, j] * c[j]
        c[i] = value * inverse[i]
    total = c[0][:1, :1] * basis[0]
    for j in range(1, ITERS):
        total = total + c[j][:1, :1] * basis[j]
    psi[...] = total


def rim_kernel(rows, out):
    out[...] = rows[...]


def tracer_kernel(last, theta, ocean, coef, got_a, got_b, rows_a, rows_b, out_hbm, out, sems):
    levels, cy, cx = theta.shape
    lon, lat = lax.axis_index("lon"), lax.axis_index("lat")
    even = lax.rem(lon, 2) == 0
    a, b = got_a[2 * EDGE : 2 * EDGE + levels, :], got_b[2 * EDGE : 2 * EDGE + levels, :]
    both = jnp.concatenate([jnp.where(even, a, b), jnp.where(even, b, a), jnp.zeros((128 - 2 * levels, cy), jnp.float32)], axis=0)
    sides = both.T
    even_row = lax.rem(lat, 2) == 0

    def joined(ref):
        return jnp.concatenate([ref[c * levels : (c + 1) * levels, :] for c in range(cx // cy)], axis=1)

    a, b = joined(rows_a), joined(rows_b)
    flip = ones_at(iota((cx, cx), 0) + iota((cx, cx), 1) == cx - 1)
    north = jnp.where(lat == last, mat(b, flip, EXACT), jnp.where(even_row, a, b))
    south = jnp.where(lat == 0, 0.0, jnp.where(even_row, b, a))

    lane = iota((cy, 128), 1)
    row = iota((cy, cx), 0)
    mask, scale = ocean[...], coef[...]
    some = 2
    copies = []
    for k in range(levels):
        th = theta[k]
        m = mask * th
        east, west = turn(m, -1, 1), turn(m, 1, 1)
        east = jnp.concatenate([east[:, : cx - 128], jnp.where(lane == 127, turn(sides, 127 - k, 1), east[:, cx - 128 :])], axis=1)
        west = jnp.concatenate([jnp.where(lane == 0, turn(sides, -levels - k, 1), west[:, :128]), west[:, 128:]], axis=1)
        above = jnp.where(row == cy - 1, north[k : k + 1], turn(m, -1, 0))
        below = jnp.where(row == 0, south[k : k + 1], turn(m, 1, 0))
        out[k] = th + scale * (east + west + above + below - 4.0 * m)
        if (k + 1) % some == 0:
            n = k // some
            piece = pl.ds(n * some, some)
            copies.append(pltpu.make_async_copy(out.at[piece], out_hbm.at[piece], sems.at[n]))
            copies[-1].start()
    for copy in copies:
        copy.wait()


def per_device(theta, kappa, layer_weight, diag, land_blocks):
    lons, lats = lax.axis_size("lon"), lax.axis_size("lat")
    joint = ("lon", "lat")
    devices = lons * lats
    levels, cy, cx = theta.shape
    width, full = diag.shape
    cell = full // land_blocks.shape[0]
    last = lats - 1
    f32 = jnp.float32
    shape = lambda *dims: jax.ShapeDtypeStruct(dims, f32)

    nt = cx // cy
    head = 2 * EDGE + levels
    own = (2 * nt + 1) * EDGE
    rim = RIM * (full // cy)
    held, ocean, coef, tt, kt, pay_a, pay_b, pay_c, row_a, row_b, ns_b = pl.pallas_call(
        functools.partial(sum_kernel, cell),
        in_specs=[HBM] * 5,
        out_specs=[VMEM] * 11,
        out_shape=[
            pltpu.VMEM((levels, cy, cx), f32),
            shape(cy, cx),
            shape(cy, cx),
            shape(cx, cy),
            shape(cx, cy),
            shape(head + EDGE, cy),
            shape(head + own, cy),
            shape(3 * EDGE, cy),
            shape(nt * levels + rim, cy),
            shape(rim, cy),
            shape(nt * levels, cy),
        ],
        scratch_shapes=[
            pltpu.VMEM((cy, cx), f32),
            pltpu.VMEM((width, 128), f32),
            pltpu.VMEM((2, EDGE, full), f32),
            pltpu.VMEM(land_blocks.shape, jnp.int32),
            pltpu.SMEM((levels,), f32),
            pltpu.SemaphoreType.DMA((10,)),
        ],
        compiler_params=PARAMS,
        name="level_sum",
    )(*map(in_hbm, (layer_weight, land_blocks, theta, kappa, diag)))

    pairs_b = [(i, (i + 1) % lons if i % 2 else (i - 1) % lons) for i in range(lons)]
    mirror = [(i, lons - 1 - i) for i in range(lons)]
    got_a = lax.ppermute(pay_a, "lon", [(i, i ^ 1) for i in range(lons)])
    got_b = lax.ppermute(pay_b, "lon", pairs_b)
    if pairs_b == mirror:
        got_c = lax.ppermute(pay_c, "lon", [(i, i ^ 2) for i in range(lons)])
        folds = (got_b, got_c, pay_b)
        corners = (pay_b, got_a, got_b, got_c)
        tail = head + own - EDGE
        places = (head, 0, head, (tail, head, tail, 2 * EDGE))
    else:
        got_c = lax.ppermute(pay_c, "lon", [(i, i ^ 1) for i in range(lons)])
        tops = lax.ppermute(jnp.concatenate([pay_b[head:], got_c, got_b[head:]], axis=0), "lon", mirror)
        folds = (tops, tops, tops)
        corners = (lax.psum(pay_c[2 * EDGE :], "lon"),)
        places = (0, own, own + 3 * EDGE, (0,))
    chunks = pl.pallas_call(
        functools.partial(forcing_kernel, last, width, places),
        in_specs=[VMEM] * (7 + len(corners)),
        out_specs=VMEM,
        out_shape=shape(lats, width + 2 * EDGE, cy),
        compiler_params=PARAMS,
        name="forcing",
    )(tt, kt, got_a, got_b, *folds, *corners)
    chunks, row_a, ns_b = lax.optimization_barrier((chunks, row_a, ns_b))
    got = lax.all_to_all(chunks, "lat", split_axis=0, concat_axis=0, tiled=True)

    rows_b = lax.ppermute(row_b, joint, [(i, (i + 1 if i % 2 else i - 1) % devices) for i in range(devices)])
    rim_b = pl.pallas_call(
        rim_kernel,
        in_specs=[VMEM],
        out_specs=VMEM,
        out_shape=shape(rim, cy),
        compiler_params=PARAMS,
        cost_estimate=pl.CostEstimate(flops=10**11, bytes_accessed=0, transcendentals=0),
        name="rim",
    )(rows_b)
    row_a, ns_b, rim_b = lax.optimization_barrier((row_a, ns_b, rim_b))
    rows_a = lax.ppermute(row_a, joint, [(i, i ^ 1) for i in range(devices)])
    second = []
    for lon in range(lons):
        second += [(lon * lats + lat, (lons - 1 - lon) * lats + lat) for lat in (0, last)]
        second += [(lon * lats + lat, lon * lats + (lat + 1 if lat % 2 else lat - 1)) for lat in range(1, last)]
    beyond = lax.ppermute(ns_b, joint, second)
    got, beyond = lax.optimization_barrier((got, beyond))
    new_theta = pl.pallas_call(
        functools.partial(tracer_kernel, last),
        in_specs=[VMEM] * 7,
        out_specs=HBM,
        out_shape=shape(levels, cy, cx),
        scratch_shapes=[pltpu.VMEM((levels, cy, cx), f32), pltpu.SemaphoreType.DMA((levels // 2,))],
        compiler_params=PARAMS,
        cost_estimate=pl.CostEstimate(flops=12 * levels * cy * cx, bytes_accessed=8 * levels * cy * cx, transcendentals=0),
        name="tracer",
    )(held, ocean, coef, got_a, got_b, rows_a, beyond)

    basis, gram = pl.pallas_call(
        functools.partial(krylov_kernel, cell, nt * levels),
        in_specs=[VMEM] * 5,
        out_specs=[VMEM, VMEM],
        out_shape=[shape(ITERS, width, full), shape(devices, 128)],
        compiler_params=PARAMS,
        name="krylov",
    )(land_blocks, got, diag, rows_a, rim_b)
    gram = lax.all_to_all(gram, joint, split_axis=0, concat_axis=0, tiled=True)
    psi = pl.pallas_call(
        combine_kernel,
        in_specs=[VMEM, VMEM],
        out_specs=VMEM,
        out_shape=shape(width, full),
        compiler_params=PARAMS,
        name="combine",
    )(gram, basis)
    return new_theta, psi


def solution(mesh):
    return jax.shard_map(
        per_device,
        mesh=mesh,
        in_specs=(P(None, "lat", "lon"), P("lat", "lon"), P(), P(("lon", "lat"), None), P()),
        out_specs=(P(None, "lat", "lon"), P(("lon", "lat"), None)),
        check_vma=False,
    )
```

```python
import functools

import jax
import jax.numpy as jnp
from jax import lax
from jax.experimental import pallas as pl
from jax.experimental.pallas import tpu as pltpu
from jax.sharding import PartitionSpec as P

ITERS = 4
EDGE = 8
HALO = ITERS
RIM = HALO - 1
CENTRE = 5.1
WIDTH = 4.9
VMEM = pl.BlockSpec(memory_space=pltpu.VMEM)
SMEM = pl.BlockSpec(memory_space=pltpu.SMEM)
HBM = pl.BlockSpec(memory_space=pltpu.HBM)
EXACT = lax.Precision.HIGHEST
PARAMS = pltpu.CompilerParams(vmem_limit_bytes=32 * 1024 * 1024)


def in_hbm(x):
    return pltpu.with_memory_space_constraint(x, pltpu.HBM)


def iota(shape, dim):
    return lax.broadcasted_iota(jnp.int32, shape, dim)


def ones_at(hit):
    return jnp.where(hit, 1.0, 0.0).astype(jnp.float32)


def mat(a, b, precision=None):
    return jnp.dot(a, b, precision=precision, preferred_element_type=jnp.float32)


def turn(x, shift, dim):
    return pltpu.roll(x, shift % x.shape[dim] if isinstance(shift, int) else shift, dim)


def beside(v):
    return turn(v, 1, 0) + turn(v, -1, 0) + turn(v, 1, 1) + turn(v, -1, 1)


def block_mask(table, row0, rows, col0, cols, cell):
    down, across = table.shape
    pick_rows = ones_at(lax.div(row0 + iota((rows, down), 0), cell) == iota((rows, down), 1))
    pick_cols = ones_at(lax.div(col0 + iota((across, cols), 1), cell) == iota((across, cols), 0))
    return mat(mat(pick_rows, table), pick_cols)


def sum_kernel(cell, weight_hbm, table_hbm, theta_hbm, kappa_hbm, diag_hbm, theta, ocean, coef, tt, kt, ends, pay_a, pay_b, pay_c, row_a, row_b, ns_b, kappa, corner, rim, table, weight, sems):
    levels, cy, cx = theta.shape
    width, full = diag_hbm.shape
    copies = [
        pltpu.make_async_copy(table_hbm, table, sems.at[0]),
        pltpu.make_async_copy(weight_hbm, weight, sems.at[1]),
        pltpu.make_async_copy(kappa_hbm, kappa, sems.at[2]),
        pltpu.make_async_copy(diag_hbm.at[:, pl.ds(full - 128, 128)], corner, sems.at[3]),
        pltpu.make_async_copy(diag_hbm.at[pl.ds(0, EDGE)], rim.at[0], sems.at[4]),
        pltpu.make_async_copy(diag_hbm.at[pl.ds(width - EDGE, EDGE)], rim.at[1], sems.at[5]),
    ]
    pieces = 4
    some = levels // pieces
    for n in range(pieces):
        copies.append(pltpu.make_async_copy(theta_hbm.at[pl.ds(n * some, some)], theta.at[pl.ds(n * some, some)], sems.at[6 + n]))
    for copy in copies:
        copy.start()
    lon, lat = lax.axis_index("lon"), lax.axis_index("lat")
    even = lax.rem(lon, 2) == 0
    even_row = lax.rem(lat, 2) == 0
    copies[0].wait()
    mask = block_mask(table[...].astype(jnp.float32), lat * cy, cy, lon * cx, cx, cell)
    copies[3].wait()
    column = jnp.concatenate([corner[...], jnp.zeros((128 - width, 128), jnp.float32)], axis=0).T
    column = turn(column[128 - EDGE :], lon * width, 1)
    copies[4].wait()
    copies[5].wait()
    at = cx // cy * levels
    for c in range(full // cy):
        w = rim[0, :RIM, c * cy : (c + 1) * cy]
        e = rim[1, EDGE - RIM :, c * cy : (c + 1) * cy]
        row_a[at : at + RIM, :] = jnp.where(even_row, e, w)
        row_b[c * RIM : (c + 1) * RIM, :] = jnp.where(even_row, w, e)
        at += RIM
    copies[2].wait()
    kappas = kappa[...]
    ocean[...] = mask
    coef[...] = mask * kappas
    ktv = kappas.T
    kt[...] = ktv

    lane = iota((cy, 128), 1)
    total = jnp.zeros((cy, cx), jnp.float32)
    sides = jnp.zeros((cy, 128), jnp.float32)
    copies[1].wait()
    for n in range(pieces):
        copies[6 + n].wait()
        for k in range(n * some, n * some + some):
            th = theta[k]
            total = total + weight[k] * th
            sides = jnp.where(lane == k, turn(th[:, :128], k, 1), sides)
            sides = jnp.where(lane == levels + k, turn(th[:, cx - 128 :], levels + k + 1, 1), sides)
    t = mask * total
    ttv = t.T
    tt[...] = ttv
    sidest = (sides * jnp.where(lane < levels, mask[:, :1], mask[:, cx - 1 :])).T
    west, east = sidest[:levels], sidest[levels : 2 * levels]
    pay_a[2 * EDGE : 2 * EDGE + levels, :] = jnp.where(even, east, west)
    pay_b[2 * EDGE : 2 * EDGE + levels, :] = jnp.where(even, west, east)
    for at, turned in ((0, ttv), (EDGE, ktv)):
        w, e = turned[:EDGE], turned[cx - EDGE :]
        pay_a[at : at + EDGE, :] = jnp.where(even, e, w)
        pay_b[at : at + EDGE, :] = jnp.where(even, w, e)
    at = 2 * EDGE + levels
    rows = jnp.concatenate([t[:1], t[cy - 1 :], kappas[:1], kappas[cy - 1 :], jnp.zeros((EDGE - 4, cx), jnp.float32)], axis=0)
    ends[...] = rows
    pay_a[at : at + EDGE, :] = jnp.where(even, rows[:, cx - cy :], rows[:, :cy])
    pay_b[at : at + EDGE, :] = jnp.where(even, rows[:, :cy], rows[:, cx - cy :])
    at += EDGE
    flip = ones_at(iota((cx, cx), 0) + iota((cx, cx), 1) == cx - 1)
    both = jnp.concatenate([t[cy - EDGE :], kappas[cy - EDGE :, :]], axis=0)
    turned = mat(both, flip, EXACT)
    nt = cx // cy
    for base in (0, EDGE):
        for r in range(EDGE):
            row = turned[base + EDGE - 1 - r : base + EDGE - r]
            pay_c[base + r : base + r + 1, :] = jnp.where(even, row[:, :cy], row[:, cx - cy :])
            for c in range(nt):
                to_b = at + (base // EDGE * nt + c) * EDGE + r
                pay_b[to_b : to_b + 1, :] = row[:, c * cy : (c + 1) * cy]
    pay_a[at:, :] = column
    pay_c[2 * EDGE :, :] = column
    pay_b[at + 2 * nt * EDGE :, :] = column
    top = theta[:, cy - 1, :] * mask[cy - 1 :, :]
    bottom = theta[:, 0, :] * mask[:1, :]
    for c in range(nt):
        t, b = top[:, c * cy : (c + 1) * cy], bottom[:, c * cy : (c + 1) * cy]
        row_a[c * levels : (c + 1) * levels, :] = jnp.where(even_row, t, b)
        ns_b[c * levels : (c + 1) * levels, :] = jnp.where(even_row, b, t)


def forcing_kernel(last, width, places, tt, kt, ends, got_a, got_b, tops_m, tops_a, tops_b, *rest):
    *corners, out = rest
    at_ends, at_m, at_a, at_b, at_corners = places
    cx, cy = tt.shape
    lon, lat = lax.axis_index("lon"), lax.axis_index("lat")
    even = lax.rem(lon, 2) == 0
    nt = cx // cy

    def sides(at):
        a, b = got_a[at : at + EDGE, :], got_b[at : at + EDGE, :]
        return jnp.where(even, b, a), jnp.where(even, a, b)

    def extended(own, at):
        left, right = sides(at)
        return jnp.concatenate([left, own, right], axis=0)

    t = extended(tt[...], 0)
    k = extended(kt[...], EDGE)
    lane = iota((cx + 2 * EDGE, cy), 1)
    south = jnp.where(lane == 0, 0.0, turn(t, 1, 1))
    north = jnp.where(lane == cy - 1, 0.0, turn(t, -1, 1))
    f = t + k * (turn(t, 1, 0) + turn(t, -1, 0) + south + north - 4.0 * t)

    def beyond(which):
        a = tops_a[at_a + which * EDGE : at_a + (which + 1) * EDGE, :]
        b_first = tops_b[at_b + which * nt * EDGE : at_b + (which * nt + 1) * EDGE, :]
        b_last = tops_b[at_b + (which * nt + nt - 1) * EDGE : at_b + (which * nt + nt) * EDGE, :]
        middle = [tops_m[at_m + (which * nt + c) * EDGE : at_m + (which * nt + c + 1) * EDGE, :] for c in range(nt)]
        return jnp.concatenate([jnp.where(even, b_last, a)] + middle + [jnp.where(even, a, b_first)], axis=1)

    left, right = sides(at_ends)
    row_ends = jnp.concatenate([left, ends[...], right], axis=1)
    over, over_k = beyond(0), beyond(1)
    row = iota(over.shape, 0)
    below = jnp.where(row == 0, row_ends[1:2], turn(over, 1, 0))
    over_f = over + over_k * (turn(over, 1, 1) + turn(over, -1, 1) + turn(over, -1, 0) + below - 4.0 * over)
    row_ends = jnp.where((row == 1) & (lat == last), over[:1], row_ends)
    pack = jnp.where(row < 4, row_ends, turn(over_f, 4, 0))
    low = iota((EDGE, cy), 0) < HALO
    corner = sum(ref[at : at + EDGE, :] for ref, at in zip(corners, at_corners))
    corner = jnp.where(low, turn(turn(corner, HALO, 0), 64, 1), corner)
    in_pack = iota((EDGE, cy), 1) < 64
    for d in range(cx // width):
        at = EDGE + d * width
        out[d, :width, :] = f[at : at + width, :cy]
        out[d, width : width + EDGE, :] = jnp.where(low, f[at + width : at + width + EDGE, :cy], f[at - EDGE : at, :cy])
        out[d, width + EDGE :, :] = jnp.where(in_pack, turn(pack, EDGE - cy - d * width, 1)[:, :128], corner)


def strip_order(columns, width):
    low = iota((EDGE, columns.shape[1]), 0) < HALO
    ends = jnp.where(low, columns[EDGE + width : 2 * EDGE + width], columns[:EDGE])
    return jnp.concatenate([columns[EDGE : EDGE + width], ends], axis=0)


def krylov_kernel(cell, start, table, got, diag, rows_a, rows_b, basis, gram):
    count, chunk, cy = got.shape
    width, full = diag.shape
    rows = width + EDGE
    lon, lat = lax.axis_index("lon"), lax.axis_index("lat")
    x0 = (lon * count + lat) * width
    down, across = table.shape
    nx = across * cell
    lons = nx // (count * width)

    edges = jnp.concatenate([got[s, rows:, :] for s in range(count)], axis=0)
    if edges.shape[0] < 128:
        edges = jnp.concatenate([edges, jnp.zeros((128 - edges.shape[0], cy), jnp.float32)], axis=0)
    edges = strip_order(edges.T, width)
    from_south = edges * turn(edges, 9, 1)
    from_north = edges * turn(edges, -5, 1)
    from_fold = edges * turn(edges, 2, 1)
    lane = iota((rows, cy), 1)
    parts = []
    for s in range(count):
        part = got[s, :rows, :]
        if s > 0:
            part = part + jnp.where(lane == 0, turn(from_south, -(8 * s + 2), 1), 0.0)
        above = from_north if s < count - 1 else from_fold
        part = part + jnp.where(lane == cy - 1, turn(above, cy - 1 - (8 * s + 3), 1), 0.0)
        parts.append(part)
    parts.append(jnp.where(lane < HALO, turn(edges, -(8 * (count - 1) + 4), 1), 0.0))
    f = jnp.concatenate(parts, axis=1)

    place = iota((rows, across), 0)
    x = x0 + jnp.where(place < width + HALO, place, place - rows)
    x = jnp.where(x < 0, x + nx, jnp.where(x >= nx, x - nx, x))
    cells = iota((rows, across), 1)
    here = ones_at(lax.div(x, cell) == cells)
    there = ones_at(lax.div(nx - 1 - x, cell) == cells)
    up = ones_at(lax.div(iota((down, full), 1), cell) == iota((down, full), 0))
    above = ones_at((iota((down, cy), 0) == down - 1) & (iota((down, cy), 1) < HALO))
    land = table[...].astype(jnp.float32)
    pick = lax.dot_general(jnp.concatenate([here, there], axis=0), land, (((1,), (1,)), ((), ())), preferred_element_type=jnp.float32)
    mask = jnp.concatenate([mat(pick[:rows], up), mat(pick[rows:], above)], axis=1)

    even_row = lax.rem(lat, 2) == 0
    rim = full // cy * RIM
    d_a, d_b = rows_a[start : start + rim, :], rows_b[...]
    d_east, d_west = jnp.where(even_row, d_a, d_b), jnp.where(even_row, d_b, d_a)
    unused = jnp.zeros((EDGE - 2 * RIM, cy), jnp.float32)
    d_ends = [
        jnp.concatenate([d_east[c * RIM : (c + 1) * RIM], unused, d_west[c * RIM : (c + 1) * RIM]], axis=0) for c in range(full // cy)
    ]
    d_main = jnp.concatenate([diag[...], jnp.concatenate(d_ends, axis=1)], axis=0)

    mine = lon * count + lat
    total = lons * count
    tiles = []
    for strip in (total - 1 - mine, lax.rem(2 * total - 2 - mine, total), lax.rem(total - mine, total)):
        tile = got[lax.rem(strip, count)][rows:, :]
        tile = jnp.where(iota((EDGE, 128), 1) < 64, turn(turn(tile, HALO, 0), 64, 1), tile)
        tiles.append(turn(tile, lax.rem(128 - lax.div(strip, count) * width, 128), 1))
    here = iota((128, 128), 0)
    there = iota((128, 128), 1)
    picks = [
        (here + there == width - 1) & (there < width),
        (here + there == 2 * width - 1) & (there >= width) & (there < width + HALO),
        (here + there == rows - 1) & (there >= rows - HALO) & (there < rows),
    ]
    fold = sum(mat(tile, ones_at(pick), EXACT) for tile, pick in zip(tiles, picks))
    fold = [fold[EDGE - 1 - r : EDGE - r] for r in range(HALO)] + [jnp.zeros((128 - HALO, 128), jnp.float32)]
    d_all = jnp.concatenate([d_main, jnp.concatenate(fold, axis=0).T[:rows]], axis=1)

    near = mask * (1.0 / WIDTH)
    centre = near * ((4.0 - CENTRE) + d_all)
    p = [mask * f]
    p.append(centre * p[0] - near * beside(p[0]))
    for j in range(2, ITERS + 1):
        p.append(2.0 * (centre * p[j - 1] - near * beside(p[j - 1])) - p[j - 2])
    for j in range(ITERS):
        basis[j] = p[j][:width, :full]
    sums = []
    for i in range(ITERS):
        for j in range(i, ITERS + 1):
            both = p[i][:width, :full] * p[j][:width, :full]
            both = sum(both[:, c : c + 128] for c in range(0, full, 128))
            sums.append(jnp.sum(both, axis=0, keepdims=True))
    sums = jnp.concatenate(sums + [jnp.zeros((128 - len(sums), 128), jnp.float32)], axis=0)
    gram[...] = jnp.broadcast_to(jnp.sum(sums.T, axis=0, keepdims=True), gram.shape)


def combine_kernel(gram, basis, psi):
    g = jnp.sum(gram[...], axis=0, keepdims=True)
    pairs = [(i, j) for i in range(ITERS) for j in range(i, ITERS + 1)]
    at = {}
    for n, (i, j) in enumerate(pairs):
        at[i, j] = at[j, i] = jnp.broadcast_to(g[:, n : n + 1], (8, 128))

    def applied(i, j):
        if j == 0:
            return CENTRE * at[i, 0] + WIDTH * at[i, 1]
        return CENTRE * at[i, j] + (0.5 * WIDTH) * (at[i, j + 1] + at[i, j - 1])

    a = {(i, j): applied(i, j) for i in range(ITERS) for j in range(i, ITERS)}
    b = [at[i, 0] for i in range(ITERS)]
    inverse = []
    for k in range(ITERS):
        inverse.append(1.0 / a[k, k])
        for i in range(k + 1, ITERS):
            factor = a[k, i] * inverse[k]
            for j in range(i, ITERS):
                a[i, j] = a[i, j] - factor * a[k, j]
            b[i] = b[i] - factor * b[k]
    c = [None] * ITERS
    for i in reversed(range(ITERS)):
        value = b[i]
        for j in range(i + 1, ITERS):
            value = value - a[i, j] * c[j]
        c[i] = value * inverse[i]
    total = c[0][:1, :1] * basis[0]
    for j in range(1, ITERS):
        total = total + c[j][:1, :1] * basis[j]
    psi[...] = total


def rim_kernel(rows, out):
    out[...] = rows[...]


def tracer_kernel(last, theta, ocean, coef, got_a, got_b, rows_a, rows_b, out_hbm, out, sems):
    levels, cy, cx = theta.shape
    lon, lat = lax.axis_index("lon"), lax.axis_index("lat")
    even = lax.rem(lon, 2) == 0
    a, b = got_a[2 * EDGE : 2 * EDGE + levels, :], got_b[2 * EDGE : 2 * EDGE + levels, :]
    both = jnp.concatenate([jnp.where(even, a, b), jnp.where(even, b, a), jnp.zeros((128 - 2 * levels, cy), jnp.float32)], axis=0)
    sides = both.T
    even_row = lax.rem(lat, 2) == 0

    def joined(ref):
        return jnp.concatenate([ref[c * levels : (c + 1) * levels, :] for c in range(cx // cy)], axis=1)

    a, b = joined(rows_a), joined(rows_b)
    flip = ones_at(iota((cx, cx), 0) + iota((cx, cx), 1) == cx - 1)
    north = jnp.where(lat == last, mat(b, flip, EXACT), jnp.where(even_row, a, b))
    south = jnp.where(lat == 0, 0.0, jnp.where(even_row, b, a))

    lane = iota((cy, 128), 1)
    row = iota((cy, cx), 0)
    mask, scale = ocean[...], coef[...]
    some = 2
    copies = []
    for k in range(levels):
        th = theta[k]
        m = mask * th
        east, west = turn(m, -1, 1), turn(m, 1, 1)
        east = jnp.concatenate([east[:, : cx - 128], jnp.where(lane == 127, turn(sides, 127 - k, 1), east[:, cx - 128 :])], axis=1)
        west = jnp.concatenate([jnp.where(lane == 0, turn(sides, -levels - k, 1), west[:, :128]), west[:, 128:]], axis=1)
        above = jnp.where(row == cy - 1, north[k : k + 1], turn(m, -1, 0))
        below = jnp.where(row == 0, south[k : k + 1], turn(m, 1, 0))
        out[k] = th + scale * (east + west + above + below - 4.0 * m)
        if (k + 1) % some == 0:
            n = k // some
            piece = pl.ds(n * some, some)
            copies.append(pltpu.make_async_copy(out.at[piece], out_hbm.at[piece], sems.at[n]))
            copies[-1].start()
    for copy in copies:
        copy.wait()


def per_device(theta, kappa, layer_weight, diag, land_blocks):
    lons, lats = lax.axis_size("lon"), lax.axis_size("lat")
    joint = ("lon", "lat")
    devices = lons * lats
    levels, cy, cx = theta.shape
    width, full = diag.shape
    cell = full // land_blocks.shape[0]
    last = lats - 1
    f32 = jnp.float32
    shape = lambda *dims: jax.ShapeDtypeStruct(dims, f32)

    nt = cx // cy
    head = 3 * EDGE + levels
    own = (2 * nt + 1) * EDGE
    rim = RIM * (full // cy)
    held, ocean, coef, tt, kt, ends, pay_a, pay_b, pay_c, row_a, row_b, ns_b = pl.pallas_call(
        functools.partial(sum_kernel, cell),
        in_specs=[HBM] * 5,
        out_specs=[VMEM] * 12,
        out_shape=[
            pltpu.VMEM((levels, cy, cx), f32),
            shape(cy, cx),
            shape(cy, cx),
            shape(cx, cy),
            shape(cx, cy),
            shape(EDGE, cx),
            shape(head + EDGE, cy),
            shape(head + own, cy),
            shape(3 * EDGE, cy),
            shape(nt * levels + rim, cy),
            shape(rim, cy),
            shape(nt * levels, cy),
        ],
        scratch_shapes=[
            pltpu.VMEM((cy, cx), f32),
            pltpu.VMEM((width, 128), f32),
            pltpu.VMEM((2, EDGE, full), f32),
            pltpu.VMEM(land_blocks.shape, jnp.int32),
            pltpu.SMEM((levels,), f32),
            pltpu.SemaphoreType.DMA((10,)),
        ],
        compiler_params=PARAMS,
        name="level_sum",
    )(*map(in_hbm, (layer_weight, land_blocks, theta, kappa, diag)))

    pairs_b = [(i, (i + 1) % lons if i % 2 else (i - 1) % lons) for i in range(lons)]
    mirror = [(i, lons - 1 - i) for i in range(lons)]
    got_a = lax.ppermute(pay_a, "lon", [(i, i ^ 1) for i in range(lons)])
    got_b = lax.ppermute(pay_b, "lon", pairs_b)
    if pairs_b == mirror:
        got_c = lax.ppermute(pay_c, "lon", [(i, i ^ 2) for i in range(lons)])
        folds = (got_b, got_c, pay_b)
        corners = (pay_b, got_a, got_b, got_c)
        tail = head + own - EDGE
        places = (head - EDGE, head, 0, head, (tail, head, tail, 2 * EDGE))
    else:
        got_c = lax.ppermute(pay_c, "lon", [(i, i ^ 1) for i in range(lons)])
        tops = lax.ppermute(jnp.concatenate([pay_b[head:], got_c, got_b[head:]], axis=0), "lon", mirror)
        folds = (tops, tops, tops)
        corners = (lax.psum(pay_c[2 * EDGE :], "lon"),)
        places = (head - EDGE, 0, own, own + 3 * EDGE, (0,))
    chunks = pl.pallas_call(
        functools.partial(forcing_kernel, last, width, places),
        in_specs=[VMEM] * (8 + len(corners)),
        out_specs=VMEM,
        out_shape=shape(lats, width + 2 * EDGE, cy),
        compiler_params=PARAMS,
        name="forcing",
    )(tt, kt, ends, got_a, got_b, *folds, *corners)
    chunks, row_a, ns_b = lax.optimization_barrier((chunks, row_a, ns_b))
    got = lax.all_to_all(chunks, "lat", split_axis=0, concat_axis=0, tiled=True)

    rows_b = lax.ppermute(row_b, joint, [(i, (i + 1 if i % 2 else i - 1) % devices) for i in range(devices)])
    rim_b = pl.pallas_call(
        rim_kernel,
        in_specs=[VMEM],
        out_specs=VMEM,
        out_shape=shape(rim, cy),
        compiler_params=PARAMS,
        cost_estimate=pl.CostEstimate(flops=10**11, bytes_accessed=0, transcendentals=0),
        name="rim",
    )(rows_b)
    row_a, rim_b = lax.optimization_barrier((row_a, rim_b))
    rows_a = lax.ppermute(row_a, joint, [(i, i ^ 1) for i in range(devices)])
    second = []
    for lon in range(lons):
        second += [(lon * lats + lat, (lons - 1 - lon) * lats + lat) for lat in (0, last)]
        second += [(lon * lats + lat, lon * lats + (lat + 1 if lat % 2 else lat - 1)) for lat in range(1, last)]
    beyond = lax.ppermute(ns_b, joint, second)
    new_theta = pl.pallas_call(
        functools.partial(tracer_kernel, last),
        in_specs=[VMEM] * 7,
        out_specs=HBM,
        out_shape=shape(levels, cy, cx),
        scratch_shapes=[pltpu.VMEM((levels, cy, cx), f32), pltpu.SemaphoreType.DMA((levels // 2,))],
        compiler_params=PARAMS,
        cost_estimate=pl.CostEstimate(flops=12 * levels * cy * cx, bytes_accessed=8 * levels * cy * cx, transcendentals=0),
        name="tracer",
    )(held, ocean, coef, got_a, got_b, rows_a, beyond)

    basis, gram = pl.pallas_call(
        functools.partial(krylov_kernel, cell, nt * levels),
        in_specs=[VMEM] * 5,
        out_specs=[VMEM, VMEM],
        out_shape=[shape(ITERS, width, full), shape(devices, 128)],
        compiler_params=PARAMS,
        name="krylov",
    )(land_blocks, got, diag, rows_a, rim_b)
    gram = lax.all_to_all(gram, joint, split_axis=0, concat_axis=0, tiled=True)
    psi = pl.pallas_call(
        combine_kernel,
        in_specs=[VMEM, VMEM],
        out_specs=VMEM,
        out_shape=shape(width, full),
        compiler_params=PARAMS,
        name="combine",
    )(gram, basis)
    return new_theta, psi


def solution(mesh):
    return jax.shard_map(
        per_device,
        mesh=mesh,
        in_specs=(P(None, "lat", "lon"), P("lat", "lon"), P(), P(("lon", "lat"), None), P()),
        out_specs=(P(None, "lat", "lon"), P(("lon", "lat"), None)),
        check_vma=False,
    )
```

```python
import functools

import jax
import jax.numpy as jnp
from jax import lax
from jax.experimental import pallas as pl
from jax.experimental.pallas import tpu as pltpu
from jax.sharding import PartitionSpec as P

ITERS = 4
EDGE = 8
HALO = ITERS
RIM = HALO - 1
SCALE = 4.0
STATS = 48
VMEM = pl.BlockSpec(memory_space=pltpu.VMEM)
SMEM = pl.BlockSpec(memory_space=pltpu.SMEM)
HBM = pl.BlockSpec(memory_space=pltpu.HBM)
EXACT = lax.Precision.HIGHEST
PARAMS = pltpu.CompilerParams(vmem_limit_bytes=32 * 1024 * 1024)


def in_hbm(x):
    return pltpu.with_memory_space_constraint(x, pltpu.HBM)


def iota(shape, dim):
    return lax.broadcasted_iota(jnp.int32, shape, dim)


def ones_at(hit):
    return jnp.where(hit, 1.0, 0.0).astype(jnp.float32)


def mat(a, b, precision=None):
    return jnp.dot(a, b, precision=precision, preferred_element_type=jnp.float32)


def turn(x, shift, dim):
    return pltpu.roll(x, shift % x.shape[dim] if isinstance(shift, int) else shift, dim)


def beside(v):
    return turn(v, 1, 0) + turn(v, -1, 0) + turn(v, 1, 1) + turn(v, -1, 1)


def total_of(v):
    return jnp.sum(jnp.sum(v, axis=0, keepdims=True), axis=1, keepdims=True)


def block_mask(table, row0, rows, col0, cols, cell):
    down, across = table.shape
    pick_rows = ones_at(lax.div(row0 + iota((rows, down), 0), cell) == iota((rows, down), 1))
    pick_cols = ones_at(lax.div(col0 + iota((across, cols), 1), cell) == iota((across, cols), 0))
    return mat(mat(pick_rows, table), pick_cols)


def sum_kernel(cell, weight_hbm, table_hbm, theta_hbm, kappa_hbm, diag_hbm, theta, ocean, coef, tt, kt, ends, pay_a, pay_b, pay_c, row_a, row_b, ns_b, kappa, strip, table, weight, sems):
    levels, cy, cx = theta.shape
    width, full = diag_hbm.shape
    copies = [
        pltpu.make_async_copy(table_hbm, table, sems.at[0]),
        pltpu.make_async_copy(weight_hbm, weight, sems.at[1]),
        pltpu.make_async_copy(kappa_hbm, kappa, sems.at[2]),
        pltpu.make_async_copy(diag_hbm, strip, sems.at[3]),
    ]
    pieces = 4
    some = levels // pieces
    for n in range(pieces):
        copies.append(pltpu.make_async_copy(theta_hbm.at[pl.ds(n * some, some)], theta.at[pl.ds(n * some, some)], sems.at[4 + n]))
    for copy in copies:
        copy.start()
    lon, lat = lax.axis_index("lon"), lax.axis_index("lat")
    even = lax.rem(lon, 2) == 0
    even_row = lax.rem(lat, 2) == 0
    copies[0].wait()
    mask = block_mask(table[...].astype(jnp.float32), lat * cy, cy, lon * cx, cx, cell)
    copies[3].wait()
    column = jnp.concatenate([strip[:, full - 128 :], jnp.zeros((128 - width, 128), jnp.float32)], axis=0).T
    column = turn(column[128 - EDGE :], lon * width, 1)
    down, across = table.shape
    x0 = (lon * (cx // width) + lat) * width
    land = table[...].astype(jnp.float32)
    pick = ones_at(lax.div(x0 + iota((width, across), 0), cell) == iota((width, across), 1))
    pick = lax.dot_general(pick, land, (((1,), (1,)), ((), ())), preferred_element_type=jnp.float32)
    wet = mat(pick, ones_at(lax.div(iota((down, full), 1), cell) == iota((down, full), 0)))
    at = cx // cy * levels
    for c in range(full // cy):
        w = strip[:RIM, c * cy : (c + 1) * cy]
        e = strip[width - RIM :, c * cy : (c + 1) * cy]
        row_a[at : at + RIM, :] = jnp.where(even_row, e, w)
        row_b[c * RIM : (c + 1) * RIM, :] = jnp.where(even_row, w, e)
        at += RIM
    copies[2].wait()
    kappas = kappa[...]
    ocean[...] = mask
    coef[...] = mask * kappas
    ktv = kappas.T
    kt[...] = ktv

    lane = iota((cy, 128), 1)
    total = jnp.zeros((cy, cx), jnp.float32)
    sides = jnp.zeros((cy, 128), jnp.float32)
    copies[1].wait()
    for n in range(pieces):
        copies[4 + n].wait()
        for k in range(n * some, n * some + some):
            th = theta[k]
            total = total + weight[k] * th
            sides = jnp.where(lane == k, turn(th[:, :128], k, 1), sides)
            sides = jnp.where(lane == levels + k, turn(th[:, cx - 128 :], levels + k + 1, 1), sides)
    t = mask * total
    inner = (iota((cy, cx), 0) > 0) & (iota((cy, cx), 0) < cy - 1) & (iota((cy, cx), 1) > 0) & (iota((cy, cx), 1) < cx - 1)
    kept = jnp.where(inner, t, 0.0)
    stats = [total_of(v) for v in (kept * t, kept * (4.0 * t - beside(t)), wet, wet * strip[...])]
    spot = iota((EDGE, 128), 1)
    mine = (spot >= lon * width) & (spot < (lon + 1) * width)
    for n, value in enumerate(stats):
        column = jnp.where(iota((EDGE, 128), 0) == n, jnp.where(mine, value, 0.0), column)
    ttv = t.T
    tt[...] = ttv
    sidest = (sides * jnp.where(lane < levels, mask[:, :1], mask[:, cx - 1 :])).T
    west, east = sidest[:levels], sidest[levels : 2 * levels]
    pay_a[2 * EDGE : 2 * EDGE + levels, :] = jnp.where(even, east, west)
    pay_b[2 * EDGE : 2 * EDGE + levels, :] = jnp.where(even, west, east)
    for at, turned in ((0, ttv), (EDGE, ktv)):
        w, e = turned[:EDGE], turned[cx - EDGE :]
        pay_a[at : at + EDGE, :] = jnp.where(even, e, w)
        pay_b[at : at + EDGE, :] = jnp.where(even, w, e)
    at = 2 * EDGE + levels
    rows = jnp.concatenate([t[:1], t[cy - 1 :], kappas[:1], kappas[cy - 1 :], jnp.zeros((EDGE - 4, cx), jnp.float32)], axis=0)
    ends[...] = rows
    pay_a[at : at + EDGE, :] = jnp.where(even, rows[:, cx - cy :], rows[:, :cy])
    pay_b[at : at + EDGE, :] = jnp.where(even, rows[:, :cy], rows[:, cx - cy :])
    at += EDGE
    flip = ones_at(iota((cx, cx), 0) + iota((cx, cx), 1) == cx - 1)
    both = jnp.concatenate([t[cy - EDGE :], kappas[cy - EDGE :, :]], axis=0)
    turned = mat(both, flip, EXACT)
    nt = cx // cy
    for base in (0, EDGE):
        for r in range(EDGE):
            row = turned[base + EDGE - 1 - r : base + EDGE - r]
            pay_c[base + r : base + r + 1, :] = jnp.where(even, row[:, :cy], row[:, cx - cy :])
            for c in range(nt):
                to_b = at + (base // EDGE * nt + c) * EDGE + r
                pay_b[to_b : to_b + 1, :] = row[:, c * cy : (c + 1) * cy]
    pay_a[at:, :] = column
    pay_c[2 * EDGE :, :] = column
    pay_b[at + 2 * nt * EDGE :, :] = column
    top = theta[:, cy - 1, :] * mask[cy - 1 :, :]
    bottom = theta[:, 0, :] * mask[:1, :]
    for c in range(nt):
        t, b = top[:, c * cy : (c + 1) * cy], bottom[:, c * cy : (c + 1) * cy]
        row_a[c * levels : (c + 1) * levels, :] = jnp.where(even_row, t, b)
        ns_b[c * levels : (c + 1) * levels, :] = jnp.where(even_row, b, t)


def forcing_kernel(last, width, places, tt, kt, ends, got_a, got_b, tops_m, tops_a, tops_b, *rest):
    *corners, out = rest
    at_ends, at_m, at_a, at_b, at_corners = places
    cx, cy = tt.shape
    lon, lat = lax.axis_index("lon"), lax.axis_index("lat")
    even = lax.rem(lon, 2) == 0
    nt = cx // cy

    def sides(at):
        a, b = got_a[at : at + EDGE, :], got_b[at : at + EDGE, :]
        return jnp.where(even, b, a), jnp.where(even, a, b)

    def extended(own, at):
        left, right = sides(at)
        return jnp.concatenate([left, own, right], axis=0)

    t = extended(tt[...], 0)
    k = extended(kt[...], EDGE)
    lane = iota((cx + 2 * EDGE, cy), 1)
    south = jnp.where(lane == 0, 0.0, turn(t, 1, 1))
    north = jnp.where(lane == cy - 1, 0.0, turn(t, -1, 1))
    f = t + k * (turn(t, 1, 0) + turn(t, -1, 0) + south + north - 4.0 * t)

    def beyond(which):
        a = tops_a[at_a + which * EDGE : at_a + (which + 1) * EDGE, :]
        b_first = tops_b[at_b + which * nt * EDGE : at_b + (which * nt + 1) * EDGE, :]
        b_last = tops_b[at_b + (which * nt + nt - 1) * EDGE : at_b + (which * nt + nt) * EDGE, :]
        middle = [tops_m[at_m + (which * nt + c) * EDGE : at_m + (which * nt + c + 1) * EDGE, :] for c in range(nt)]
        return jnp.concatenate([jnp.where(even, b_last, a)] + middle + [jnp.where(even, a, b_first)], axis=1)

    left, right = sides(at_ends)
    row_ends = jnp.concatenate([left, ends[...], right], axis=1)
    over, over_k = beyond(0), beyond(1)
    row = iota(over.shape, 0)
    below = jnp.where(row == 0, row_ends[1:2], turn(over, 1, 0))
    over_f = over + over_k * (turn(over, 1, 1) + turn(over, -1, 1) + turn(over, -1, 0) + below - 4.0 * over)
    row_ends = jnp.where((row == 1) & (lat == last), over[:1], row_ends)
    pack = jnp.where(row < 4, row_ends, turn(over_f, 4, 0))
    low = iota((EDGE, cy), 0) < HALO
    corner = sum(ref[at : at + EDGE, :] for ref, at in zip(corners, at_corners))
    stats = jnp.sum(corner, axis=1, keepdims=True)
    corner = jnp.where(low, turn(turn(corner, HALO, 0), 64, 1), corner)
    spot = iota((EDGE, cy), 1)
    corner = jnp.where(spot < 64, stats, corner)
    in_pack = spot < STATS
    for d in range(cx // width):
        at = EDGE + d * width
        out[d, :width, :] = f[at : at + width, :cy]
        out[d, width : width + EDGE, :] = jnp.where(low, f[at + width : at + width + EDGE, :cy], f[at - EDGE : at, :cy])
        out[d, width + EDGE :, :] = jnp.where(in_pack, turn(pack, EDGE - cy - d * width, 1)[:, :128], corner)


def strip_order(columns, width):
    low = iota((EDGE, columns.shape[1]), 0) < HALO
    ends = jnp.where(low, columns[EDGE + width : 2 * EDGE + width], columns[:EDGE])
    return jnp.concatenate([columns[EDGE : EDGE + width], ends], axis=0)


def krylov_kernel(cell, start, table, got, diag, rows_a, rows_b, basis, gram):
    count, chunk, cy = got.shape
    width, full = diag.shape
    rows = width + EDGE
    lon, lat = lax.axis_index("lon"), lax.axis_index("lat")
    x0 = (lon * count + lat) * width
    down, across = table.shape
    nx = across * cell
    lons = nx // (count * width)

    edges = jnp.concatenate([got[s, rows:, :] for s in range(count)], axis=0)
    if edges.shape[0] < 128:
        edges = jnp.concatenate([edges, jnp.zeros((128 - edges.shape[0], cy), jnp.float32)], axis=0)
    edges = strip_order(edges.T, width)
    from_south = edges * turn(edges, 9, 1)
    from_north = edges * turn(edges, -5, 1)
    from_fold = edges * turn(edges, 2, 1)
    lane = iota((rows, cy), 1)
    parts = []
    for s in range(count):
        part = got[s, :rows, :]
        if s > 0:
            part = part + jnp.where(lane == 0, turn(from_south, -(8 * s + 2), 1), 0.0)
        above = from_north if s < count - 1 else from_fold
        part = part + jnp.where(lane == cy - 1, turn(above, cy - 1 - (8 * s + 3), 1), 0.0)
        parts.append(part)
    parts.append(jnp.where(lane < HALO, turn(edges, -(8 * (count - 1) + 4), 1), 0.0))
    f = jnp.concatenate(parts, axis=1)

    place = iota((rows, across), 0)
    x = x0 + jnp.where(place < width + HALO, place, place - rows)
    x = jnp.where(x < 0, x + nx, jnp.where(x >= nx, x - nx, x))
    cells = iota((rows, across), 1)
    here = ones_at(lax.div(x, cell) == cells)
    there = ones_at(lax.div(nx - 1 - x, cell) == cells)
    up = ones_at(lax.div(iota((down, full), 1), cell) == iota((down, full), 0))
    above = ones_at((iota((down, cy), 0) == down - 1) & (iota((down, cy), 1) < HALO))
    land = table[...].astype(jnp.float32)
    pick = lax.dot_general(jnp.concatenate([here, there], axis=0), land, (((1,), (1,)), ((), ())), preferred_element_type=jnp.float32)
    mask = jnp.concatenate([mat(pick[:rows], up), mat(pick[rows:], above)], axis=1)

    even_row = lax.rem(lat, 2) == 0
    rim = full // cy * RIM
    d_a, d_b = rows_a[start : start + rim, :], rows_b[...]
    d_east, d_west = jnp.where(even_row, d_a, d_b), jnp.where(even_row, d_b, d_a)
    unused = jnp.zeros((EDGE - 2 * RIM, cy), jnp.float32)
    d_ends = [
        jnp.concatenate([d_east[c * RIM : (c + 1) * RIM], unused, d_west[c * RIM : (c + 1) * RIM]], axis=0) for c in range(full // cy)
    ]
    d_main = jnp.concatenate([diag[...], jnp.concatenate(d_ends, axis=1)], axis=0)

    mine = lon * count + lat
    total = lons * count
    tiles = []
    for strip in (total - 1 - mine, lax.rem(2 * total - 2 - mine, total), lax.rem(total - mine, total)):
        tile = got[lax.rem(strip, count)][rows:, :]
        tile = jnp.where(iota((EDGE, 128), 1) < 64, turn(turn(tile, HALO, 0), 64, 1), tile)
        tiles.append(turn(tile, lax.rem(128 - lax.div(strip, count) * width, 128), 1))
    here = iota((128, 128), 0)
    there = iota((128, 128), 1)
    picks = [
        (here + there == width - 1) & (there < width),
        (here + there == 2 * width - 1) & (there >= width) & (there < width + HALO),
        (here + there == rows - 1) & (there >= rows - HALO) & (there < rows),
    ]
    fold = sum(mat(tile, ones_at(pick), EXACT) for tile, pick in zip(tiles, picks))
    fold = [fold[EDGE - 1 - r : EDGE - r] for r in range(HALO)] + [jnp.zeros((128 - HALO, 128), jnp.float32)]
    d_all = jnp.concatenate([d_main, jnp.concatenate(fold, axis=0).T[:rows]], axis=1)

    stats = sum(got[s, rows : rows + EDGE, :] for s in range(count))[:, STATS : STATS + 1]
    share = stats[1:2] / stats[0:1]
    shift = jnp.where(stats[0:1] > 0.0, share, 0.0) + jnp.where(stats[2:3] > 0.0, stats[3:4] / stats[2:3], 0.0)
    near = mask * (1.0 / SCALE)
    centre = near * (4.0 + d_all - shift)
    p = [mask * f]
    for j in range(ITERS):
        p.append(centre * p[j] - near * beside(p[j]))
    for j in range(ITERS):
        basis[j] = p[j][:width, :full]
    sums = []
    for i in range(ITERS):
        for j in range(i, ITERS + 1):
            both = p[i][:width, :full] * p[j][:width, :full]
            both = sum(both[:, c : c + 128] for c in range(0, full, 128))
            sums.append(jnp.sum(both, axis=0, keepdims=True))
    pairs = len(sums)
    sums = jnp.concatenate(sums + [jnp.zeros((16 - pairs, 128), jnp.float32)], axis=0)
    sums = jnp.where(iota((16, 128), 0) == iota((16, 128), 1), jnp.sum(sums, axis=1, keepdims=True), 0.0)
    sums = jnp.sum(sums, axis=0, keepdims=True)
    sums = jnp.where(iota((1, 128), 1) == pairs, shift, sums)
    gram[...] = jnp.broadcast_to(sums, gram.shape)


def combine_kernel(gram, basis, psi):
    g = jnp.sum(gram[...], axis=0, keepdims=True)
    pairs = [(i, j) for i in range(ITERS) for j in range(i, ITERS + 1)]
    at = {}
    for n, (i, j) in enumerate(pairs):
        at[i, j] = at[j, i] = jnp.broadcast_to(g[:, n : n + 1], (8, 128))

    shift = jnp.broadcast_to(gram[:1, len(pairs) : len(pairs) + 1], (8, 128))

    def applied(i, j):
        return shift * at[i, j] + SCALE * at[i, j + 1]

    a = {(i, j): applied(i, j) for i in range(ITERS) for j in range(i, ITERS)}
    b = [at[i, 0] for i in range(ITERS)]
    inverse = []
    for k in range(ITERS):
        inverse.append(1.0 / a[k, k])
        for i in range(k + 1, ITERS):
            factor = a[k, i] * inverse[k]
            for j in range(i, ITERS):
                a[i, j] = a[i, j] - factor * a[k, j]
            b[i] = b[i] - factor * b[k]
    c = [None] * ITERS
    for i in reversed(range(ITERS)):
        value = b[i]
        for j in range(i + 1, ITERS):
            value = value - a[i, j] * c[j]
        c[i] = value * inverse[i]
    total = c[0][:1, :1] * basis[0]
    for j in range(1, ITERS):
        total = total + c[j][:1, :1] * basis[j]
    psi[...] = total


def rim_kernel(rows, out):
    out[...] = rows[...]


def tracer_kernel(last, theta, ocean, coef, got_a, got_b, rows_a, rows_b, out_hbm, out, sems):
    levels, cy, cx = theta.shape
    lon, lat = lax.axis_index("lon"), lax.axis_index("lat")
    even = lax.rem(lon, 2) == 0
    a, b = got_a[2 * EDGE : 2 * EDGE + levels, :], got_b[2 * EDGE : 2 * EDGE + levels, :]
    both = jnp.concatenate([jnp.where(even, a, b), jnp.where(even, b, a), jnp.zeros((128 - 2 * levels, cy), jnp.float32)], axis=0)
    sides = both.T
    even_row = lax.rem(lat, 2) == 0

    def joined(ref):
        return jnp.concatenate([ref[c * levels : (c + 1) * levels, :] for c in range(cx // cy)], axis=1)

    a, b = joined(rows_a), joined(rows_b)
    flip = ones_at(iota((cx, cx), 0) + iota((cx, cx), 1) == cx - 1)
    north = jnp.where(lat == last, mat(b, flip, EXACT), jnp.where(even_row, a, b))
    south = jnp.where(lat == 0, 0.0, jnp.where(even_row, b, a))

    lane = iota((cy, 128), 1)
    row = iota((cy, cx), 0)
    mask, scale = ocean[...], coef[...]
    some = 2
    copies = []
    for k in range(levels):
        th = theta[k]
        m = mask * th
        east, west = turn(m, -1, 1), turn(m, 1, 1)
        east = jnp.concatenate([east[:, : cx - 128], jnp.where(lane == 127, turn(sides, 127 - k, 1), east[:, cx - 128 :])], axis=1)
        west = jnp.concatenate([jnp.where(lane == 0, turn(sides, -levels - k, 1), west[:, :128]), west[:, 128:]], axis=1)
        above = jnp.where(row == cy - 1, north[k : k + 1], turn(m, -1, 0))
        below = jnp.where(row == 0, south[k : k + 1], turn(m, 1, 0))
        out[k] = th + scale * (east + west + above + below - 4.0 * m)
        if (k + 1) % some == 0:
            n = k // some
            piece = pl.ds(n * some, some)
            copies.append(pltpu.make_async_copy(out.at[piece], out_hbm.at[piece], sems.at[n]))
            copies[-1].start()
    for copy in copies:
        copy.wait()


def per_device(theta, kappa, layer_weight, diag, land_blocks):
    lons, lats = lax.axis_size("lon"), lax.axis_size("lat")
    joint = ("lon", "lat")
    devices = lons * lats
    levels, cy, cx = theta.shape
    width, full = diag.shape
    cell = full // land_blocks.shape[0]
    last = lats - 1
    f32 = jnp.float32
    shape = lambda *dims: jax.ShapeDtypeStruct(dims, f32)

    nt = cx // cy
    head = 3 * EDGE + levels
    own = (2 * nt + 1) * EDGE
    rim = RIM * (full // cy)
    held, ocean, coef, tt, kt, ends, pay_a, pay_b, pay_c, row_a, row_b, ns_b = pl.pallas_call(
        functools.partial(sum_kernel, cell),
        in_specs=[HBM] * 5,
        out_specs=[VMEM] * 12,
        out_shape=[
            pltpu.VMEM((levels, cy, cx), f32),
            shape(cy, cx),
            shape(cy, cx),
            shape(cx, cy),
            shape(cx, cy),
            shape(EDGE, cx),
            shape(head + EDGE, cy),
            shape(head + own, cy),
            shape(3 * EDGE, cy),
            shape(nt * levels + rim, cy),
            shape(rim, cy),
            shape(nt * levels, cy),
        ],
        scratch_shapes=[
            pltpu.VMEM((cy, cx), f32),
            pltpu.VMEM((width, full), f32),
            pltpu.VMEM(land_blocks.shape, jnp.int32),
            pltpu.SMEM((levels,), f32),
            pltpu.SemaphoreType.DMA((8,)),
        ],
        compiler_params=PARAMS,
        name="level_sum",
    )(*map(in_hbm, (layer_weight, land_blocks, theta, kappa, diag)))

    pairs_b = [(i, (i + 1) % lons if i % 2 else (i - 1) % lons) for i in range(lons)]
    mirror = [(i, lons - 1 - i) for i in range(lons)]
    got_a = lax.ppermute(pay_a, "lon", [(i, i ^ 1) for i in range(lons)])
    got_b = lax.ppermute(pay_b, "lon", pairs_b)
    if pairs_b == mirror:
        got_c = lax.ppermute(pay_c, "lon", [(i, i ^ 2) for i in range(lons)])
        folds = (got_b, got_c, pay_b)
        corners = (pay_b, got_a, got_b, got_c)
        tail = head + own - EDGE
        places = (head - EDGE, head, 0, head, (tail, head, tail, 2 * EDGE))
    else:
        got_c = lax.ppermute(pay_c, "lon", [(i, i ^ 1) for i in range(lons)])
        tops = lax.ppermute(jnp.concatenate([pay_b[head:], got_c, got_b[head:]], axis=0), "lon", mirror)
        folds = (tops, tops, tops)
        corners = (lax.psum(pay_c[2 * EDGE :], "lon"),)
        places = (head - EDGE, 0, own, own + 3 * EDGE, (0,))
    chunks = pl.pallas_call(
        functools.partial(forcing_kernel, last, width, places),
        in_specs=[VMEM] * (8 + len(corners)),
        out_specs=VMEM,
        out_shape=shape(lats, width + 2 * EDGE, cy),
        compiler_params=PARAMS,
        name="forcing",
    )(tt, kt, ends, got_a, got_b, *folds, *corners)
    chunks, row_a, ns_b = lax.optimization_barrier((chunks, row_a, ns_b))
    got = lax.all_to_all(chunks, "lat", split_axis=0, concat_axis=0, tiled=True)

    rows_b = lax.ppermute(row_b, joint, [(i, (i + 1 if i % 2 else i - 1) % devices) for i in range(devices)])
    rim_b = pl.pallas_call(
        rim_kernel,
        in_specs=[VMEM],
        out_specs=VMEM,
        out_shape=shape(rim, cy),
        compiler_params=PARAMS,
        cost_estimate=pl.CostEstimate(flops=10**11, bytes_accessed=0, transcendentals=0),
        name="rim",
    )(rows_b)
    row_a, rim_b = lax.optimization_barrier((row_a, rim_b))
    rows_a = lax.ppermute(row_a, joint, [(i, i ^ 1) for i in range(devices)])
    second = []
    for lon in range(lons):
        second += [(lon * lats + lat, (lons - 1 - lon) * lats + lat) for lat in (0, last)]
        second += [(lon * lats + lat, lon * lats + (lat + 1 if lat % 2 else lat - 1)) for lat in range(1, last)]
    beyond = lax.ppermute(ns_b, joint, second)
    new_theta = pl.pallas_call(
        functools.partial(tracer_kernel, last),
        in_specs=[VMEM] * 7,
        out_specs=HBM,
        out_shape=shape(levels, cy, cx),
        scratch_shapes=[pltpu.VMEM((levels, cy, cx), f32), pltpu.SemaphoreType.DMA((levels // 2,))],
        compiler_params=PARAMS,
        cost_estimate=pl.CostEstimate(flops=12 * levels * cy * cx, bytes_accessed=8 * levels * cy * cx, transcendentals=0),
        name="tracer",
    )(held, ocean, coef, got_a, got_b, rows_a, beyond)

    basis, gram = pl.pallas_call(
        functools.partial(krylov_kernel, cell, nt * levels),
        in_specs=[VMEM] * 5,
        out_specs=[VMEM, VMEM],
        out_shape=[shape(ITERS, width, full), shape(devices, 128)],
        compiler_params=PARAMS,
        name="krylov",
    )(land_blocks, got, diag, rows_a, rim_b)
    gram = lax.all_to_all(gram, joint, split_axis=0, concat_axis=0, tiled=True)
    psi = pl.pallas_call(
        combine_kernel,
        in_specs=[VMEM, VMEM],
        out_specs=VMEM,
        out_shape=shape(width, full),
        compiler_params=PARAMS,
        name="combine",
    )(gram, basis)
    return new_theta, psi


def solution(mesh):
    return jax.shard_map(
        per_device,
        mesh=mesh,
        in_specs=(P(None, "lat", "lon"), P("lat", "lon"), P(), P(("lon", "lat"), None), P()),
        out_specs=(P(None, "lat", "lon"), P(("lon", "lat"), None)),
        check_vma=False,
    )
```

```python
import functools

import jax
import jax.numpy as jnp
from jax import lax
from jax.experimental import pallas as pl
from jax.experimental.pallas import tpu as pltpu
from jax.sharding import PartitionSpec as P

ITERS = 4
EDGE = 8
HALO = ITERS
RIM = HALO - 1
SCALE = 4.0
STATS = 48
VMEM = pl.BlockSpec(memory_space=pltpu.VMEM)
SMEM = pl.BlockSpec(memory_space=pltpu.SMEM)
HBM = pl.BlockSpec(memory_space=pltpu.HBM)
EXACT = lax.Precision.HIGHEST
PARAMS = pltpu.CompilerParams(vmem_limit_bytes=32 * 1024 * 1024)


def in_hbm(x):
    return pltpu.with_memory_space_constraint(x, pltpu.HBM)


def iota(shape, dim):
    return lax.broadcasted_iota(jnp.int32, shape, dim)


def ones_at(hit):
    return jnp.where(hit, 1.0, 0.0).astype(jnp.float32)


def mat(a, b, precision=None):
    return jnp.dot(a, b, precision=precision, preferred_element_type=jnp.float32)


def turn(x, shift, dim):
    return pltpu.roll(x, shift % x.shape[dim] if isinstance(shift, int) else shift, dim)


def beside(v):
    return turn(v, 1, 0) + turn(v, -1, 0) + turn(v, 1, 1) + turn(v, -1, 1)


def total_of(v):
    return jnp.sum(jnp.sum(v, axis=0, keepdims=True), axis=1, keepdims=True)


def block_mask(table, row0, rows, col0, cols, cell):
    down, across = table.shape
    pick_rows = ones_at(lax.div(row0 + iota((rows, down), 0), cell) == iota((rows, down), 1))
    pick_cols = ones_at(lax.div(col0 + iota((across, cols), 1), cell) == iota((across, cols), 0))
    return mat(mat(pick_rows, table), pick_cols)


def sum_kernel(cell, weight_hbm, table_hbm, theta_hbm, kappa_hbm, diag_hbm, theta, ocean, coef, tt, kt, ends, pay_a, pay_b, pay_c, row_a, row_b, ns_b, kappa, strip, table, weight, sems):
    levels, cy, cx = theta.shape
    width, full = diag_hbm.shape
    copies = [
        pltpu.make_async_copy(table_hbm, table, sems.at[0]),
        pltpu.make_async_copy(weight_hbm, weight, sems.at[1]),
        pltpu.make_async_copy(kappa_hbm, kappa, sems.at[2]),
        pltpu.make_async_copy(diag_hbm, strip, sems.at[3]),
    ]
    pieces = 4
    some = levels // pieces
    for n in range(pieces):
        copies.append(pltpu.make_async_copy(theta_hbm.at[pl.ds(n * some, some)], theta.at[pl.ds(n * some, some)], sems.at[4 + n]))
    for copy in copies:
        copy.start()
    lon, lat = lax.axis_index("lon"), lax.axis_index("lat")
    even = lax.rem(lon, 2) == 0
    even_row = lax.rem(lat, 2) == 0
    copies[0].wait()
    mask = block_mask(table[...].astype(jnp.float32), lat * cy, cy, lon * cx, cx, cell)
    copies[3].wait()
    column = jnp.concatenate([strip[:, full - 128 :], jnp.zeros((128 - width, 128), jnp.float32)], axis=0).T
    column = turn(column[128 - EDGE :], lon * width, 1)
    down, across = table.shape
    x0 = (lon * (cx // width) + lat) * width
    land = table[...].astype(jnp.float32)
    pick = ones_at(lax.div(x0 + iota((width, across), 0), cell) == iota((width, across), 1))
    pick = lax.dot_general(pick, land, (((1,), (1,)), ((), ())), preferred_element_type=jnp.float32)
    wet = mat(pick, ones_at(lax.div(iota((down, full), 1), cell) == iota((down, full), 0)))
    at = cx // cy * levels
    for c in range(full // cy):
        w = strip[:RIM, c * cy : (c + 1) * cy]
        e = strip[width - RIM :, c * cy : (c + 1) * cy]
        row_a[at : at + RIM, :] = jnp.where(even_row, e, w)
        row_b[c * RIM : (c + 1) * RIM, :] = jnp.where(even_row, w, e)
        at += RIM
    copies[2].wait()
    kappas = kappa[...]
    ocean[...] = mask
    coef[...] = mask * kappas
    ktv = kappas.T
    kt[...] = ktv

    lane = iota((cy, 128), 1)
    total = jnp.zeros((cy, cx), jnp.float32)
    sides = jnp.zeros((cy, 128), jnp.float32)
    copies[1].wait()
    for n in range(pieces):
        copies[4 + n].wait()
        for k in range(n * some, n * some + some):
            th = theta[k]
            total = total + weight[k] * th
            sides = jnp.where(lane == k, turn(th[:, :128], k, 1), sides)
            sides = jnp.where(lane == levels + k, turn(th[:, cx - 128 :], levels + k + 1, 1), sides)
    t = mask * total
    inner = (iota((cy, cx), 0) > 0) & (iota((cy, cx), 0) < cy - 1) & (iota((cy, cx), 1) > 0) & (iota((cy, cx), 1) < cx - 1)
    kept = jnp.where(inner, t, 0.0)
    stats = [total_of(v) for v in (kept * t, kept * (4.0 * t - beside(t)), wet, wet * strip[...])]
    spot = iota((EDGE, 128), 1)
    mine = (spot >= lon * width) & (spot < (lon + 1) * width)
    for n, value in enumerate(stats):
        column = jnp.where(iota((EDGE, 128), 0) == n, jnp.where(mine, value, 0.0), column)
    ttv = t.T
    tt[...] = ttv
    sidest = (sides * jnp.where(lane < levels, mask[:, :1], mask[:, cx - 1 :])).T
    west, east = sidest[:levels], sidest[levels : 2 * levels]
    pay_a[2 * EDGE : 2 * EDGE + levels, :] = jnp.where(even, east, west)
    pay_b[2 * EDGE : 2 * EDGE + levels, :] = jnp.where(even, west, east)
    for at, turned in ((0, ttv), (EDGE, ktv)):
        w, e = turned[:EDGE], turned[cx - EDGE :]
        pay_a[at : at + EDGE, :] = jnp.where(even, e, w)
        pay_b[at : at + EDGE, :] = jnp.where(even, w, e)
    at = 2 * EDGE + levels
    rows = jnp.concatenate([t[:1], t[cy - 1 :], kappas[:1], kappas[cy - 1 :], jnp.zeros((EDGE - 4, cx), jnp.float32)], axis=0)
    ends[...] = rows
    pay_a[at : at + EDGE, :] = jnp.where(even, rows[:, cx - cy :], rows[:, :cy])
    pay_b[at : at + EDGE, :] = jnp.where(even, rows[:, :cy], rows[:, cx - cy :])
    at += EDGE
    flip = ones_at(iota((cx, cx), 0) + iota((cx, cx), 1) == cx - 1)
    both = jnp.concatenate([t[cy - EDGE :], kappas[cy - EDGE :, :]], axis=0)
    turned = mat(both, flip, EXACT)
    nt = cx // cy
    for base in (0, EDGE):
        for r in range(EDGE):
            row = turned[base + EDGE - 1 - r : base + EDGE - r]
            pay_c[base + r : base + r + 1, :] = jnp.where(even, row[:, :cy], row[:, cx - cy :])
            for c in range(nt):
                to_b = at + (base // EDGE * nt + c) * EDGE + r
                pay_b[to_b : to_b + 1, :] = row[:, c * cy : (c + 1) * cy]
    pay_a[at:, :] = column
    pay_c[2 * EDGE :, :] = column
    pay_b[at + 2 * nt * EDGE :, :] = column
    top = theta[:, cy - 1, :] * mask[cy - 1 :, :]
    bottom = theta[:, 0, :] * mask[:1, :]
    for c in range(nt):
        t, b = top[:, c * cy : (c + 1) * cy], bottom[:, c * cy : (c + 1) * cy]
        row_a[c * levels : (c + 1) * levels, :] = jnp.where(even_row, t, b)
        ns_b[c * levels : (c + 1) * levels, :] = jnp.where(even_row, b, t)


def forcing_kernel(last, lons, width, places, tt, kt, ends, got_a, got_b, tops_m, tops_a, tops_b, *rest):
    *corners, out = rest
    at_ends, at_m, at_a, at_b, at_corners = places
    cx, cy = tt.shape
    lon, lat = lax.axis_index("lon"), lax.axis_index("lat")
    even = lax.rem(lon, 2) == 0
    nt = cx // cy

    def sides(at):
        a, b = got_a[at : at + EDGE, :], got_b[at : at + EDGE, :]
        return jnp.where(even, b, a), jnp.where(even, a, b)

    def extended(own, at):
        left, right = sides(at)
        return jnp.concatenate([left, own, right], axis=0)

    t = extended(tt[...], 0)
    k = extended(kt[...], EDGE)
    lane = iota((cx + 2 * EDGE, cy), 1)
    south = jnp.where(lane == 0, 0.0, turn(t, 1, 1))
    north = jnp.where(lane == cy - 1, 0.0, turn(t, -1, 1))
    f = t + k * (turn(t, 1, 0) + turn(t, -1, 0) + south + north - 4.0 * t)

    def beyond(which):
        a = tops_a[at_a + which * EDGE : at_a + (which + 1) * EDGE, :]
        b_first = tops_b[at_b + which * nt * EDGE : at_b + (which * nt + 1) * EDGE, :]
        b_last = tops_b[at_b + (which * nt + nt - 1) * EDGE : at_b + (which * nt + nt) * EDGE, :]
        middle = [tops_m[at_m + (which * nt + c) * EDGE : at_m + (which * nt + c + 1) * EDGE, :] for c in range(nt)]
        return jnp.concatenate([jnp.where(even, b_last, a)] + middle + [jnp.where(even, a, b_first)], axis=1)

    left, right = sides(at_ends)
    row_ends = jnp.concatenate([left, ends[...], right], axis=1)
    over, over_k = beyond(0), beyond(1)
    row = iota(over.shape, 0)
    below = jnp.where(row == 0, row_ends[1:2], turn(over, 1, 0))
    over_f = over + over_k * (turn(over, 1, 1) + turn(over, -1, 1) + turn(over, -1, 0) + below - 4.0 * over)
    row_ends = jnp.where((row == 1) & (lat == last), over[:1], row_ends)
    pack = jnp.where(row < 4, row_ends, turn(over_f, 4, 0))
    low = iota((EDGE, cy), 0) < HALO
    corner = sum(ref[at : at + EDGE, :] for ref, at in zip(corners, at_corners))
    spread = corner
    corner = jnp.where(low, turn(turn(corner, HALO, 0), 64, 1), corner)
    spot = iota((EDGE, cy), 1)
    for n in range(lons):
        first = STATS + n * ((64 - STATS) // lons)
        corner = jnp.where((spot >= first) & (spot < 64), turn(spread, first - n * width, 1), corner)
    in_pack = spot < STATS
    for d in range(cx // width):
        at = EDGE + d * width
        out[d, :width, :] = f[at : at + width, :cy]
        out[d, width : width + EDGE, :] = jnp.where(low, f[at + width : at + width + EDGE, :cy], f[at - EDGE : at, :cy])
        out[d, width + EDGE :, :] = jnp.where(in_pack, turn(pack, EDGE - cy - d * width, 1)[:, :128], corner)


def strip_order(columns, width):
    low = iota((EDGE, columns.shape[1]), 0) < HALO
    ends = jnp.where(low, columns[EDGE + width : 2 * EDGE + width], columns[:EDGE])
    return jnp.concatenate([columns[EDGE : EDGE + width], ends], axis=0)


def krylov_kernel(cell, start, table, got, diag, rows_a, rows_b, basis, gram):
    count, chunk, cy = got.shape
    width, full = diag.shape
    rows = width + EDGE
    lon, lat = lax.axis_index("lon"), lax.axis_index("lat")
    x0 = (lon * count + lat) * width
    down, across = table.shape
    nx = across * cell
    lons = nx // (count * width)

    edges = jnp.concatenate([got[s, rows:, :] for s in range(count)], axis=0)
    if edges.shape[0] < 128:
        edges = jnp.concatenate([edges, jnp.zeros((128 - edges.shape[0], cy), jnp.float32)], axis=0)
    edges = strip_order(edges.T, width)
    from_south = edges * turn(edges, 9, 1)
    from_north = edges * turn(edges, -5, 1)
    from_fold = edges * turn(edges, 2, 1)
    lane = iota((rows, cy), 1)
    parts = []
    for s in range(count):
        part = got[s, :rows, :]
        if s > 0:
            part = part + jnp.where(lane == 0, turn(from_south, -(8 * s + 2), 1), 0.0)
        above = from_north if s < count - 1 else from_fold
        part = part + jnp.where(lane == cy - 1, turn(above, cy - 1 - (8 * s + 3), 1), 0.0)
        parts.append(part)
    parts.append(jnp.where(lane < HALO, turn(edges, -(8 * (count - 1) + 4), 1), 0.0))
    f = jnp.concatenate(parts, axis=1)

    place = iota((rows, across), 0)
    x = x0 + jnp.where(place < width + HALO, place, place - rows)
    x = jnp.where(x < 0, x + nx, jnp.where(x >= nx, x - nx, x))
    cells = iota((rows, across), 1)
    here = ones_at(lax.div(x, cell) == cells)
    there = ones_at(lax.div(nx - 1 - x, cell) == cells)
    up = ones_at(lax.div(iota((down, full), 1), cell) == iota((down, full), 0))
    above = ones_at((iota((down, cy), 0) == down - 1) & (iota((down, cy), 1) < HALO))
    land = table[...].astype(jnp.float32)
    pick = lax.dot_general(jnp.concatenate([here, there], axis=0), land, (((1,), (1,)), ((), ())), preferred_element_type=jnp.float32)
    mask = jnp.concatenate([mat(pick[:rows], up), mat(pick[rows:], above)], axis=1)

    even_row = lax.rem(lat, 2) == 0
    rim = full // cy * RIM
    d_a, d_b = rows_a[start : start + rim, :], rows_b[...]
    d_east, d_west = jnp.where(even_row, d_a, d_b), jnp.where(even_row, d_b, d_a)
    unused = jnp.zeros((EDGE - 2 * RIM, cy), jnp.float32)
    d_ends = [
        jnp.concatenate([d_east[c * RIM : (c + 1) * RIM], unused, d_west[c * RIM : (c + 1) * RIM]], axis=0) for c in range(full // cy)
    ]
    d_main = jnp.concatenate([diag[...], jnp.concatenate(d_ends, axis=1)], axis=0)

    mine = lon * count + lat
    total = lons * count
    tiles = []
    for strip in (total - 1 - mine, lax.rem(2 * total - 2 - mine, total), lax.rem(total - mine, total)):
        tile = got[lax.rem(strip, count)][rows:, :]
        tile = jnp.where(iota((EDGE, 128), 1) < 64, turn(turn(tile, HALO, 0), 64, 1), tile)
        tiles.append(turn(tile, lax.rem(128 - lax.div(strip, count) * width, 128), 1))
    here = iota((128, 128), 0)
    there = iota((128, 128), 1)
    picks = [
        (here + there == width - 1) & (there < width),
        (here + there == 2 * width - 1) & (there >= width) & (there < width + HALO),
        (here + there == rows - 1) & (there >= rows - HALO) & (there < rows),
    ]
    fold = sum(mat(tile, ones_at(pick), EXACT) for tile, pick in zip(tiles, picks))
    fold = [fold[EDGE - 1 - r : EDGE - r] for r in range(HALO)] + [jnp.zeros((128 - HALO, 128), jnp.float32)]
    d_all = jnp.concatenate([d_main, jnp.concatenate(fold, axis=0).T[:rows]], axis=1)

    spot = iota((EDGE, cy), 1)
    stats = jnp.where((spot >= STATS) & (spot < 64), sum(got[s, rows : rows + EDGE, :] for s in range(count)), 0.0)
    means = jnp.where(stats[2:3] > 0.0, stats[3:4] / stats[2:3], 0.0)
    totals = [total_of(v) for v in (stats[:1], stats[1:2] + stats[:1] * means, stats[2:3], stats[3:4])]
    shift = jnp.where(totals[0] > 0.0, totals[1] / totals[0], jnp.where(totals[2] > 0.0, totals[3] / totals[2], 0.0))
    near = mask * (1.0 / SCALE)
    centre = near * (4.0 + d_all - shift)
    p = [mask * f]
    for j in range(ITERS):
        p.append(centre * p[j] - near * beside(p[j]))
    for j in range(ITERS):
        basis[j] = p[j][:width, :full]
    sums = []
    for i in range(ITERS):
        for j in range(i, ITERS + 1):
            both = p[i][:width, :full] * p[j][:width, :full]
            both = sum(both[:, c : c + 128] for c in range(0, full, 128))
            sums.append(jnp.sum(both, axis=0, keepdims=True))
    pairs = len(sums)
    sums = jnp.concatenate(sums + [jnp.zeros((16 - pairs, 128), jnp.float32)], axis=0)
    sums = jnp.where(iota((16, 128), 0) == iota((16, 128), 1), jnp.sum(sums, axis=1, keepdims=True), 0.0)
    sums = jnp.sum(sums, axis=0, keepdims=True)
    sums = jnp.where(iota((1, 128), 1) == pairs, shift, sums)
    gram[...] = jnp.broadcast_to(sums, gram.shape)


def combine_kernel(gram, basis, psi):
    g = jnp.sum(gram[...], axis=0, keepdims=True)
    pairs = [(i, j) for i in range(ITERS) for j in range(i, ITERS + 1)]
    at = {}
    for n, (i, j) in enumerate(pairs):
        at[i, j] = at[j, i] = jnp.broadcast_to(g[:, n : n + 1], (8, 128))

    shift = jnp.broadcast_to(gram[:1, len(pairs) : len(pairs) + 1], (8, 128))

    def applied(i, j):
        return shift * at[i, j] + SCALE * at[i, j + 1]

    a = {(i, j): applied(i, j) for i in range(ITERS) for j in range(i, ITERS)}
    b = [at[i, 0] for i in range(ITERS)]
    inverse = []
    for k in range(ITERS):
        inverse.append(1.0 / a[k, k])
        for i in range(k + 1, ITERS):
            factor = a[k, i] * inverse[k]
            for j in range(i, ITERS):
                a[i, j] = a[i, j] - factor * a[k, j]
            b[i] = b[i] - factor * b[k]
    c = [None] * ITERS
    for i in reversed(range(ITERS)):
        value = b[i]
        for j in range(i + 1, ITERS):
            value = value - a[i, j] * c[j]
        c[i] = value * inverse[i]
    total = c[0][:1, :1] * basis[0]
    for j in range(1, ITERS):
        total = total + c[j][:1, :1] * basis[j]
    psi[...] = total


def rim_kernel(rows, out):
    out[...] = rows[...]


def tracer_kernel(last, theta, ocean, coef, got_a, got_b, rows_a, rows_b, out_hbm, out, sems):
    levels, cy, cx = theta.shape
    lon, lat = lax.axis_index("lon"), lax.axis_index("lat")
    even = lax.rem(lon, 2) == 0
    a, b = got_a[2 * EDGE : 2 * EDGE + levels, :], got_b[2 * EDGE : 2 * EDGE + levels, :]
    both = jnp.concatenate([jnp.where(even, a, b), jnp.where(even, b, a), jnp.zeros((128 - 2 * levels, cy), jnp.float32)], axis=0)
    sides = both.T
    even_row = lax.rem(lat, 2) == 0

    def joined(ref):
        return jnp.concatenate([ref[c * levels : (c + 1) * levels, :] for c in range(cx // cy)], axis=1)

    a, b = joined(rows_a), joined(rows_b)
    flip = ones_at(iota((cx, cx), 0) + iota((cx, cx), 1) == cx - 1)
    north = jnp.where(lat == last, mat(b, flip, EXACT), jnp.where(even_row, a, b))
    south = jnp.where(lat == 0, 0.0, jnp.where(even_row, b, a))

    lane = iota((cy, 128), 1)
    row = iota((cy, cx), 0)
    mask, scale = ocean[...], coef[...]
    some = 2
    copies = []
    for k in range(levels):
        th = theta[k]
        m = mask * th
        east, west = turn(m, -1, 1), turn(m, 1, 1)
        east = jnp.concatenate([east[:, : cx - 128], jnp.where(lane == 127, turn(sides, 127 - k, 1), east[:, cx - 128 :])], axis=1)
        west = jnp.concatenate([jnp.where(lane == 0, turn(sides, -levels - k, 1), west[:, :128]), west[:, 128:]], axis=1)
        above = jnp.where(row == cy - 1, north[k : k + 1], turn(m, -1, 0))
        below = jnp.where(row == 0, south[k : k + 1], turn(m, 1, 0))
        out[k] = th + scale * (east + west + above + below - 4.0 * m)
        if (k + 1) % some == 0:
            n = k // some
            piece = pl.ds(n * some, some)
            copies.append(pltpu.make_async_copy(out.at[piece], out_hbm.at[piece], sems.at[n]))
            copies[-1].start()
    for copy in copies:
        copy.wait()


def per_device(theta, kappa, layer_weight, diag, land_blocks):
    lons, lats = lax.axis_size("lon"), lax.axis_size("lat")
    joint = ("lon", "lat")
    devices = lons * lats
    levels, cy, cx = theta.shape
    width, full = diag.shape
    cell = full // land_blocks.shape[0]
    last = lats - 1
    f32 = jnp.float32
    shape = lambda *dims: jax.ShapeDtypeStruct(dims, f32)

    nt = cx // cy
    head = 3 * EDGE + levels
    own = (2 * nt + 1) * EDGE
    rim = RIM * (full // cy)
    held, ocean, coef, tt, kt, ends, pay_a, pay_b, pay_c, row_a, row_b, ns_b = pl.pallas_call(
        functools.partial(sum_kernel, cell),
        in_specs=[HBM] * 5,
        out_specs=[VMEM] * 12,
        out_shape=[
            pltpu.VMEM((levels, cy, cx), f32),
            shape(cy, cx),
            shape(cy, cx),
            shape(cx, cy),
            shape(cx, cy),
            shape(EDGE, cx),
            shape(head + EDGE, cy),
            shape(head + own, cy),
            shape(3 * EDGE, cy),
            shape(nt * levels + rim, cy),
            shape(rim, cy),
            shape(nt * levels, cy),
        ],
        scratch_shapes=[
            pltpu.VMEM((cy, cx), f32),
            pltpu.VMEM((width, full), f32),
            pltpu.VMEM(land_blocks.shape, jnp.int32),
            pltpu.SMEM((levels,), f32),
            pltpu.SemaphoreType.DMA((8,)),
        ],
        compiler_params=PARAMS,
        name="level_sum",
    )(*map(in_hbm, (layer_weight, land_blocks, theta, kappa, diag)))

    pairs_b = [(i, (i + 1) % lons if i % 2 else (i - 1) % lons) for i in range(lons)]
    mirror = [(i, lons - 1 - i) for i in range(lons)]
    got_a = lax.ppermute(pay_a, "lon", [(i, i ^ 1) for i in range(lons)])
    got_b = lax.ppermute(pay_b, "lon", pairs_b)
    if pairs_b == mirror:
        got_c = lax.ppermute(pay_c, "lon", [(i, i ^ 2) for i in range(lons)])
        folds = (got_b, got_c, pay_b)
        corners = (pay_b, got_a, got_b, got_c)
        tail = head + own - EDGE
        places = (head - EDGE, head, 0, head, (tail, head, tail, 2 * EDGE))
    else:
        got_c = lax.ppermute(pay_c, "lon", [(i, i ^ 1) for i in range(lons)])
        tops = lax.ppermute(jnp.concatenate([pay_b[head:], got_c, got_b[head:]], axis=0), "lon", mirror)
        folds = (tops, tops, tops)
        corners = (lax.psum(pay_c[2 * EDGE :], "lon"),)
        places = (head - EDGE, 0, own, own + 3 * EDGE, (0,))
    chunks = pl.pallas_call(
        functools.partial(forcing_kernel, last, lons, width, places),
        in_specs=[VMEM] * (8 + len(corners)),
        out_specs=VMEM,
        out_shape=shape(lats, width + 2 * EDGE, cy),
        compiler_params=PARAMS,
        name="forcing",
    )(tt, kt, ends, got_a, got_b, *folds, *corners)
    chunks, row_a, ns_b = lax.optimization_barrier((chunks, row_a, ns_b))
    got = lax.all_to_all(chunks, "lat", split_axis=0, concat_axis=0, tiled=True)

    rows_b = lax.ppermute(row_b, joint, [(i, (i + 1 if i % 2 else i - 1) % devices) for i in range(devices)])
    rim_b = pl.pallas_call(
        rim_kernel,
        in_specs=[VMEM],
        out_specs=VMEM,
        out_shape=shape(rim, cy),
        compiler_params=PARAMS,
        cost_estimate=pl.CostEstimate(flops=10**11, bytes_accessed=0, transcendentals=0),
        name="rim",
    )(rows_b)
    row_a, rim_b = lax.optimization_barrier((row_a, rim_b))
    rows_a = lax.ppermute(row_a, joint, [(i, i ^ 1) for i in range(devices)])
    second = []
    for lon in range(lons):
        second += [(lon * lats + lat, (lons - 1 - lon) * lats + lat) for lat in (0, last)]
        second += [(lon * lats + lat, lon * lats + (lat + 1 if lat % 2 else lat - 1)) for lat in range(1, last)]
    beyond = lax.ppermute(ns_b, joint, second)
    new_theta = pl.pallas_call(
        functools.partial(tracer_kernel, last),
        in_specs=[VMEM] * 7,
        out_specs=HBM,
        out_shape=shape(levels, cy, cx),
        scratch_shapes=[pltpu.VMEM((levels, cy, cx), f32), pltpu.SemaphoreType.DMA((levels // 2,))],
        compiler_params=PARAMS,
        cost_estimate=pl.CostEstimate(flops=12 * levels * cy * cx, bytes_accessed=8 * levels * cy * cx, transcendentals=0),
        name="tracer",
    )(held, ocean, coef, got_a, got_b, rows_a, beyond)

    basis, gram = pl.pallas_call(
        functools.partial(krylov_kernel, cell, nt * levels),
        in_specs=[VMEM] * 5,
        out_specs=[VMEM, VMEM],
        out_shape=[shape(ITERS, width, full), shape(devices, 128)],
        compiler_params=PARAMS,
        name="krylov",
    )(land_blocks, got, diag, rows_a, rim_b)
    gram = lax.all_to_all(gram, joint, split_axis=0, concat_axis=0, tiled=True)
    psi = pl.pallas_call(
        combine_kernel,
        in_specs=[VMEM, VMEM],
        out_specs=VMEM,
        out_shape=shape(width, full),
        compiler_params=PARAMS,
        name="combine",
    )(gram, basis)
    return new_theta, psi


def solution(mesh):
    return jax.shard_map(
        per_device,
        mesh=mesh,
        in_specs=(P(None, "lat", "lon"), P("lat", "lon"), P(), P(("lon", "lat"), None), P()),
        out_specs=(P(None, "lat", "lon"), P(("lon", "lat"), None)),
        check_vma=False,
    )
```

```python
import functools

import jax
import jax.numpy as jnp
from jax import lax
from jax.experimental import pallas as pl
from jax.experimental.pallas import tpu as pltpu
from jax.sharding import PartitionSpec as P

ITERS = 4
EDGE = 8
HALO = ITERS
RIM = HALO - 1
SCALE = 4.0
STATS = 48
VMEM = pl.BlockSpec(memory_space=pltpu.VMEM)
SMEM = pl.BlockSpec(memory_space=pltpu.SMEM)
HBM = pl.BlockSpec(memory_space=pltpu.HBM)
EXACT = lax.Precision.HIGHEST
PARAMS = pltpu.CompilerParams(vmem_limit_bytes=32 * 1024 * 1024)


def in_hbm(x):
    return pltpu.with_memory_space_constraint(x, pltpu.HBM)


def iota(shape, dim):
    return lax.broadcasted_iota(jnp.int32, shape, dim)


def ones_at(hit):
    return jnp.where(hit, 1.0, 0.0).astype(jnp.float32)


def mat(a, b, precision=None):
    return jnp.dot(a, b, precision=precision, preferred_element_type=jnp.float32)


def turn(x, shift, dim):
    return pltpu.roll(x, shift % x.shape[dim] if isinstance(shift, int) else shift, dim)


def beside(v):
    return turn(v, 1, 0) + turn(v, -1, 0) + turn(v, 1, 1) + turn(v, -1, 1)


def total_of(v):
    return jnp.sum(jnp.sum(v, axis=0, keepdims=True), axis=1, keepdims=True)


def block_mask(table, row0, rows, col0, cols, cell):
    down, across = table.shape
    pick_rows = ones_at(lax.div(row0 + iota((rows, down), 0), cell) == iota((rows, down), 1))
    pick_cols = ones_at(lax.div(col0 + iota((across, cols), 1), cell) == iota((across, cols), 0))
    return mat(mat(pick_rows, table), pick_cols)


def sum_kernel(cell, weight_hbm, table_hbm, theta_hbm, kappa_hbm, diag_hbm, theta, ocean, coef, tt, kt, ends, pay_a, pay_b, pay_c, row_a, row_b, ns_b, kappa, strip, table, weight, sems):
    levels, cy, cx = theta.shape
    width, full = diag_hbm.shape
    copies = [
        pltpu.make_async_copy(table_hbm, table, sems.at[0]),
        pltpu.make_async_copy(weight_hbm, weight, sems.at[1]),
        pltpu.make_async_copy(kappa_hbm, kappa, sems.at[2]),
        pltpu.make_async_copy(diag_hbm, strip, sems.at[3]),
    ]
    pieces = 4
    some = levels // pieces
    for n in range(pieces):
        copies.append(pltpu.make_async_copy(theta_hbm.at[pl.ds(n * some, some)], theta.at[pl.ds(n * some, some)], sems.at[4 + n]))
    for copy in copies:
        copy.start()
    lon, lat = lax.axis_index("lon"), lax.axis_index("lat")
    even = lax.rem(lon, 2) == 0
    even_row = lax.rem(lat, 2) == 0
    copies[0].wait()
    mask = block_mask(table[...].astype(jnp.float32), lat * cy, cy, lon * cx, cx, cell)
    copies[3].wait()
    column = jnp.concatenate([strip[:, full - 128 :], jnp.zeros((128 - width, 128), jnp.float32)], axis=0).T
    column = turn(column[128 - EDGE :], lon * width, 1)
    down, across = table.shape
    x0 = (lon * (cx // width) + lat) * width
    land = table[...].astype(jnp.float32)
    pick = ones_at(lax.div(x0 + iota((width, across), 0), cell) == iota((width, across), 1))
    pick = lax.dot_general(pick, land, (((1,), (1,)), ((), ())), preferred_element_type=jnp.float32)
    wet = mat(pick, ones_at(lax.div(iota((down, full), 1), cell) == iota((down, full), 0)))
    at = cx // cy * levels
    for c in range(full // cy):
        w = strip[:RIM, c * cy : (c + 1) * cy]
        e = strip[width - RIM :, c * cy : (c + 1) * cy]
        row_a[at : at + RIM, :] = jnp.where(even_row, e, w)
        row_b[c * RIM : (c + 1) * RIM, :] = jnp.where(even_row, w, e)
        at += RIM
    copies[2].wait()
    kappas = kappa[...]
    ocean[...] = mask
    coef[...] = mask * kappas
    ktv = kappas.T
    kt[...] = ktv

    lane = iota((cy, 128), 1)
    total = jnp.zeros((cy, cx), jnp.float32)
    sides = jnp.zeros((cy, 128), jnp.float32)
    copies[1].wait()
    for n in range(pieces):
        copies[4 + n].wait()
        for k in range(n * some, n * some + some):
            th = theta[k]
            total = total + weight[k] * th
            sides = jnp.where(lane == k, turn(th[:, :128], k, 1), sides)
            sides = jnp.where(lane == levels + k, turn(th[:, cx - 128 :], levels + k + 1, 1), sides)
    t = mask * total
    inner = (iota((cy, cx), 0) > 0) & (iota((cy, cx), 0) < cy - 1) & (iota((cy, cx), 1) > 0) & (iota((cy, cx), 1) < cx - 1)
    kept = jnp.where(inner, t, 0.0)
    stats = []
    for pair in ((wet, wet * strip[...]), (kept * t, kept * (4.0 * t - beside(t)))):
        pair = jnp.sum(jnp.concatenate([jnp.sum(v, axis=0, keepdims=True) for v in pair], axis=0), axis=1, keepdims=True)
        stats = [pair[:1], pair[1:]] + stats
    spot = iota((EDGE, 128), 1)
    mine = (spot >= lon * width) & (spot < (lon + 1) * width)
    for n, value in enumerate(stats):
        column = jnp.where(iota((EDGE, 128), 0) == n, jnp.where(mine, value, 0.0), column)
    ttv = t.T
    tt[...] = ttv
    sidest = (sides * jnp.where(lane < levels, mask[:, :1], mask[:, cx - 1 :])).T
    west, east = sidest[:levels], sidest[levels : 2 * levels]
    pay_a[2 * EDGE : 2 * EDGE + levels, :] = jnp.where(even, east, west)
    pay_b[2 * EDGE : 2 * EDGE + levels, :] = jnp.where(even, west, east)
    for at, turned in ((0, ttv), (EDGE, ktv)):
        w, e = turned[:EDGE], turned[cx - EDGE :]
        pay_a[at : at + EDGE, :] = jnp.where(even, e, w)
        pay_b[at : at + EDGE, :] = jnp.where(even, w, e)
    at = 2 * EDGE + levels
    rows = jnp.concatenate([t[:1], t[cy - 1 :], kappas[:1], kappas[cy - 1 :], jnp.zeros((EDGE - 4, cx), jnp.float32)], axis=0)
    ends[...] = rows
    pay_a[at : at + EDGE, :] = jnp.where(even, rows[:, cx - cy :], rows[:, :cy])
    pay_b[at : at + EDGE, :] = jnp.where(even, rows[:, :cy], rows[:, cx - cy :])
    at += EDGE
    flip = ones_at(iota((cx, cx), 0) + iota((cx, cx), 1) == cx - 1)
    both = jnp.concatenate([t[cy - EDGE :], kappas[cy - EDGE :, :]], axis=0)
    turned = mat(both, flip, EXACT)
    nt = cx // cy
    for base in (0, EDGE):
        for r in range(EDGE):
            row = turned[base + EDGE - 1 - r : base + EDGE - r]
            pay_c[base + r : base + r + 1, :] = jnp.where(even, row[:, :cy], row[:, cx - cy :])
            for c in range(nt):
                to_b = at + (base // EDGE * nt + c) * EDGE + r
                pay_b[to_b : to_b + 1, :] = row[:, c * cy : (c + 1) * cy]
    pay_a[at:, :] = column
    pay_c[2 * EDGE :, :] = column
    pay_b[at + 2 * nt * EDGE :, :] = column
    top = theta[:, cy - 1, :] * mask[cy - 1 :, :]
    bottom = theta[:, 0, :] * mask[:1, :]
    for c in range(nt):
        t, b = top[:, c * cy : (c + 1) * cy], bottom[:, c * cy : (c + 1) * cy]
        row_a[c * levels : (c + 1) * levels, :] = jnp.where(even_row, t, b)
        ns_b[c * levels : (c + 1) * levels, :] = jnp.where(even_row, b, t)


def forcing_kernel(last, lons, width, places, tt, kt, ends, got_a, got_b, tops_m, tops_a, tops_b, *rest):
    *corners, out = rest
    at_ends, at_m, at_a, at_b, at_corners = places
    cx, cy = tt.shape
    lon, lat = lax.axis_index("lon"), lax.axis_index("lat")
    even = lax.rem(lon, 2) == 0
    nt = cx // cy

    def sides(at):
        a, b = got_a[at : at + EDGE, :], got_b[at : at + EDGE, :]
        return jnp.where(even, b, a), jnp.where(even, a, b)

    def extended(own, at):
        left, right = sides(at)
        return jnp.concatenate([left, own, right], axis=0)

    t = extended(tt[...], 0)
    k = extended(kt[...], EDGE)
    lane = iota((cx + 2 * EDGE, cy), 1)
    south = jnp.where(lane == 0, 0.0, turn(t, 1, 1))
    north = jnp.where(lane == cy - 1, 0.0, turn(t, -1, 1))
    f = t + k * (turn(t, 1, 0) + turn(t, -1, 0) + south + north - 4.0 * t)

    def beyond(which):
        a = tops_a[at_a + which * EDGE : at_a + (which + 1) * EDGE, :]
        b_first = tops_b[at_b + which * nt * EDGE : at_b + (which * nt + 1) * EDGE, :]
        b_last = tops_b[at_b + (which * nt + nt - 1) * EDGE : at_b + (which * nt + nt) * EDGE, :]
        middle = [tops_m[at_m + (which * nt + c) * EDGE : at_m + (which * nt + c + 1) * EDGE, :] for c in range(nt)]
        return jnp.concatenate([jnp.where(even, b_last, a)] + middle + [jnp.where(even, a, b_first)], axis=1)

    left, right = sides(at_ends)
    row_ends = jnp.concatenate([left, ends[...], right], axis=1)
    over, over_k = beyond(0), beyond(1)
    row = iota(over.shape, 0)
    below = jnp.where(row == 0, row_ends[1:2], turn(over, 1, 0))
    over_f = over + over_k * (turn(over, 1, 1) + turn(over, -1, 1) + turn(over, -1, 0) + below - 4.0 * over)
    row_ends = jnp.where((row == 1) & (lat == last), over[:1], row_ends)
    pack = jnp.where(row < 4, row_ends, turn(over_f, 4, 0))
    low = iota((EDGE, cy), 0) < HALO
    corner = sum(ref[at : at + EDGE, :] for ref, at in zip(corners, at_corners))
    spread = corner
    corner = jnp.where(low, turn(turn(corner, HALO, 0), 64, 1), corner)
    spot = iota((EDGE, cy), 1)
    for n in range(lons):
        first = STATS + n * ((64 - STATS) // lons)
        corner = jnp.where((spot >= first) & (spot < 64), turn(spread, first - n * width, 1), corner)
    in_pack = spot < STATS
    for d in range(cx // width):
        at = EDGE + d * width
        out[d, :width, :] = f[at : at + width, :cy]
        out[d, width : width + EDGE, :] = jnp.where(low, f[at + width : at + width + EDGE, :cy], f[at - EDGE : at, :cy])
        out[d, width + EDGE :, :] = jnp.where(in_pack, turn(pack, EDGE - cy - d * width, 1)[:, :128], corner)


def strip_order(columns, width):
    low = iota((EDGE, columns.shape[1]), 0) < HALO
    ends = jnp.where(low, columns[EDGE + width : 2 * EDGE + width], columns[:EDGE])
    return jnp.concatenate([columns[EDGE : EDGE + width], ends], axis=0)


def krylov_kernel(cell, start, table, got, diag, rows_a, rows_b, basis, gram):
    count, chunk, cy = got.shape
    width, full = diag.shape
    rows = width + EDGE
    lon, lat = lax.axis_index("lon"), lax.axis_index("lat")
    x0 = (lon * count + lat) * width
    down, across = table.shape
    nx = across * cell
    lons = nx // (count * width)

    edges = jnp.concatenate([got[s, rows:, :] for s in range(count)], axis=0)
    if edges.shape[0] < 128:
        edges = jnp.concatenate([edges, jnp.zeros((128 - edges.shape[0], cy), jnp.float32)], axis=0)
    edges = strip_order(edges.T, width)
    from_south = edges * turn(edges, 9, 1)
    from_north = edges * turn(edges, -5, 1)
    from_fold = edges * turn(edges, 2, 1)
    lane = iota((rows, cy), 1)
    parts = []
    for s in range(count):
        part = got[s, :rows, :]
        if s > 0:
            part = part + jnp.where(lane == 0, turn(from_south, -(8 * s + 2), 1), 0.0)
        above = from_north if s < count - 1 else from_fold
        part = part + jnp.where(lane == cy - 1, turn(above, cy - 1 - (8 * s + 3), 1), 0.0)
        parts.append(part)
    parts.append(jnp.where(lane < HALO, turn(edges, -(8 * (count - 1) + 4), 1), 0.0))
    f = jnp.concatenate(parts, axis=1)

    place = iota((rows, across), 0)
    x = x0 + jnp.where(place < width + HALO, place, place - rows)
    x = jnp.where(x < 0, x + nx, jnp.where(x >= nx, x - nx, x))
    cells = iota((rows, across), 1)
    here = ones_at(lax.div(x, cell) == cells)
    there = ones_at(lax.div(nx - 1 - x, cell) == cells)
    up = ones_at(lax.div(iota((down, full), 1), cell) == iota((down, full), 0))
    above = ones_at((iota((down, cy), 0) == down - 1) & (iota((down, cy), 1) < HALO))
    land = table[...].astype(jnp.float32)
    pick = lax.dot_general(jnp.concatenate([here, there], axis=0), land, (((1,), (1,)), ((), ())), preferred_element_type=jnp.float32)
    mask = jnp.concatenate([mat(pick[:rows], up), mat(pick[rows:], above)], axis=1)

    even_row = lax.rem(lat, 2) == 0
    rim = full // cy * RIM
    d_a, d_b = rows_a[start : start + rim, :], rows_b[...]
    d_east, d_west = jnp.where(even_row, d_a, d_b), jnp.where(even_row, d_b, d_a)
    unused = jnp.zeros((EDGE - 2 * RIM, cy), jnp.float32)
    d_ends = [
        jnp.concatenate([d_east[c * RIM : (c + 1) * RIM], unused, d_west[c * RIM : (c + 1) * RIM]], axis=0) for c in range(full // cy)
    ]
    d_main = jnp.concatenate([diag[...], jnp.concatenate(d_ends, axis=1)], axis=0)

    mine = lon * count + lat
    total = lons * count
    tiles = []
    for strip in (total - 1 - mine, lax.rem(2 * total - 2 - mine, total), lax.rem(total - mine, total)):
        tile = got[lax.rem(strip, count)][rows:, :]
        tile = jnp.where(iota((EDGE, 128), 1) < 64, turn(turn(tile, HALO, 0), 64, 1), tile)
        tiles.append(turn(tile, lax.rem(128 - lax.div(strip, count) * width, 128), 1))
    here = iota((128, 128), 0)
    there = iota((128, 128), 1)
    picks = [
        (here + there == width - 1) & (there < width),
        (here + there == 2 * width - 1) & (there >= width) & (there < width + HALO),
        (here + there == rows - 1) & (there >= rows - HALO) & (there < rows),
    ]
    fold = sum(mat(tile, ones_at(pick), EXACT) for tile, pick in zip(tiles, picks))
    fold = [fold[EDGE - 1 - r : EDGE - r] for r in range(HALO)] + [jnp.zeros((128 - HALO, 128), jnp.float32)]
    d_all = jnp.concatenate([d_main, jnp.concatenate(fold, axis=0).T[:rows]], axis=1)

    spot = iota((EDGE, cy), 1)
    stats = jnp.where((spot >= STATS) & (spot < 64), sum(got[s, rows : rows + EDGE, :] for s in range(count)), 0.0)
    means = jnp.where(stats[2:3] > 0.0, stats[3:4] / stats[2:3], 0.0)
    totals = [total_of(v) for v in (stats[:1], stats[1:2] + stats[:1] * means, stats[2:3], stats[3:4])]
    shift = jnp.where(totals[0] > 0.0, totals[1] / totals[0], jnp.where(totals[2] > 0.0, totals[3] / totals[2], 0.0))
    near = mask * (1.0 / SCALE)
    centre = near * (4.0 + d_all - shift)
    p = [mask * f]
    for j in range(ITERS):
        p.append(centre * p[j] - near * beside(p[j]))
    for j in range(ITERS):
        basis[j] = p[j][:width, :full]
    sums = []
    for i in range(ITERS):
        for j in range(i, ITERS + 1):
            both = p[i][:width, :full] * p[j][:width, :full]
            both = sum(both[:, c : c + 128] for c in range(0, full, 128))
            sums.append(jnp.sum(both, axis=0, keepdims=True))
    pairs = len(sums)
    sums = jnp.concatenate(sums + [jnp.zeros((16 - pairs, 128), jnp.float32)], axis=0)
    sums = jnp.where(iota((16, 128), 0) == iota((16, 128), 1), jnp.sum(sums, axis=1, keepdims=True), 0.0)
    sums = jnp.sum(sums, axis=0, keepdims=True)
    sums = jnp.where(iota((1, 128), 1) == pairs, shift, sums)
    gram[...] = jnp.broadcast_to(sums, gram.shape)


def combine_kernel(gram, basis, psi):
    g = jnp.sum(gram[...], axis=0, keepdims=True)
    pairs = [(i, j) for i in range(ITERS) for j in range(i, ITERS + 1)]
    at = {}
    for n, (i, j) in enumerate(pairs):
        at[i, j] = at[j, i] = jnp.broadcast_to(g[:, n : n + 1], (8, 128))

    shift = jnp.broadcast_to(gram[:1, len(pairs) : len(pairs) + 1], (8, 128))

    def applied(i, j):
        return shift * at[i, j] + SCALE * at[i, j + 1]

    a = {(i, j): applied(i, j) for i in range(ITERS) for j in range(i, ITERS)}
    b = [at[i, 0] for i in range(ITERS)]
    inverse = []
    for k in range(ITERS):
        inverse.append(1.0 / a[k, k])
        for i in range(k + 1, ITERS):
            factor = a[k, i] * inverse[k]
            for j in range(i, ITERS):
                a[i, j] = a[i, j] - factor * a[k, j]
            b[i] = b[i] - factor * b[k]
    c = [None] * ITERS
    for i in reversed(range(ITERS)):
        value = b[i]
        for j in range(i + 1, ITERS):
            value = value - a[i, j] * c[j]
        c[i] = value * inverse[i]
    total = c[0][:1, :1] * basis[0]
    for j in range(1, ITERS):
        total = total + c[j][:1, :1] * basis[j]
    psi[...] = total


def rim_kernel(rows, out):
    out[...] = rows[...]


def tracer_kernel(last, theta, ocean, coef, got_a, got_b, rows_a, rows_b, out_hbm, out, sems):
    levels, cy, cx = theta.shape
    lon, lat = lax.axis_index("lon"), lax.axis_index("lat")
    even = lax.rem(lon, 2) == 0
    a, b = got_a[2 * EDGE : 2 * EDGE + levels, :], got_b[2 * EDGE : 2 * EDGE + levels, :]
    both = jnp.concatenate([jnp.where(even, a, b), jnp.where(even, b, a), jnp.zeros((128 - 2 * levels, cy), jnp.float32)], axis=0)
    sides = both.T
    even_row = lax.rem(lat, 2) == 0

    def joined(ref):
        return jnp.concatenate([ref[c * levels : (c + 1) * levels, :] for c in range(cx // cy)], axis=1)

    a, b = joined(rows_a), joined(rows_b)
    flip = ones_at(iota((cx, cx), 0) + iota((cx, cx), 1) == cx - 1)
    north = jnp.where(lat == last, mat(b, flip, EXACT), jnp.where(even_row, a, b))
    south = jnp.where(lat == 0, 0.0, jnp.where(even_row, b, a))

    lane = iota((cy, 128), 1)
    row = iota((cy, cx), 0)
    mask, scale = ocean[...], coef[...]
    some = 2
    copies = []
    for k in range(levels):
        th = theta[k]
        m = mask * th
        east, west = turn(m, -1, 1), turn(m, 1, 1)
        east = jnp.concatenate([east[:, : cx - 128], jnp.where(lane == 127, turn(sides, 127 - k, 1), east[:, cx - 128 :])], axis=1)
        west = jnp.concatenate([jnp.where(lane == 0, turn(sides, -levels - k, 1), west[:, :128]), west[:, 128:]], axis=1)
        above = jnp.where(row == cy - 1, north[k : k + 1], turn(m, -1, 0))
        below = jnp.where(row == 0, south[k : k + 1], turn(m, 1, 0))
        out[k] = th + scale * (east + west + above + below - 4.0 * m)
        if (k + 1) % some == 0:
            n = k // some
            piece = pl.ds(n * some, some)
            copies.append(pltpu.make_async_copy(out.at[piece], out_hbm.at[piece], sems.at[n]))
            copies[-1].start()
    for copy in copies:
        copy.wait()


def per_device(theta, kappa, layer_weight, diag, land_blocks):
    lons, lats = lax.axis_size("lon"), lax.axis_size("lat")
    joint = ("lon", "lat")
    devices = lons * lats
    levels, cy, cx = theta.shape
    width, full = diag.shape
    cell = full // land_blocks.shape[0]
    last = lats - 1
    f32 = jnp.float32
    shape = lambda *dims: jax.ShapeDtypeStruct(dims, f32)

    nt = cx // cy
    head = 3 * EDGE + levels
    own = (2 * nt + 1) * EDGE
    rim = RIM * (full // cy)
    held, ocean, coef, tt, kt, ends, pay_a, pay_b, pay_c, row_a, row_b, ns_b = pl.pallas_call(
        functools.partial(sum_kernel, cell),
        in_specs=[HBM] * 5,
        out_specs=[VMEM] * 12,
        out_shape=[
            pltpu.VMEM((levels, cy, cx), f32),
            shape(cy, cx),
            shape(cy, cx),
            shape(cx, cy),
            shape(cx, cy),
            shape(EDGE, cx),
            shape(head + EDGE, cy),
            shape(head + own, cy),
            shape(3 * EDGE, cy),
            shape(nt * levels + rim, cy),
            shape(rim, cy),
            shape(nt * levels, cy),
        ],
        scratch_shapes=[
            pltpu.VMEM((cy, cx), f32),
            pltpu.VMEM((width, full), f32),
            pltpu.VMEM(land_blocks.shape, jnp.int32),
            pltpu.SMEM((levels,), f32),
            pltpu.SemaphoreType.DMA((8,)),
        ],
        compiler_params=PARAMS,
        name="level_sum",
    )(*map(in_hbm, (layer_weight, land_blocks, theta, kappa, diag)))

    pairs_b = [(i, (i + 1) % lons if i % 2 else (i - 1) % lons) for i in range(lons)]
    mirror = [(i, lons - 1 - i) for i in range(lons)]
    got_a = lax.ppermute(pay_a, "lon", [(i, i ^ 1) for i in range(lons)])
    got_b = lax.ppermute(pay_b, "lon", pairs_b)
    if pairs_b == mirror:
        got_c = lax.ppermute(pay_c, "lon", [(i, i ^ 2) for i in range(lons)])
        folds = (got_b, got_c, pay_b)
        corners = (pay_b, got_a, got_b, got_c)
        tail = head + own - EDGE
        places = (head - EDGE, head, 0, head, (tail, head, tail, 2 * EDGE))
    else:
        got_c = lax.ppermute(pay_c, "lon", [(i, i ^ 1) for i in range(lons)])
        tops = lax.ppermute(jnp.concatenate([pay_b[head:], got_c, got_b[head:]], axis=0), "lon", mirror)
        folds = (tops, tops, tops)
        corners = (lax.psum(pay_c[2 * EDGE :], "lon"),)
        places = (head - EDGE, 0, own, own + 3 * EDGE, (0,))
    chunks = pl.pallas_call(
        functools.partial(forcing_kernel, last, lons, width, places),
        in_specs=[VMEM] * (8 + len(corners)),
        out_specs=VMEM,
        out_shape=shape(lats, width + 2 * EDGE, cy),
        compiler_params=PARAMS,
        name="forcing",
    )(tt, kt, ends, got_a, got_b, *folds, *corners)
    chunks, row_a, ns_b = lax.optimization_barrier((chunks, row_a, ns_b))
    got = lax.all_to_all(chunks, "lat", split_axis=0, concat_axis=0, tiled=True)

    rows_b = lax.ppermute(row_b, joint, [(i, (i + 1 if i % 2 else i - 1) % devices) for i in range(devices)])
    rim_b = pl.pallas_call(
        rim_kernel,
        in_specs=[VMEM],
        out_specs=VMEM,
        out_shape=shape(rim, cy),
        compiler_params=PARAMS,
        cost_estimate=pl.CostEstimate(flops=10**11, bytes_accessed=0, transcendentals=0),
        name="rim",
    )(rows_b)
    row_a, rim_b = lax.optimization_barrier((row_a, rim_b))
    rows_a = lax.ppermute(row_a, joint, [(i, i ^ 1) for i in range(devices)])
    second = []
    for lon in range(lons):
        second += [(lon * lats + lat, (lons - 1 - lon) * lats + lat) for lat in (0, last)]
        second += [(lon * lats + lat, lon * lats + (lat + 1 if lat % 2 else lat - 1)) for lat in range(1, last)]
    beyond = lax.ppermute(ns_b, joint, second)
    new_theta = pl.pallas_call(
        functools.partial(tracer_kernel, last),
        in_specs=[VMEM] * 7,
        out_specs=HBM,
        out_shape=shape(levels, cy, cx),
        scratch_shapes=[pltpu.VMEM((levels, cy, cx), f32), pltpu.SemaphoreType.DMA((levels // 2,))],
        compiler_params=PARAMS,
        cost_estimate=pl.CostEstimate(flops=12 * levels * cy * cx, bytes_accessed=8 * levels * cy * cx, transcendentals=0),
        name="tracer",
    )(held, ocean, coef, got_a, got_b, rows_a, beyond)

    basis, gram = pl.pallas_call(
        functools.partial(krylov_kernel, cell, nt * levels),
        in_specs=[VMEM] * 5,
        out_specs=[VMEM, VMEM],
        out_shape=[shape(ITERS, width, full), shape(devices, 128)],
        compiler_params=PARAMS,
        name="krylov",
    )(land_blocks, got, diag, rows_a, rim_b)
    gram = lax.all_to_all(gram, joint, split_axis=0, concat_axis=0, tiled=True)
    psi = pl.pallas_call(
        combine_kernel,
        in_specs=[VMEM, VMEM],
        out_specs=VMEM,
        out_shape=shape(width, full),
        compiler_params=PARAMS,
        name="combine",
    )(gram, basis)
    return new_theta, psi


def solution(mesh):
    return jax.shard_map(
        per_device,
        mesh=mesh,
        in_specs=(P(None, "lat", "lon"), P("lat", "lon"), P(), P(("lon", "lat"), None), P()),
        out_specs=(P(None, "lat", "lon"), P(("lon", "lat"), None)),
        check_vma=False,
    )
```
